128 devices in a mesh: mp: 8 (over y, core), mem: 16 (over z, x).
Axes of the slice: x: 4, y: 4, z: 4, core: 2. Of those that a mesh axis runs over, the one named last changes fastest.
Arguments:
- tokens: bfloat16 [16, 8192], P(None, 'mem'), may hold values from -6 to 6
- attn_gain: bfloat16 [8192], P('mem'), may hold values from 0.099609375 to 1.8984375
- query_key_value_weight: bfloat16 [8192, 10240], P('mem', 'mp'), may hold values from -0.0625 to 0.0625
- paged_key_store: bfloat16 [2048, 8, 128, 128], P('mem', 'mp'), may hold values from -110 to 110
- paged_value_store: bfloat16 [2048, 8, 128, 128], P('mem', 'mp'), may hold values from -6 to 6
- lengths: int32 [4], replicated, may hold values from 1 to 65536, as said below
- block_table: int32 [4, 512], replicated, may hold values from -1 to 2047, as said below
- out_weight: bfloat16 [8192, 8192], P('mp', 'mem'), may hold values from -0.47851562 to 0.47851562
- mlp_gain: bfloat16 [8192], P('mem'), may hold values from 0.099609375 to 1.8984375
- gate_weight: bfloat16 [8192, 28672], P('mem', 'mp'), may hold values from -0.0625 to 0.0625
- up_weight: bfloat16 [8192, 28672], P('mem', 'mp'), may hold values from -0.0625 to 0.0625
- down_weight: bfloat16 [28672, 8192], P('mp', 'mem'), may hold values from -0.03125 to 0.03125
Outputs:
- layer_out: bfloat16 [16, 8192], P(None, 'mem')
The draws below stay inside these ranges and needn't reach their ends.
Inputs may be any that keep to these rules, and one draw needn't show every extreme that they name: `lengths`: at least one request has exactly 65536 cached tokens. `block_table`: entry b of request r is a pool block for b < ceil(lengths[r] / 128) and -1 otherwise; no pool block is named twice in the table.
All inputs are finite; a program needn't handle non-finite values.
Results may differ from the reference program's by a relative error of at most 0.015.
The reference program's roundings to bfloat16 on the way (of `scaled_in`, `queries`, `attended`, `after_attn`, `scaled_mid` and `hidden`) count: a program that leaves them out, or rounds other values in their place, can miss the bound.
Values may be sent and summed in bfloat16 or wider, within the bound.
A program may use at most 64 MiB of HBM per device.

```python
import math
import jax
import jax.numpy as jnp
from jax import lax

MODEL_SIZE = 8192
QUERY_HEADS = 64
KEY_HEADS = 8
HEAD_SIZE = 128
FF = 28672
REQUEST_COUNT = 4
NEW_POSITIONS = 4
SLOTS = 128
BLOCK_TOKENS = 128
QUERY_PER_KV = 8
ROWS = 16
POOL_BLOCKS = 2048
MAXB = 512


def placement(key):
    part_keys = jax.random.split(key, 5)
    request_ids = jnp.arange(REQUEST_COUNT, dtype=jnp.int32)
    counts = jax.random.randint(part_keys[0], (REQUEST_COUNT,), MAXB // 4, MAXB + 1)
    chosen = jax.random.randint(part_keys[1], (), 0, REQUEST_COUNT)
    counts = jnp.where(request_ids == chosen, MAXB, counts)
    tails = jax.random.randint(part_keys[2], (REQUEST_COUNT,), 1, BLOCK_TOKENS + 1)
    lengths = jnp.where(request_ids == chosen, MAXB * BLOCK_TOKENS, (counts - 1) * BLOCK_TOKENS + tails)
    holders = POOL_BLOCKS // SLOTS
    device_rank = jax.random.permutation(part_keys[3], holders)
    slot_ids = jnp.arange(POOL_BLOCKS, dtype=jnp.int32)
    noise = jax.random.randint(part_keys[4], (POOL_BLOCKS,), 0, 65536)
    scores = (noise + device_rank[slot_ids // SLOTS] * (32768 // holders)) * POOL_BLOCKS + slot_ids
    ordering = jnp.argsort(scores).astype(jnp.int32)
    starts = jnp.cumsum(counts) - counts
    block_ids = jnp.arange(MAXB, dtype=jnp.int32)
    index = jnp.clip(starts[:, None] + block_ids[None, :], 0, POOL_BLOCKS - 1)
    table = jnp.where(block_ids[None, :] < counts[:, None], ordering[index], -1)
    return (lengths.astype(jnp.int32), table.astype(jnp.int32))


def draw_lengths(key, part):
    return placement(key)[0]


def draw_block_table(key, part):
    return placement(key)[1]


def draw_paged_key_store(key, part):
    key = jax.random.fold_in(key, 3)
    array_shape = (POOL_BLOCKS, KEY_HEADS, BLOCK_TOKENS, HEAD_SIZE)
    values = jnp.clip(jax.random.normal(key, array_shape, jnp.float32), -6.0, 6.0)
    return values.astype(jnp.bfloat16)


def steps_of(key, dims, pieces, smallest, high):
    level, own = 1.0, jax.random.fold_in(key, 6)
    for dim, parts in pieces:
        steps = jnp.exp(jax.random.uniform(jax.random.fold_in(own, dim), (parts,), jnp.float32, smallest / len(pieces), high / len(pieces)))
        level = level * jnp.repeat(steps, dims[dim] // parts).reshape([-1 if axis == dim else 1 for axis in range(len(dims))])
    return level


def bell_draw(stream_key, dims, scale, limit, cuts=(), held_as=jnp.bfloat16):
    drawn = jax.random.normal(stream_key, dims, jnp.float32) * scale
    if len(cuts) > 0:
        drawn = steps_of(stream_key, dims, cuts, -0.22, 0.18) * drawn
    return jnp.clip(drawn, min=-limit, max=limit).astype(held_as)


def setup_inputs(seed: int = 0) -> dict:
    key_of = jax.random.split(jax.random.key(seed), 13)
    tokens = bell_draw(key_of[0], (ROWS, MODEL_SIZE), 1.0, 6.0, ((1, 16),))
    attn_gain = jnp.clip(1.0 + 0.18 * jax.random.normal(key_of[1], (MODEL_SIZE,), jnp.float32), 0.099609375, 1.8984375).astype(jnp.bfloat16)
    query_key_value_weight = bell_draw(key_of[2], (MODEL_SIZE, KEY_HEADS * (QUERY_PER_KV + 2) * HEAD_SIZE), MODEL_SIZE ** -0.5, 0.0625, ((0, 16), (1, 8)))
    paged_key_store = draw_paged_key_store(jax.random.fold_in(key_of[12], 71), 0)
    paged_value_store = bell_draw(key_of[4], (POOL_BLOCKS, KEY_HEADS, BLOCK_TOKENS, HEAD_SIZE), 1.0, 6.0, ((0, 16), (1, 8)))
    lengths = draw_lengths(jax.random.fold_in(key_of[12], 71), 0)
    block_table = draw_block_table(jax.random.fold_in(key_of[12], 71), 0)
    out_weight = bell_draw(key_of[7], (QUERY_HEADS * HEAD_SIZE, MODEL_SIZE), 0.08, 0.47851562, ((0, 8), (1, 16)))
    mlp_gain = jnp.clip(1.0 + 0.18 * jax.random.normal(key_of[8], (MODEL_SIZE,), jnp.float32), 0.099609375, 1.8984375).astype(jnp.bfloat16)
    gate_weight = bell_draw(key_of[9], (MODEL_SIZE, FF), MODEL_SIZE ** -0.5, 0.0625, ((0, 16), (1, 8)))
    up_weight = bell_draw(key_of[10], (MODEL_SIZE, FF), MODEL_SIZE ** -0.5, 0.0625, ((0, 16), (1, 8)))
    down_weight = bell_draw(key_of[11], (FF, MODEL_SIZE), FF ** -0.5, 0.03125, ((0, 8), (1, 16)))
    return dict(tokens=tokens, attn_gain=attn_gain, query_key_value_weight=query_key_value_weight, paged_key_store=paged_key_store, paged_value_store=paged_value_store, lengths=lengths, block_table=block_table, out_weight=out_weight, mlp_gain=mlp_gain, gate_weight=gate_weight, up_weight=up_weight, down_weight=down_weight)


EPSILON = 1e-05
ROPE_BASE = 500000.0

def rotate(values, position):
    half_dim = values.shape[-1] // 2
    inverse = jnp.exp(jnp.arange(half_dim, dtype=jnp.float32) * (-2.0 * math.log(ROPE_BASE) / values.shape[-1]))
    angle = position[..., None] * inverse
    cosine = jnp.cos(angle)
    sine = jnp.sin(angle)
    first = values[..., :half_dim]
    second = values[..., half_dim:]
    return jnp.concatenate([first * cosine - second * sine, second * cosine + first * sine], axis=-1)

def reference(tokens, attn_gain, query_key_value_weight, paged_key_store, paged_value_store, lengths, block_table, out_weight, mlp_gain, gate_weight, up_weight, down_weight):
    query_group = QUERY_HEADS // KEY_HEADS
    token_f = tokens.astype(jnp.float32)
    inverse_one = 1.0 / jnp.sqrt(lax.optimization_barrier(jnp.sum(token_f * token_f, axis=1)) / MODEL_SIZE + EPSILON)
    scaled_in = (token_f * attn_gain.astype(jnp.float32)).astype(jnp.bfloat16)
    projected_rows = jnp.dot(scaled_in, query_key_value_weight, preferred_element_type=jnp.float32) * inverse_one[:, None]
    projected_rows = projected_rows.reshape(REQUEST_COUNT, NEW_POSITIONS, KEY_HEADS, query_group + 2, HEAD_SIZE)
    position = (lengths[:, None] + jnp.arange(NEW_POSITIONS, dtype=jnp.int32)[None, :]).astype(jnp.float32)
    queries = rotate(projected_rows[:, :, :, :query_group], position[:, :, None, None]).astype(jnp.bfloat16)
    new_keys = rotate(projected_rows[:, :, :, query_group], position[:, :, None]).astype(jnp.bfloat16)
    new_values = projected_rows[:, :, :, query_group + 1].astype(jnp.bfloat16)
    scale = 1.0 / math.sqrt(HEAD_SIZE)
    causal = jnp.arange(NEW_POSITIONS)[None, :] <= jnp.arange(NEW_POSITIONS)[:, None]
    context_length = MAXB * BLOCK_TOKENS

    def attend(inputs):
        query_rows, key_rows, value_rows, table_row, length = inputs
        block_locations = jnp.maximum(table_row, 0).astype(jnp.int32)
        stored_keys = jnp.transpose(paged_key_store[block_locations], (1, 0, 2, 3)).reshape(KEY_HEADS, context_length, HEAD_SIZE).astype(jnp.float32)
        stored_values = jnp.transpose(paged_value_store[block_locations], (1, 0, 2, 3)).reshape(KEY_HEADS, context_length, HEAD_SIZE).astype(jnp.float32)
        query_f = query_rows.astype(jnp.float32)
        cached_scores = jnp.einsum('nkgd,kjd->kngj', query_f, stored_keys, precision=lax.Precision.HIGHEST) * scale
        valid = jnp.arange(context_length) < length
        cached_scores = jnp.where(valid, cached_scores, -jnp.inf)
        own_scores = jnp.einsum('nkgd,mkd->kngm', query_f, key_rows.astype(jnp.float32), precision=lax.Precision.HIGHEST) * scale
        own_scores = jnp.where(causal[None, :, None, :], own_scores, -jnp.inf)
        every = jnp.concatenate([cached_scores, own_scores], axis=-1)
        largest = lax.optimization_barrier(jnp.max(every, axis=-1, keepdims=True))
        weights = jnp.exp(every - largest)
        total = lax.optimization_barrier(jnp.sum(weights, axis=-1, keepdims=True))
        mixed = jnp.einsum('kngj,kjd->kngd', weights[..., :context_length], stored_values, precision=lax.Precision.HIGHEST)
        mixed = mixed + jnp.einsum('kngm,mkd->kngd', weights[..., context_length:], value_rows.astype(jnp.float32), precision=lax.Precision.HIGHEST)
        return jnp.transpose(mixed / total, (1, 0, 2, 3))
    attended = lax.map(attend, (queries, new_keys, new_values, block_table, lengths))
    attended = attended.reshape(REQUEST_COUNT * NEW_POSITIONS, QUERY_HEADS * HEAD_SIZE).astype(jnp.bfloat16)
    after_attn = (token_f + jnp.dot(attended, out_weight, preferred_element_type=jnp.float32)).astype(jnp.bfloat16)
    after_f = after_attn.astype(jnp.float32)
    inverse_two = 1.0 / jnp.sqrt(lax.optimization_barrier(jnp.sum(after_f * after_f, axis=1)) / MODEL_SIZE + EPSILON)
    scaled_mid = (after_f * mlp_gain.astype(jnp.float32)).astype(jnp.bfloat16)
    gate_part = jnp.dot(scaled_mid, gate_weight, preferred_element_type=jnp.float32) * inverse_two[:, None]
    up_part = jnp.dot(scaled_mid, up_weight, preferred_element_type=jnp.float32) * inverse_two[:, None]
    hidden = (jax.nn.silu(gate_part) * up_part).astype(jnp.bfloat16)
    return (after_f + jnp.dot(hidden, down_weight, preferred_element_type=jnp.float32)).astype(jnp.bfloat16)
```

```python
import functools
import math

import jax
import jax.numpy as jnp
import numpy as np
from jax import lax
from jax.experimental import pallas as pl
from jax.experimental.pallas import tpu as pltpu
from jax.sharding import PartitionSpec as P

MESH = pl.DeviceIdType.MESH
F32 = jnp.float32
BF16 = jnp.bfloat16

EPSILON = 1e-05
ROPE_BASE = 500000.0
FLOOR_SCORE = -1e30
LANES = 128
HEADS = 8
NEW = 4
REQUESTS = 4
GROUP = NEW * HEADS
OWNER = 256
TILE = 16
PIECES = 4

HALF_PI = (1.5703125, 0.000484466552734375, -6.397578377557687e-07)


def sine_cosine(angle):
    turns = jnp.floor(angle * (2.0 / math.pi) + 0.5)
    r = ((angle - turns * HALF_PI[0]) - turns * HALF_PI[1]) - turns * HALF_PI[2]
    z = r * r
    sine = r + r * z * (-1.6666654611e-1 + z * (8.3321608736e-3 + z * (-1.9515295891e-4)))
    cosine = 1.0 - 0.5 * z + z * z * (
        4.166664568298827e-2 + z * (-1.388731625493765e-3 + z * 2.443315711809948e-5)
    )
    quadrant = turns - 4.0 * jnp.floor(turns * 0.25)
    odd = (quadrant == 1.0) | (quadrant == 3.0)
    s, c = jnp.where(odd, cosine, sine), jnp.where(odd, sine, cosine)
    s = jnp.where(quadrant >= 2.0, -s, s)
    c = jnp.where((quadrant == 1.0) | (quadrant == 2.0), -c, c)
    return s, c


STEPS = 32000.0
FINE = 256.0


def code_of(value):
    return jnp.log(jnp.maximum(value, 1e-30)) * (FINE / math.log(2.0))


def value_of(code):
    return jnp.exp2(code * (1.0 / FINE))


def kernel(
    members,
    peers,
    model_width,
    lengths,
    tokens_hbm,
    gain_one,
    gain_two,
    freq_hbm,
    table_hbm,
    wqkv_hbm,
    keys_hbm,
    values_hbm,
    wout_hbm,
    wgate_hbm,
    wup_hbm,
    wdown_hbm,
    out_ref,
    tokens,
    freq,
    table,
    wqkv,
    keys,
    values,
    wout,
    wgate,
    wup,
    wdown,
    queries,
    codes,
    slot_codes,
    tops_ref,
    scores,
    s1,
    r1,
    s2,
    r2,
    s4,
    r4,
    s5,
    r5,
    token_lines,
    s5b,
    r5b,
    s5c,
    r5c,
    g6a,
    s6a,
    r6a,
    g6b,
    s6b,
    r6b,
    s7,
    r7,
    g7,
    s7b,
    r7b,
    s7c,
    r7c,
    code_sem,
    fetch_sem,
    send_sem,
    recv_sem,
):
    me = lax.axis_index("mem")
    mine = lax.axis_index("mp")
    rows = tokens.shape[0]
    slots = keys.shape[0]
    block_len = keys.shape[1]
    chunks = wgate.shape[1] // LANES
    half = s7.shape[0]

    barrier = pltpu.get_barrier_semaphore()
    for k in range(1, members):
        pl.semaphore_signal(
            barrier, inc=1, device_id={"mem": lax.rem(me + k, members)}, device_id_type=MESH
        )
    for k in range(1, peers):
        pl.semaphore_signal(
            barrier, inc=1, device_id={"mp": lax.rem(mine + k, peers)}, device_id_type=MESH
        )

    fetched = {}

    def fetch(name, source, target, pieces=1):
        size = target.shape[0] // pieces
        fetched[name] = []
        for p in range(pieces):
            index = sum(len(v) for v in fetched.values())
            part = pl.ds(p * size, size)
            copy = pltpu.make_async_copy(source.at[part], target.at[part], fetch_sem.at[index])
            copy.start()
            fetched[name].append(copy)

    def ready(*names):
        for name in names:
            for copy in fetched[name]:
                copy.wait()

    fetch("tokens", tokens_hbm, tokens)
    fetch("wqkv", wqkv_hbm, wqkv, PIECES)
    fetch("table", table_hbm, table)
    fetch("freq", freq_hbm, freq)

    def send_members(phase, source_of, target):
        for k in range(1, members):
            other = lax.rem(me + k, members)
            pltpu.make_async_remote_copy(
                src_ref=source_of(other),
                dst_ref=target,
                send_sem=send_sem.at[phase],
                recv_sem=recv_sem.at[phase],
                device_id={"mem": other},
                device_id_type=MESH,
            ).start()

    def send_peers(phase, source_of, target):
        for k in range(1, peers):
            other = lax.rem(mine + k, peers)
            pltpu.make_async_remote_copy(
                src_ref=source_of(other),
                dst_ref=target,
                send_sem=send_sem.at[phase],
                recv_sem=recv_sem.at[phase],
                device_id={"mp": other},
                device_id_type=MESH,
            ).start()

    cuts = tokens.shape[1] // LANES
    lines_own = rows // peers * cuts
    own_lines = pl.ds(pl.multiple_of(mine * lines_own, lines_own), lines_own)

    def spread(ref, array):
        for c in range(cuts):
            ref[pl.ds(c, rows, stride=cuts), :] = array[:, c * LANES : (c + 1) * LANES]

    def gather(ref):
        return jnp.concatenate([ref[pl.ds(c, rows, stride=cuts), :] for c in range(cuts)], axis=1)

    def sum_peers(phase, partial, residual, staged, landed, rounded, whole, between=None):
        spread(staged, partial)
        send_peers(
            phase, lambda other: staged.at[pl.ds(other * lines_own, lines_own)], landed.at[mine]
        )
        landed[mine] = staged[own_lines, :]
        if between is not None:
            between()
        wait_bytes(landed.at[pl.ds(0, peers - 1)], recv_sem.at[phase])
        total = landed[0]
        for j in range(1, peers):
            total = total + landed[j]
        share = (residual + total).astype(BF16).astype(F32)
        rounded[...] = share
        whole[own_lines, :] = share
        send_peers(phase + 1, lambda other: rounded, whole.at[own_lines])
        wait_bytes(whole.at[pl.ds(0, (peers - 1) * lines_own)], recv_sem.at[phase + 1])
        return share, gather(whole)

    def wait_bytes(window, semaphore):
        pltpu.make_async_copy(window, window, semaphore).wait()

    ready("tokens")
    token_f = tokens[...].astype(F32)
    scaled_in = (token_f * gain_one[...].astype(F32)[None, :]).astype(BF16)
    square_one = jnp.sum(token_f * token_f, axis=1, keepdims=True)
    ready("wqkv")
    fetch("keys", keys_hbm.at[:, 0], keys, PIECES)
    fetch("values", values_hbm.at[:, 0], values, PIECES)
    projected = jnp.dot(scaled_in, wqkv[...], preferred_element_type=F32)
    for c in range(HEADS + 2):
        s1[pl.ds(c, rows, stride=rows), :] = projected[:, c * LANES : (c + 1) * LANES]
    s1[pl.ds(HEADS + 2, rows, stride=rows), :] = jnp.broadcast_to(square_one, (rows, LANES))

    pl.semaphore_wait(barrier, members - 1 + peers - 1)

    used = HEADS + 3
    send_members(
        0, lambda other: s1.at[pl.ds(other * rows, used)], r1.at[me, pl.ds(0, used)]
    )
    r1[me] = s1[pl.ds(pl.multiple_of(me * rows, rows), rows), :]

    fetch("wout", wout_hbm, wout, 2)
    fetch("wgate", wgate_hbm, wgate, PIECES)
    fetch("wup", wup_hbm, wup, PIECES)
    fetch("wdown", wdown_hbm, wdown, PIECES)

    request, place = me // NEW, lax.rem(me, NEW)
    ready("freq")
    position = (lengths[request] + place).astype(F32)
    sine, cosine = sine_cosine(position * freq[...])
    lane_row = lax.broadcasted_iota(jnp.int32, (1, LANES), 1)
    sine = jnp.where(lane_row < LANES // 2, -sine, sine)

    ready("table")
    first_slot = me * slots
    max_blocks = table.shape[1]
    block_start = lax.broadcasted_iota(jnp.int32, (1, max_blocks), 1) * block_len
    slot_ids = first_slot + lax.broadcasted_iota(jnp.int32, (slots, max_blocks), 0)
    code = jnp.zeros((slots, max_blocks), jnp.int32)
    for r in range(REQUESTS):
        held = jnp.clip(lengths[r] - block_start, 0, block_len)
        held = jnp.where(held > 0, held + r * OWNER, 0)
        code = code + jnp.where(table[r : r + 1, :] == slot_ids, held, 0)
    code = jnp.sum(code, axis=1, keepdims=True)
    diagonal = lax.broadcasted_iota(jnp.int32, (slots, slots), 0) == lax.broadcasted_iota(
        jnp.int32, (slots, slots), 1
    )
    code = jnp.sum(jnp.where(diagonal, code, 0), axis=0, keepdims=True)
    owner_row = code // OWNER
    codes[0:1, :] = code
    to_scalars = pltpu.make_async_copy(codes, slot_codes, code_sem)
    to_scalars.start()

    wait_bytes(r1.at[pl.ds(0, members - 1), pl.ds(0, used)], recv_sem.at[0])
    total = r1[0]
    for j in range(1, members):
        total = total + r1[j]
    inverse_one = 1.0 / jnp.sqrt(total[HEADS + 2 : HEADS + 3, :] / model_width + EPSILON)
    total = total * inverse_one
    turned = total * cosine + pltpu.roll(total, LANES // 2, 1) * sine
    head_row = lax.broadcasted_iota(jnp.int32, total.shape, 0)
    s2[...] = jnp.where(head_row <= HEADS, turned, total).astype(BF16)
    r2[me] = s2[...]
    send_members(1, lambda other: s2, r2.at[me])
    wait_bytes(r2.at[pl.ds(0, members - 1)], recv_sem.at[1])

    for r in range(REQUESTS):
        queries[r] = jnp.concatenate(
            [r2[r * NEW + t].astype(F32)[:HEADS] for t in range(NEW)], axis=0
        ).astype(BF16)
    factor = math.log2(math.e) / math.sqrt(LANES)
    lane_group = lax.broadcasted_iota(jnp.int32, (GROUP, LANES), 1)
    to_scalars.wait()
    ready("keys")

    def slot_of(slot):
        value = slot_codes[0, slot]
        return value // OWNER, lax.rem(value, OWNER)

    def score_step(step, best):
        for j in range(TILE):
            slot = step * TILE + j
            owner, count = slot_of(slot)
            score = lax.dot_general(
                queries[owner],
                keys[slot],
                (((1,), (1,)), ((), ())),
                preferred_element_type=F32,
            )
            score = jnp.where(lane_group < count, score, FLOOR_SCORE)
            scores[slot] = score
            best = jnp.where(lane_group == slot, jnp.max(score, axis=1, keepdims=True), best)
        return best

    floor = jnp.full((GROUP, LANES), FLOOR_SCORE, F32)
    slot_best = lax.fori_loop(0, slots // TILE, score_step, floor)
    best = []
    for r in range(REQUESTS):
        own = jnp.where(owner_row == r, slot_best, FLOOR_SCORE)
        best.append(jnp.broadcast_to(jnp.max(own, axis=1, keepdims=True), (GROUP, LANES)))
        tops_ref[r] = best[r]
    ready("values")

    def value_step(step, carry):
        sums, mixed = carry
        line = []
        for j in range(TILE):
            slot = step * TILE + j
            owner, _ = slot_of(slot)
            weight = jnp.exp2((scores[slot] - tops_ref[owner]) * factor)
            sums = jnp.where(lane_group == slot, jnp.sum(weight, axis=1, keepdims=True), sums)
            weight = weight.astype(BF16)
            line.append(
                jnp.concatenate(
                    [jnp.where(owner == r, weight, jnp.zeros_like(weight)) for r in range(REQUESTS)],
                    axis=0,
                )
            )
        block = values[pl.ds(step * TILE, TILE)].reshape(TILE * block_len, LANES)
        mixed = mixed + jnp.dot(
            jnp.concatenate(line, axis=1), block, preferred_element_type=F32
        )
        return sums, mixed

    slot_sums, mixed = lax.fori_loop(
        0,
        slots // TILE,
        value_step,
        (jnp.zeros((GROUP, LANES), F32), jnp.zeros((REQUESTS * GROUP, LANES), F32)),
    )
    lane_tile = lax.broadcasted_iota(jnp.int32, (HEADS, LANES), 1)
    for r in range(REQUESTS):
        own = jnp.where(owner_row == r, slot_sums, 0.0)
        whole = jnp.broadcast_to(jnp.sum(own, axis=1, keepdims=True), (GROUP, LANES))
        for t in range(NEW):
            part = slice(t * HEADS, (t + 1) * HEADS)
            i = r * NEW + t
            s4[i, :HEADS, :] = mixed[i * HEADS : (i + 1) * HEADS]
            s4[i, HEADS:, :] = jnp.where(lane_tile < LANES // 2, best[r][part], whole[part])
    send_members(2, lambda other: s4.at[other], r4.at[me])
    r4[me] = s4[me]

    row_queries = r2[me].astype(F32)[:HEADS]
    own_scores, own_values = [], []
    for t in range(NEW):
        fresh = r2[request * NEW + t].astype(F32)
        score = jnp.sum(row_queries * fresh[HEADS : HEADS + 1], axis=1, keepdims=True)
        score = jnp.broadcast_to(score, (HEADS, LANES))
        own_scores.append(jnp.where(t <= place, score, FLOOR_SCORE))
        own_values.append(fresh[HEADS + 1 : HEADS + 2])
    top = functools.reduce(jnp.maximum, own_scores)

    wait_bytes(r4.at[pl.ds(0, members - 1)], recv_sem.at[2])
    tops, wholes = [], []
    for j in range(members):
        both = r4[j, HEADS:, :]
        swapped = pltpu.roll(both, LANES // 2, 1)
        tops.append(jnp.where(lane_tile < LANES // 2, both, swapped))
        wholes.append(jnp.where(lane_tile < LANES // 2, swapped, both))
    top = functools.reduce(jnp.maximum, tops, top)
    mix, whole = jnp.zeros((HEADS, LANES), F32), jnp.zeros((HEADS, LANES), F32)
    for t in range(NEW):
        weight = jnp.exp2((own_scores[t] - top) * factor)
        whole = whole + weight
        mix = mix + weight * own_values[t]
    for j in range(members):
        shrink = jnp.exp2((tops[j] - top) * factor)
        whole = whole + wholes[j] * shrink
        mix = mix + r4[j, :HEADS, :] * shrink
    s5[...] = mix / whole
    own_rows = pl.ds(pl.multiple_of(me * HEADS, HEADS), HEADS)
    r5[own_rows, :] = s5[...]
    send_members(3, lambda other: s5, r5.at[own_rows])
    ready("wout")
    wait_bytes(r5.at[pl.ds(0, (members - 1) * HEADS)], recv_sem.at[3])

    attended = jnp.concatenate(
        [r5[pl.ds(h, rows, stride=HEADS), :].astype(BF16) for h in range(HEADS)], axis=1
    )
    spread(token_lines, token_f)
    share, after_f = sum_peers(
        4,
        jnp.dot(attended, wout[...], preferred_element_type=F32),
        token_lines[own_lines, :],
        s5b,
        r5b,
        s5c,
        r5c,
    )
    ready("wgate", "wup")

    scaled_mid = (after_f * gain_two[...].astype(F32)[None, :]).astype(BF16)
    square_mid = jnp.sum(after_f * after_f, axis=1, keepdims=True)
    columns = 4 * LANES
    line_ids = lax.broadcasted_iota(jnp.int32, (half, LANES), 0)
    square_code = code_of(square_mid)
    square_whole = jnp.floor(square_code)
    square_rest = jnp.floor((square_code - square_whole) * STEPS + 0.5)
    for index, (weight, staged, packed, landed) in enumerate(
        ((wgate, g6a, s6a, r6a), (wup, g6b, s6b, r6b))
    ):
        largest = jnp.zeros((rows, LANES), F32)
        for n in range(weight.shape[1] // columns):
            part = jnp.dot(
                scaled_mid,
                weight[:, n * columns : (n + 1) * columns],
                preferred_element_type=F32,
            )
            for c in range(columns // LANES):
                line = n * (columns // LANES) + c
                piece = part[:, c * LANES : (c + 1) * LANES]
                staged[pl.ds(line, rows, stride=half), :] = piece
                largest = jnp.maximum(largest, jnp.abs(piece))
        unit_code = jnp.ceil(code_of(jnp.max(largest, axis=1, keepdims=True)))
        to_steps = jnp.broadcast_to(STEPS / value_of(unit_code), (rows, LANES))
        for line, extra in enumerate((unit_code, square_whole, square_rest)):
            staged[pl.ds(chunks + line, rows, stride=half), :] = jnp.broadcast_to(
                extra, (rows, LANES)
            )
        for i in range(rows):
            line = staged[i * half : (i + 1) * half, :]
            line = jnp.where(
                line_ids < chunks, jnp.floor(line * to_steps[i : i + 1] + 0.5), line
            )
            packed[i] = line.astype(jnp.int32).astype(jnp.int16)
        landed[me] = packed[me]
        send_members(6 + index, lambda other: packed.at[other], landed.at[me])

    def add_up(landed):
        whole, square = jnp.zeros((half, LANES), F32), jnp.zeros((1, LANES), F32)
        for j in range(members):
            part = landed[j].astype(jnp.int32).astype(F32)
            codes = part[chunks : chunks + 3]
            whole = whole + part * (value_of(codes[0:1]) * (1.0 / STEPS))
            square = square + value_of(codes[1:2] + codes[2:3] * (1.0 / STEPS))
        return whole, square

    wait_bytes(r6a.at[pl.ds(0, members - 1)], recv_sem.at[6])
    gate, square = add_up(r6a)
    inverse_two = 1.0 / jnp.sqrt(square / model_width + EPSILON)
    gate = gate * inverse_two
    gate = gate / (1.0 + jnp.exp(-gate))
    wait_bytes(r6b.at[pl.ds(0, members - 1)], recv_sem.at[7])
    up, _ = add_up(r6b)
    s7[...] = (gate * (up * inverse_two)).astype(BF16)
    r7[me] = s7[...]
    send_members(8, lambda other: s7, r7.at[me])
    ready("wdown")
    wait_bytes(r7.at[pl.ds(0, members - 1)], recv_sem.at[8])

    for i in range(rows):
        g7[i * half : (i + 1) * half, :] = r7[i].astype(F32)
    down = jnp.zeros((rows, wdown.shape[1]), F32)
    for n in range(chunks // 4):
        hidden = jnp.concatenate(
            [g7[pl.ds(n * 4 + c, rows, stride=half), :].astype(BF16) for c in range(4)], axis=1
        )
        down = down + jnp.dot(
            hidden, wdown[n * 4 * LANES : (n + 1) * 4 * LANES, :], preferred_element_type=F32
        )
    _, result = sum_peers(9, down, share, s7b, r7b, s7c, r7c)
    out_ref[...] = result.astype(BF16)

    wait_bytes(r1.at[pl.ds(0, members - 1), pl.ds(0, used)], send_sem.at[0])
    wait_bytes(r2.at[pl.ds(0, members - 1)], send_sem.at[1])
    wait_bytes(r4.at[pl.ds(0, members - 1)], send_sem.at[2])
    wait_bytes(r5.at[pl.ds(0, (members - 1) * HEADS)], send_sem.at[3])
    for phase, landed, whole in ((4, r5b, r5c), (9, r7b, r7c)):
        wait_bytes(landed.at[pl.ds(0, peers - 1)], send_sem.at[phase])
        wait_bytes(whole.at[pl.ds(0, (peers - 1) * lines_own)], send_sem.at[phase + 1])
    for phase, landed in ((6, r6a), (7, r6b), (8, r7)):
        wait_bytes(landed.at[pl.ds(0, members - 1)], send_sem.at[phase])


def local(
    members,
    peers,
    tokens,
    attn_gain,
    query_key_value_weight,
    paged_key_store,
    paged_value_store,
    lengths,
    block_table,
    out_weight,
    mlp_gain,
    gate_weight,
    up_weight,
    down_weight,
):
    rows, width_part = tokens.shape
    slots, _, block_len, head_dim = paged_key_store.shape
    hidden_part = gate_weight.shape[1]
    half = (hidden_part // LANES + 3 + 15) // 16 * 16
    exponents = np.arange(head_dim // 2, dtype=np.float32) * np.float32(
        -2.0 * math.log(ROPE_BASE) / head_dim
    )
    inverse = np.exp(exponents.astype(np.float64)).astype(np.float32)
    freq = jnp.asarray(np.concatenate([inverse, inverse])[None, :])

    any_spec = pl.BlockSpec(memory_space=pl.ANY)
    vmem_spec = pl.BlockSpec(memory_space=pltpu.VMEM)
    cuts = width_part // LANES
    lines_own = rows // peers * cuts
    scratch = [
        pltpu.VMEM(tokens.shape, BF16),
        pltpu.VMEM(freq.shape, F32),
        pltpu.VMEM(block_table.shape, jnp.int32),
        pltpu.VMEM(query_key_value_weight.shape, BF16),
        pltpu.VMEM((slots, block_len, head_dim), BF16),
        pltpu.VMEM((slots, block_len, head_dim), BF16),
        pltpu.VMEM(out_weight.shape, BF16),
        pltpu.VMEM(gate_weight.shape, BF16),
        pltpu.VMEM(up_weight.shape, BF16),
        pltpu.VMEM(down_weight.shape, BF16),
        pltpu.VMEM((REQUESTS, GROUP, head_dim), BF16),
        pltpu.VMEM((8, slots), jnp.int32),
        pltpu.SMEM((8, slots), jnp.int32),
        pltpu.VMEM((REQUESTS, GROUP, LANES), F32),
        pltpu.VMEM((slots, GROUP, LANES), F32),
        pltpu.VMEM((rows * rows, LANES), F32),
        pltpu.VMEM((members, rows, LANES), F32),
        pltpu.VMEM((16, LANES), BF16),
        pltpu.VMEM((members, 16, LANES), BF16),
        pltpu.VMEM((members, 2 * HEADS, LANES), F32),
        pltpu.VMEM((members, 2 * HEADS, LANES), F32),
        pltpu.VMEM((HEADS, LANES), F32),
        pltpu.VMEM((members * HEADS, LANES), F32),
        pltpu.VMEM((rows * cuts, LANES), F32),
        pltpu.VMEM((rows * cuts, LANES), F32),
        pltpu.VMEM((peers, lines_own, LANES), F32),
        pltpu.VMEM((lines_own, LANES), F32),
        pltpu.VMEM((rows * cuts, LANES), F32),
        pltpu.VMEM((rows * half, LANES), F32),
        pltpu.VMEM((members, half, LANES), jnp.int16),
        pltpu.VMEM((members, half, LANES), jnp.int16),
        pltpu.VMEM((rows * half, LANES), F32),
        pltpu.VMEM((members, half, LANES), jnp.int16),
        pltpu.VMEM((members, half, LANES), jnp.int16),
        pltpu.VMEM((half, LANES), BF16),
        pltpu.VMEM((members, half, LANES), BF16),
        pltpu.VMEM((rows * half, LANES), F32),
        pltpu.VMEM((rows * cuts, LANES), F32),
        pltpu.VMEM((peers, lines_own, LANES), F32),
        pltpu.VMEM((lines_own, LANES), F32),
        pltpu.VMEM((rows * cuts, LANES), F32),
        pltpu.SemaphoreType.DMA,
        pltpu.SemaphoreType.DMA((3 + 6 * PIECES + 2,)),
        pltpu.SemaphoreType.DMA((11,)),
        pltpu.SemaphoreType.DMA((11,)),
    ]
    return pl.pallas_call(
        functools.partial(kernel, members, peers, width_part * members),
        out_shape=jax.ShapeDtypeStruct(tokens.shape, BF16),
        in_specs=[
            pl.BlockSpec(memory_space=pltpu.SMEM),
            any_spec,
            vmem_spec,
            vmem_spec,
        ]
        + [any_spec] * 9,
        out_specs=vmem_spec,
        scratch_shapes=scratch,
        compiler_params=pltpu.CompilerParams(
            collective_id=0, has_side_effects=True, vmem_limit_bytes=56 * 1024 * 1024
        ),
        name="decoder_layer",
    )(
        lengths,
        tokens,
        attn_gain,
        mlp_gain,
        freq,
        block_table,
        query_key_value_weight,
        paged_key_store,
        paged_value_store,
        out_weight,
        gate_weight,
        up_weight,
        down_weight,
    )


def solution(mesh):
    return jax.shard_map(
        functools.partial(local, mesh.shape["mem"], mesh.shape["mp"]),
        mesh=mesh,
        in_specs=(
            P(None, "mem"),
            P("mem"),
            P("mem", "mp"),
            P("mem", "mp", None, None),
            P("mem", "mp", None, None),
            P(),
            P(),
            P("mp", "mem"),
            P("mem"),
            P("mem", "mp"),
            P("mem", "mp"),
            P("mp", "mem"),
        ),
        out_specs=P(None, "mem"),
        check_vma=False,
    )
```

```python
import functools
import math

import jax
import jax.numpy as jnp
import numpy as np
from jax import lax
from jax.experimental import pallas as pl
from jax.experimental.pallas import tpu as pltpu
from jax.sharding import PartitionSpec as P

MESH = pl.DeviceIdType.MESH
F32 = jnp.float32
BF16 = jnp.bfloat16

EPSILON = 1e-05
ROPE_BASE = 500000.0
FLOOR_SCORE = -1e30
LANES = 128
HEADS = 8
NEW = 4
REQUESTS = 4
GROUP = NEW * HEADS
OWNER = 256
TILE = 16
PIECES = 4

HALF_PI = (1.5703125, 0.000484466552734375, -6.397578377557687e-07)


def sine_cosine(angle):
    turns = jnp.floor(angle * (2.0 / math.pi) + 0.5)
    r = ((angle - turns * HALF_PI[0]) - turns * HALF_PI[1]) - turns * HALF_PI[2]
    z = r * r
    sine = r + r * z * (-1.6666654611e-1 + z * (8.3321608736e-3 + z * (-1.9515295891e-4)))
    cosine = 1.0 - 0.5 * z + z * z * (
        4.166664568298827e-2 + z * (-1.388731625493765e-3 + z * 2.443315711809948e-5)
    )
    quadrant = turns - 4.0 * jnp.floor(turns * 0.25)
    odd = (quadrant == 1.0) | (quadrant == 3.0)
    s, c = jnp.where(odd, cosine, sine), jnp.where(odd, sine, cosine)
    s = jnp.where(quadrant >= 2.0, -s, s)
    c = jnp.where((quadrant == 1.0) | (quadrant == 2.0), -c, c)
    return s, c


STEPS = 32000.0
FINE = 256.0


def code_of(value):
    return jnp.log(jnp.maximum(value, 1e-30)) * (FINE / math.log(2.0))


def value_of(code):
    return jnp.exp2(code * (1.0 / FINE))


def kernel(
    members,
    peers,
    model_width,
    lengths,
    tokens_hbm,
    gain_one,
    gain_two,
    freq_hbm,
    table_hbm,
    wqkv_hbm,
    keys_hbm,
    values_hbm,
    wout_hbm,
    wgate_hbm,
    wup_hbm,
    wdown_hbm,
    out_ref,
    tokens,
    freq,
    table,
    wqkv,
    keys,
    values,
    wout,
    wgate,
    wup,
    wdown,
    queries,
    codes,
    slot_codes,
    tops_ref,
    scores,
    s1,
    r1,
    s2,
    r2,
    s4,
    r4,
    s5,
    r5,
    s5b,
    r5b,
    g6a,
    s6a,
    r6a,
    g6b,
    s6b,
    r6b,
    s7,
    r7,
    g7,
    s7b,
    r7b,
    code_sem,
    fetch_sem,
    send_sem,
    recv_sem,
):
    me = lax.axis_index("mem")
    mine = lax.axis_index("mp")
    rows = tokens.shape[0]
    slots = keys.shape[0]
    block_len = keys.shape[1]
    chunks = wgate.shape[1] // LANES
    half = s7.shape[0]

    barrier = pltpu.get_barrier_semaphore()
    for k in range(1, members):
        pl.semaphore_signal(
            barrier, inc=1, device_id={"mem": lax.rem(me + k, members)}, device_id_type=MESH
        )
    for k in range(1, peers):
        pl.semaphore_signal(
            barrier, inc=1, device_id={"mp": lax.rem(mine + k, peers)}, device_id_type=MESH
        )

    fetched = {}

    def fetch(name, source, target, pieces=1):
        size = target.shape[0] // pieces
        fetched[name] = []
        for p in range(pieces):
            index = sum(len(v) for v in fetched.values())
            part = pl.ds(p * size, size)
            copy = pltpu.make_async_copy(source.at[part], target.at[part], fetch_sem.at[index])
            copy.start()
            fetched[name].append(copy)

    def ready(*names):
        for name in names:
            for copy in fetched[name]:
                copy.wait()

    fetch("tokens", tokens_hbm, tokens)
    fetch("wqkv", wqkv_hbm, wqkv, PIECES)
    fetch("table", table_hbm, table)
    fetch("freq", freq_hbm, freq)

    def send_members(phase, source_of, target):
        for k in range(1, members):
            other = lax.rem(me + k, members)
            pltpu.make_async_remote_copy(
                src_ref=source_of(other),
                dst_ref=target,
                send_sem=send_sem.at[phase],
                recv_sem=recv_sem.at[phase],
                device_id={"mem": other},
                device_id_type=MESH,
            ).start()

    def send_peers(phase, source, target):
        for k in range(1, peers):
            other = lax.rem(mine + k, peers)
            pltpu.make_async_remote_copy(
                src_ref=source,
                dst_ref=target,
                send_sem=send_sem.at[phase],
                recv_sem=recv_sem.at[phase],
                device_id={"mp": other},
                device_id_type=MESH,
            ).start()

    width = tokens.shape[1]

    def sum_peers(phase, partial, staged, landed):
        unit_code = jnp.ceil(code_of(jnp.max(jnp.abs(partial), axis=1, keepdims=True)))
        steps = jnp.floor(partial * (STEPS / value_of(unit_code)) + 0.5)
        staged[:, :width] = steps.astype(jnp.int32).astype(jnp.int16)
        staged[:, width:] = (
            jnp.broadcast_to(unit_code, (rows, LANES)).astype(jnp.int32).astype(jnp.int16)
        )
        send_peers(phase, staged, landed.at[mine])
        landed[mine] = staged[...]
        wait_bytes(landed.at[pl.ds(0, peers - 1)], recv_sem.at[phase])
        total = jnp.zeros((rows, width), F32)
        for j in range(peers):
            part = landed[j].astype(jnp.int32).astype(F32)
            unit = value_of(part[:, width:]) * (1.0 / STEPS)
            total = total + part[:, :width] * jnp.concatenate([unit] * (width // LANES), axis=1)
        return total

    def wait_bytes(window, semaphore):
        pltpu.make_async_copy(window, window, semaphore).wait()

    ready("tokens")
    token_f = tokens[...].astype(F32)
    scaled_in = (token_f * gain_one[...].astype(F32)[None, :]).astype(BF16)
    square_one = jnp.sum(token_f * token_f, axis=1, keepdims=True)
    ready("wqkv")
    projected = jnp.dot(scaled_in, wqkv[...], preferred_element_type=F32)
    for c in range(HEADS + 2):
        s1[pl.ds(c, rows, stride=rows), :] = projected[:, c * LANES : (c + 1) * LANES]
    s1[pl.ds(HEADS + 2, rows, stride=rows), :] = jnp.broadcast_to(square_one, (rows, LANES))

    pl.semaphore_wait(barrier, members - 1 + peers - 1)

    used = HEADS + 3
    send_members(
        0, lambda other: s1.at[pl.ds(other * rows, used)], r1.at[me, pl.ds(0, used)]
    )
    r1[me] = s1[pl.ds(pl.multiple_of(me * rows, rows), rows), :]

    fetch("keys", keys_hbm.at[:, 0], keys, PIECES)
    fetch("values", values_hbm.at[:, 0], values, PIECES)

    request, place = me // NEW, lax.rem(me, NEW)
    ready("freq")
    position = (lengths[request] + place).astype(F32)
    sine, cosine = sine_cosine(position * freq[...])
    lane_row = lax.broadcasted_iota(jnp.int32, (1, LANES), 1)
    sine = jnp.where(lane_row < LANES // 2, -sine, sine)

    ready("table")
    first_slot = me * slots
    max_blocks = table.shape[1]
    block_start = lax.broadcasted_iota(jnp.int32, (1, max_blocks), 1) * block_len
    slot_ids = first_slot + lax.broadcasted_iota(jnp.int32, (slots, max_blocks), 0)
    code = jnp.zeros((slots, max_blocks), jnp.int32)
    for r in range(REQUESTS):
        held = jnp.clip(lengths[r] - block_start, 0, block_len)
        held = jnp.where(held > 0, held + r * OWNER, 0)
        code = code + jnp.where(table[r : r + 1, :] == slot_ids, held, 0)
    code = jnp.sum(code, axis=1, keepdims=True)
    diagonal = lax.broadcasted_iota(jnp.int32, (slots, slots), 0) == lax.broadcasted_iota(
        jnp.int32, (slots, slots), 1
    )
    code = jnp.sum(jnp.where(diagonal, code, 0), axis=0, keepdims=True)
    owner_row = code // OWNER
    codes[0:1, :] = code
    to_scalars = pltpu.make_async_copy(codes, slot_codes, code_sem)
    to_scalars.start()

    wait_bytes(r1.at[pl.ds(0, members - 1), pl.ds(0, used)], recv_sem.at[0])
    total = r1[0]
    for j in range(1, members):
        total = total + r1[j]
    inverse_one = 1.0 / jnp.sqrt(total[HEADS + 2 : HEADS + 3, :] / model_width + EPSILON)
    total = total * inverse_one
    turned = total * cosine + pltpu.roll(total, LANES // 2, 1) * sine
    head_row = lax.broadcasted_iota(jnp.int32, total.shape, 0)
    s2[...] = jnp.where(head_row <= HEADS, turned, total).astype(BF16)
    r2[me] = s2[...]
    send_members(1, lambda other: s2, r2.at[me])
    fetch("wout", wout_hbm, wout, 2)
    fetch("wgate", wgate_hbm, wgate, PIECES)
    fetch("wup", wup_hbm, wup, PIECES)
    fetch("wdown", wdown_hbm, wdown, PIECES)
    wait_bytes(r2.at[pl.ds(0, members - 1)], recv_sem.at[1])

    for r in range(REQUESTS):
        queries[r] = jnp.concatenate(
            [r2[r * NEW + t].astype(F32)[:HEADS] for t in range(NEW)], axis=0
        ).astype(BF16)
    factor = math.log2(math.e) / math.sqrt(LANES)
    lane_group = lax.broadcasted_iota(jnp.int32, (GROUP, LANES), 1)
    to_scalars.wait()
    ready("keys")

    def slot_of(slot):
        value = slot_codes[0, slot]
        return value // OWNER, lax.rem(value, OWNER)

    def score_step(step, best):
        for j in range(TILE):
            slot = step * TILE + j
            owner, count = slot_of(slot)
            score = lax.dot_general(
                queries[owner],
                keys[slot],
                (((1,), (1,)), ((), ())),
                preferred_element_type=F32,
            )
            score = jnp.where(lane_group < count, score, FLOOR_SCORE)
            scores[slot] = score
            best = jnp.where(lane_group == slot, jnp.max(score, axis=1, keepdims=True), best)
        return best

    floor = jnp.full((GROUP, LANES), FLOOR_SCORE, F32)
    slot_best = lax.fori_loop(0, slots // TILE, score_step, floor)
    best = []
    for r in range(REQUESTS):
        own = jnp.where(owner_row == r, slot_best, FLOOR_SCORE)
        best.append(jnp.broadcast_to(jnp.max(own, axis=1, keepdims=True), (GROUP, LANES)))
        tops_ref[r] = best[r]
    ready("values")

    def value_step(step, carry):
        sums, mixed = carry
        line = []
        for j in range(TILE):
            slot = step * TILE + j
            owner, _ = slot_of(slot)
            weight = jnp.exp2((scores[slot] - tops_ref[owner]) * factor)
            sums = jnp.where(lane_group == slot, jnp.sum(weight, axis=1, keepdims=True), sums)
            weight = weight.astype(BF16)
            line.append(
                jnp.concatenate(
                    [jnp.where(owner == r, weight, jnp.zeros_like(weight)) for r in range(REQUESTS)],
                    axis=0,
                )
            )
        block = values[pl.ds(step * TILE, TILE)].reshape(TILE * block_len, LANES)
        mixed = mixed + jnp.dot(
            jnp.concatenate(line, axis=1), block, preferred_element_type=F32
        )
        return sums, mixed

    slot_sums, mixed = lax.fori_loop(
        0,
        slots // TILE,
        value_step,
        (jnp.zeros((GROUP, LANES), F32), jnp.zeros((REQUESTS * GROUP, LANES), F32)),
    )
    lane_tile = lax.broadcasted_iota(jnp.int32, (HEADS, LANES), 1)
    for r in range(REQUESTS):
        own = jnp.where(owner_row == r, slot_sums, 0.0)
        whole = jnp.broadcast_to(jnp.sum(own, axis=1, keepdims=True), (GROUP, LANES))
        for t in range(NEW):
            part = slice(t * HEADS, (t + 1) * HEADS)
            i = r * NEW + t
            s4[i, :HEADS, :] = mixed[i * HEADS : (i + 1) * HEADS]
            s4[i, HEADS:, :] = jnp.where(lane_tile < LANES // 2, best[r][part], whole[part])
    send_members(2, lambda other: s4.at[other], r4.at[me])
    r4[me] = s4[me]

    row_queries = r2[me].astype(F32)[:HEADS]
    own_scores, own_values = [], []
    for t in range(NEW):
        fresh = r2[request * NEW + t].astype(F32)
        score = jnp.sum(row_queries * fresh[HEADS : HEADS + 1], axis=1, keepdims=True)
        score = jnp.broadcast_to(score, (HEADS, LANES))
        own_scores.append(jnp.where(t <= place, score, FLOOR_SCORE))
        own_values.append(fresh[HEADS + 1 : HEADS + 2])
    top = functools.reduce(jnp.maximum, own_scores)

    wait_bytes(r4.at[pl.ds(0, members - 1)], recv_sem.at[2])
    tops, wholes = [], []
    for j in range(members):
        both = r4[j, HEADS:, :]
        swapped = pltpu.roll(both, LANES // 2, 1)
        tops.append(jnp.where(lane_tile < LANES // 2, both, swapped))
        wholes.append(jnp.where(lane_tile < LANES // 2, swapped, both))
    top = functools.reduce(jnp.maximum, tops, top)
    mix, whole = jnp.zeros((HEADS, LANES), F32), jnp.zeros((HEADS, LANES), F32)
    for t in range(NEW):
        weight = jnp.exp2((own_scores[t] - top) * factor)
        whole = whole + weight
        mix = mix + weight * own_values[t]
    for j in range(members):
        shrink = jnp.exp2((tops[j] - top) * factor)
        whole = whole + wholes[j] * shrink
        mix = mix + r4[j, :HEADS, :] * shrink
    s5[...] = mix / whole
    own_rows = pl.ds(pl.multiple_of(me * HEADS, HEADS), HEADS)
    r5[own_rows, :] = s5[...]
    send_members(3, lambda other: s5, r5.at[own_rows])
    ready("wout")
    wait_bytes(r5.at[pl.ds(0, (members - 1) * HEADS)], recv_sem.at[3])

    attended = jnp.concatenate(
        [r5[pl.ds(h, rows, stride=HEADS), :].astype(BF16) for h in range(HEADS)], axis=1
    )
    partial = jnp.dot(attended, wout[...], preferred_element_type=F32)
    after_f = (token_f + sum_peers(4, partial, s5b, r5b)).astype(BF16).astype(F32)
    ready("wgate", "wup")

    scaled_mid = (after_f * gain_two[...].astype(F32)[None, :]).astype(BF16)
    square_mid = jnp.sum(after_f * after_f, axis=1, keepdims=True)
    columns = 4 * LANES
    line_ids = lax.broadcasted_iota(jnp.int32, (half, LANES), 0)
    square_code = code_of(square_mid)
    square_whole = jnp.floor(square_code)
    square_rest = jnp.floor((square_code - square_whole) * STEPS + 0.5)
    for index, (weight, staged, packed, landed) in enumerate(
        ((wgate, g6a, s6a, r6a), (wup, g6b, s6b, r6b))
    ):
        largest = jnp.zeros((rows, LANES), F32)
        for n in range(weight.shape[1] // columns):
            part = jnp.dot(
                scaled_mid,
                weight[:, n * columns : (n + 1) * columns],
                preferred_element_type=F32,
            )
            for c in range(columns // LANES):
                line = n * (columns // LANES) + c
                piece = part[:, c * LANES : (c + 1) * LANES]
                staged[pl.ds(line, rows, stride=half), :] = piece
                largest = jnp.maximum(largest, jnp.abs(piece))
        unit_code = jnp.ceil(code_of(jnp.max(largest, axis=1, keepdims=True)))
        to_steps = jnp.broadcast_to(STEPS / value_of(unit_code), (rows, LANES))
        for line, extra in enumerate((unit_code, square_whole, square_rest)):
            staged[pl.ds(chunks + line, rows, stride=half), :] = jnp.broadcast_to(
                extra, (rows, LANES)
            )
        for i in range(rows):
            line = staged[i * half : (i + 1) * half, :]
            line = jnp.where(
                line_ids < chunks, jnp.floor(line * to_steps[i : i + 1] + 0.5), line
            )
            packed[i] = line.astype(jnp.int32).astype(jnp.int16)
        landed[me] = packed[me]
        send_members(5 + index, lambda other: packed.at[other], landed.at[me])

    def add_up(landed):
        whole, square = jnp.zeros((half, LANES), F32), jnp.zeros((1, LANES), F32)
        for j in range(members):
            part = landed[j].astype(jnp.int32).astype(F32)
            codes = part[chunks : chunks + 3]
            whole = whole + part * (value_of(codes[0:1]) * (1.0 / STEPS))
            square = square + value_of(codes[1:2] + codes[2:3] * (1.0 / STEPS))
        return whole, square

    wait_bytes(r6a.at[pl.ds(0, members - 1)], recv_sem.at[5])
    gate, square = add_up(r6a)
    inverse_two = 1.0 / jnp.sqrt(square / model_width + EPSILON)
    gate = gate * inverse_two
    gate = gate / (1.0 + jnp.exp(-gate))
    wait_bytes(r6b.at[pl.ds(0, members - 1)], recv_sem.at[6])
    up, _ = add_up(r6b)
    s7[...] = (gate * (up * inverse_two)).astype(BF16)
    r7[me] = s7[...]
    send_members(7, lambda other: s7, r7.at[me])
    ready("wdown")
    wait_bytes(r7.at[pl.ds(0, members - 1)], recv_sem.at[7])

    for i in range(rows):
        g7[i * half : (i + 1) * half, :] = r7[i].astype(F32)
    down = jnp.zeros((rows, wdown.shape[1]), F32)
    for n in range(chunks // 4):
        hidden = jnp.concatenate(
            [g7[pl.ds(n * 4 + c, rows, stride=half), :].astype(BF16) for c in range(4)], axis=1
        )
        down = down + jnp.dot(
            hidden, wdown[n * 4 * LANES : (n + 1) * 4 * LANES, :], preferred_element_type=F32
        )
    out_ref[...] = (after_f + sum_peers(8, down, s7b, r7b)).astype(BF16)

    wait_bytes(r1.at[pl.ds(0, members - 1), pl.ds(0, used)], send_sem.at[0])
    wait_bytes(r2.at[pl.ds(0, members - 1)], send_sem.at[1])
    wait_bytes(r4.at[pl.ds(0, members - 1)], send_sem.at[2])
    wait_bytes(r5.at[pl.ds(0, (members - 1) * HEADS)], send_sem.at[3])
    for phase, landed in ((4, r5b), (8, r7b)):
        wait_bytes(landed.at[pl.ds(0, peers - 1)], send_sem.at[phase])
    for phase, landed in ((5, r6a), (6, r6b), (7, r7)):
        wait_bytes(landed.at[pl.ds(0, members - 1)], send_sem.at[phase])


def local(
    members,
    peers,
    tokens,
    attn_gain,
    query_key_value_weight,
    paged_key_store,
    paged_value_store,
    lengths,
    block_table,
    out_weight,
    mlp_gain,
    gate_weight,
    up_weight,
    down_weight,
):
    rows, width_part = tokens.shape
    slots, _, block_len, head_dim = paged_key_store.shape
    hidden_part = gate_weight.shape[1]
    half = (hidden_part // LANES + 3 + 15) // 16 * 16
    exponents = np.arange(head_dim // 2, dtype=np.float32) * np.float32(
        -2.0 * math.log(ROPE_BASE) / head_dim
    )
    inverse = np.exp(exponents.astype(np.float64)).astype(np.float32)
    freq = jnp.asarray(np.concatenate([inverse, inverse])[None, :])

    any_spec = pl.BlockSpec(memory_space=pl.ANY)
    vmem_spec = pl.BlockSpec(memory_space=pltpu.VMEM)
    scratch = [
        pltpu.VMEM(tokens.shape, BF16),
        pltpu.VMEM(freq.shape, F32),
        pltpu.VMEM(block_table.shape, jnp.int32),
        pltpu.VMEM(query_key_value_weight.shape, BF16),
        pltpu.VMEM((slots, block_len, head_dim), BF16),
        pltpu.VMEM((slots, block_len, head_dim), BF16),
        pltpu.VMEM(out_weight.shape, BF16),
        pltpu.VMEM(gate_weight.shape, BF16),
        pltpu.VMEM(up_weight.shape, BF16),
        pltpu.VMEM(down_weight.shape, BF16),
        pltpu.VMEM((REQUESTS, GROUP, head_dim), BF16),
        pltpu.VMEM((8, slots), jnp.int32),
        pltpu.SMEM((8, slots), jnp.int32),
        pltpu.VMEM((REQUESTS, GROUP, LANES), F32),
        pltpu.VMEM((slots, GROUP, LANES), F32),
        pltpu.VMEM((rows * rows, LANES), F32),
        pltpu.VMEM((members, rows, LANES), F32),
        pltpu.VMEM((16, LANES), BF16),
        pltpu.VMEM((members, 16, LANES), BF16),
        pltpu.VMEM((members, 2 * HEADS, LANES), F32),
        pltpu.VMEM((members, 2 * HEADS, LANES), F32),
        pltpu.VMEM((HEADS, LANES), F32),
        pltpu.VMEM((members * HEADS, LANES), F32),
        pltpu.VMEM((rows, width_part + LANES), jnp.int16),
        pltpu.VMEM((peers, rows, width_part + LANES), jnp.int16),
        pltpu.VMEM((rows * half, LANES), F32),
        pltpu.VMEM((members, half, LANES), jnp.int16),
        pltpu.VMEM((members, half, LANES), jnp.int16),
        pltpu.VMEM((rows * half, LANES), F32),
        pltpu.VMEM((members, half, LANES), jnp.int16),
        pltpu.VMEM((members, half, LANES), jnp.int16),
        pltpu.VMEM((half, LANES), BF16),
        pltpu.VMEM((members, half, LANES), BF16),
        pltpu.VMEM((rows * half, LANES), F32),
        pltpu.VMEM((rows, width_part + LANES), jnp.int16),
        pltpu.VMEM((peers, rows, width_part + LANES), jnp.int16),
        pltpu.SemaphoreType.DMA,
        pltpu.SemaphoreType.DMA((3 + 6 * PIECES + 2,)),
        pltpu.SemaphoreType.DMA((9,)),
        pltpu.SemaphoreType.DMA((9,)),
    ]
    return pl.pallas_call(
        functools.partial(kernel, members, peers, width_part * members),
        out_shape=jax.ShapeDtypeStruct(tokens.shape, BF16),
        in_specs=[
            pl.BlockSpec(memory_space=pltpu.SMEM),
            any_spec,
            vmem_spec,
            vmem_spec,
        ]
        + [any_spec] * 9,
        out_specs=vmem_spec,
        scratch_shapes=scratch,
        compiler_params=pltpu.CompilerParams(
            collective_id=0, has_side_effects=True, vmem_limit_bytes=56 * 1024 * 1024
        ),
        name="decoder_layer",
    )(
        lengths,
        tokens,
        attn_gain,
        mlp_gain,
        freq,
        block_table,
        query_key_value_weight,
        paged_key_store,
        paged_value_store,
        out_weight,
        gate_weight,
        up_weight,
        down_weight,
    )


def solution(mesh):
    return jax.shard_map(
        functools.partial(local, mesh.shape["mem"], mesh.shape["mp"]),
        mesh=mesh,
        in_specs=(
            P(None, "mem"),
            P("mem"),
            P("mem", "mp"),
            P("mem", "mp", None, None),
            P("mem", "mp", None, None),
            P(),
            P(),
            P("mp", "mem"),
            P("mem"),
            P("mem", "mp"),
            P("mem", "mp"),
            P("mp", "mem"),
        ),
        out_specs=P(None, "mem"),
        check_vma=False,
    )
```

```python
import functools
import math

import jax
import jax.numpy as jnp
import numpy as np
from jax import lax
from jax.experimental import pallas as pl
from jax.experimental.pallas import tpu as pltpu
from jax.sharding import PartitionSpec as P

MESH = pl.DeviceIdType.MESH
F32 = jnp.float32
BF16 = jnp.bfloat16

EPSILON = 1e-05
ROPE_BASE = 500000.0
FLOOR_SCORE = -1e30
LANES = 128
HEADS = 8
NEW = 4
REQUESTS = 4
GROUP = NEW * HEADS
OWNER = 256
VALUE_TILE = 8
TILE = 16
GROUPS = 4
LINES = 8
PIECES = 4

HALF_PI = (1.5703125, 0.000484466552734375, -6.397578377557687e-07)


def sine_cosine(angle):
    turns = jnp.floor(angle * (2.0 / math.pi) + 0.5)
    r = ((angle - turns * HALF_PI[0]) - turns * HALF_PI[1]) - turns * HALF_PI[2]
    z = r * r
    sine = r + r * z * (-1.6666654611e-1 + z * (8.3321608736e-3 + z * (-1.9515295891e-4)))
    cosine = 1.0 - 0.5 * z + z * z * (
        4.166664568298827e-2 + z * (-1.388731625493765e-3 + z * 2.443315711809948e-5)
    )
    quadrant = turns - 4.0 * jnp.floor(turns * 0.25)
    odd = (quadrant == 1.0) | (quadrant == 3.0)
    s, c = jnp.where(odd, cosine, sine), jnp.where(odd, sine, cosine)
    s = jnp.where(quadrant >= 2.0, -s, s)
    c = jnp.where((quadrant == 1.0) | (quadrant == 2.0), -c, c)
    return s, c


STEPS = 32000.0
FINE = 256.0


def code_of(value):
    return jnp.log(jnp.maximum(value, 1e-30)) * (FINE / math.log(2.0))


def value_of(code):
    return jnp.exp2(code * (1.0 / FINE))


def kernel(
    members,
    peers,
    model_width,
    lengths,
    tokens_hbm,
    gain_one,
    gain_two,
    freq_hbm,
    table_hbm,
    wqkv_hbm,
    keys_hbm,
    values_hbm,
    wout_hbm,
    wgate_hbm,
    wup_hbm,
    wdown_hbm,
    out_ref,
    tokens,
    freq,
    table,
    wqkv,
    keys,
    values,
    wout,
    wgate,
    wup,
    wdown,
    queries,
    codes,
    slot_codes,
    tops_ref,
    scores,
    s1,
    r1,
    s2,
    r2,
    s4,
    r4,
    s5,
    r5,
    s5b,
    r5b,
    g6,
    s6,
    r6,
    s7,
    r7,
    g7,
    s7b,
    r7b,
    code_sem,
    fetch_sem,
    send_sem,
    recv_sem,
    group_sem,
):
    me = lax.axis_index("mem")
    mine = lax.axis_index("mp")
    rows = tokens.shape[0]
    slots = keys.shape[0]
    block_len = keys.shape[1]

    barrier = pltpu.get_barrier_semaphore()
    for k in range(1, members):
        pl.semaphore_signal(
            barrier, inc=1, device_id={"mem": lax.rem(me + k, members)}, device_id_type=MESH
        )
    for k in range(1, peers):
        pl.semaphore_signal(
            barrier, inc=1, device_id={"mp": lax.rem(mine + k, peers)}, device_id_type=MESH
        )

    fetched = {}

    def fetch(name, source, target, pieces=1):
        size = target.shape[0] // pieces
        fetched[name] = []
        for p in range(pieces):
            index = sum(len(v) for v in fetched.values())
            part = pl.ds(p * size, size)
            copy = pltpu.make_async_copy(source.at[part], target.at[part], fetch_sem.at[index])
            copy.start()
            fetched[name].append(copy)

    def ready(*names):
        for name in names:
            for copy in fetched[name]:
                copy.wait()

    fetch("tokens", tokens_hbm, tokens)
    fetch("wqkv", wqkv_hbm, wqkv, PIECES)
    fetch("table", table_hbm, table)
    fetch("freq", freq_hbm, freq)

    def send_members(phase, source_of, target):
        for k in range(1, members):
            other = lax.rem(me + k, members)
            pltpu.make_async_remote_copy(
                src_ref=source_of(other),
                dst_ref=target,
                send_sem=send_sem.at[phase],
                recv_sem=recv_sem.at[phase],
                device_id={"mem": other},
                device_id_type=MESH,
            ).start()

    def send_peers(phase, source, target):
        for k in range(1, peers):
            other = lax.rem(mine + k, peers)
            pltpu.make_async_remote_copy(
                src_ref=source,
                dst_ref=target,
                send_sem=send_sem.at[phase],
                recv_sem=recv_sem.at[phase],
                device_id={"mp": other},
                device_id_type=MESH,
            ).start()

    width = tokens.shape[1]

    def sum_peers(phase, partial, staged, landed):
        unit_code = jnp.ceil(code_of(jnp.max(jnp.abs(partial), axis=1, keepdims=True)))
        steps = jnp.floor(partial * (STEPS / value_of(unit_code)) + 0.5)
        staged[:, :width] = steps.astype(jnp.int32).astype(jnp.int16)
        staged[:, width:] = (
            jnp.broadcast_to(unit_code, (rows, LANES)).astype(jnp.int32).astype(jnp.int16)
        )
        send_peers(phase, staged, landed.at[mine])
        landed[mine] = staged[...]
        wait_bytes(landed.at[pl.ds(0, peers - 1)], recv_sem.at[phase])
        total = jnp.zeros((rows, width), F32)
        for j in range(peers):
            part = landed[j].astype(jnp.int32).astype(F32)
            unit = value_of(part[:, width:]) * (1.0 / STEPS)
            total = total + part[:, :width] * jnp.concatenate([unit] * (width // LANES), axis=1)
        return total

    def wait_bytes(window, semaphore):
        pltpu.make_async_copy(window, window, semaphore).wait()

    ready("tokens")
    token_f = tokens[...].astype(F32)
    scaled_in = (token_f * gain_one[...].astype(F32)[None, :]).astype(BF16)
    square_one = jnp.sum(token_f * token_f, axis=1, keepdims=True)
    ready("wqkv")
    projected = jnp.dot(scaled_in, wqkv[...], preferred_element_type=F32)
    for c in range(HEADS + 2):
        s1[pl.ds(c, rows, stride=rows), :] = projected[:, c * LANES : (c + 1) * LANES]
    s1[pl.ds(HEADS + 2, rows, stride=rows), :] = jnp.broadcast_to(square_one, (rows, LANES))

    pl.semaphore_wait(barrier, members - 1 + peers - 1)

    used = HEADS + 3
    send_members(
        0, lambda other: s1.at[pl.ds(other * rows, used)], r1.at[me, pl.ds(0, used)]
    )
    r1[me] = s1[pl.ds(pl.multiple_of(me * rows, rows), rows), :]

    fetch("keys", keys_hbm.at[:, 0], keys, PIECES)
    fetch("values", values_hbm.at[:, 0], values, PIECES)

    request, place = me // NEW, lax.rem(me, NEW)
    ready("freq")
    position = (lengths[request] + place).astype(F32)
    sine, cosine = sine_cosine(position * freq[...])
    lane_row = lax.broadcasted_iota(jnp.int32, (1, LANES), 1)
    sine = jnp.where(lane_row < LANES // 2, -sine, sine)

    wait_bytes(r1.at[pl.ds(0, members - 1), pl.ds(0, used)], recv_sem.at[0])
    total = r1[0]
    for j in range(1, members):
        total = total + r1[j]
    inverse_one = 1.0 / jnp.sqrt(total[HEADS + 2 : HEADS + 3, :] / model_width + EPSILON)
    total = total * inverse_one
    turned = total * cosine + pltpu.roll(total, LANES // 2, 1) * sine
    head_row = lax.broadcasted_iota(jnp.int32, total.shape, 0)
    s2[...] = jnp.where(head_row <= HEADS, turned, total).astype(BF16)
    r2[me] = s2[...]
    send_members(1, lambda other: s2, r2.at[me])
    fetch("wout", wout_hbm, wout, 2)
    fetch("wgate", wgate_hbm, wgate, PIECES)
    fetch("wup", wup_hbm, wup, PIECES)
    fetch("wdown", wdown_hbm, wdown, PIECES)

    ready("table")
    first_slot = me * slots
    max_blocks = table.shape[1]
    block_start = lax.broadcasted_iota(jnp.int32, (1, max_blocks), 1) * block_len
    slot_ids = first_slot + lax.broadcasted_iota(jnp.int32, (slots, max_blocks), 0)
    code = jnp.zeros((slots, max_blocks), jnp.int32)
    for r in range(REQUESTS):
        held = jnp.clip(lengths[r] - block_start, 0, block_len)
        held = jnp.where(held > 0, held + r * OWNER, 0)
        code = code + jnp.where(table[r : r + 1, :] == slot_ids, held, 0)
    code = jnp.sum(code, axis=1, keepdims=True)
    diagonal = lax.broadcasted_iota(jnp.int32, (slots, slots), 0) == lax.broadcasted_iota(
        jnp.int32, (slots, slots), 1
    )
    code = jnp.sum(jnp.where(diagonal, code, 0), axis=0, keepdims=True)
    owner_row = code // OWNER
    codes[0:1, :] = code
    to_scalars = pltpu.make_async_copy(codes, slot_codes, code_sem)
    to_scalars.start()

    wait_bytes(r2.at[pl.ds(0, members - 1)], recv_sem.at[1])

    for r in range(REQUESTS):
        queries[r] = jnp.concatenate(
            [r2[r * NEW + t].astype(F32)[:HEADS] for t in range(NEW)], axis=0
        ).astype(BF16)
    factor = math.log2(math.e) / math.sqrt(LANES)
    lane_group = lax.broadcasted_iota(jnp.int32, (GROUP, LANES), 1)
    to_scalars.wait()
    ready("keys")

    def slot_of(slot):
        value = slot_codes[0, slot]
        return value // OWNER, lax.rem(value, OWNER)

    def score_step(step, best):
        for j in range(TILE):
            slot = step * TILE + j
            owner, count = slot_of(slot)
            score = lax.dot_general(
                queries[owner],
                keys[slot],
                (((1,), (1,)), ((), ())),
                preferred_element_type=F32,
            )
            score = jnp.where(lane_group < count, score, FLOOR_SCORE)
            scores[slot] = score
            best = jnp.where(lane_group == slot, jnp.max(score, axis=1, keepdims=True), best)
        return best

    floor = jnp.full((GROUP, LANES), FLOOR_SCORE, F32)
    slot_best = lax.fori_loop(0, slots // TILE, score_step, floor)
    best = []
    for r in range(REQUESTS):
        own = jnp.where(owner_row == r, slot_best, FLOOR_SCORE)
        best.append(jnp.broadcast_to(jnp.max(own, axis=1, keepdims=True), (GROUP, LANES)))
        tops_ref[r] = best[r]
    ready("values")

    def value_step(step, carry):
        sums, mixed = carry
        high_line, low_line = [], []
        for j in range(VALUE_TILE):
            slot = step * VALUE_TILE + j
            owner, _ = slot_of(slot)
            weight = jnp.exp2((scores[slot] - tops_ref[owner]) * factor)
            sums = jnp.where(lane_group == slot, jnp.sum(weight, axis=1, keepdims=True), sums)
            high = weight.astype(BF16)
            low = (weight - high.astype(F32)).astype(BF16)
            for line, part in ((high_line, high), (low_line, low)):
                line.append(
                    jnp.concatenate(
                        [jnp.where(owner == r, part, jnp.zeros_like(part)) for r in range(REQUESTS)],
                        axis=0,
                    )
                )
        block = values[pl.ds(step * VALUE_TILE, VALUE_TILE)].reshape(VALUE_TILE * block_len, LANES)
        both = jnp.concatenate(
            [jnp.concatenate(high_line, axis=1), jnp.concatenate(low_line, axis=1)], axis=0
        )
        both = jnp.dot(both, block, preferred_element_type=F32)
        return sums, mixed + (both[: REQUESTS * GROUP] + both[REQUESTS * GROUP :])

    slot_sums, mixed = lax.fori_loop(
        0,
        slots // VALUE_TILE,
        value_step,
        (jnp.zeros((GROUP, LANES), F32), jnp.zeros((REQUESTS * GROUP, LANES), F32)),
    )
    lane_tile = lax.broadcasted_iota(jnp.int32, (HEADS, LANES), 1)
    for r in range(REQUESTS):
        own = jnp.where(owner_row == r, slot_sums, 0.0)
        whole = jnp.broadcast_to(jnp.sum(own, axis=1, keepdims=True), (GROUP, LANES))
        for t in range(NEW):
            part = slice(t * HEADS, (t + 1) * HEADS)
            i = r * NEW + t
            s4[i, :HEADS, :] = mixed[i * HEADS : (i + 1) * HEADS]
            s4[i, HEADS:, :] = jnp.where(lane_tile < LANES // 2, best[r][part], whole[part])
    send_members(2, lambda other: s4.at[other], r4.at[me])
    r4[me] = s4[me]

    row_queries = r2[me].astype(F32)[:HEADS]
    own_scores, own_values = [], []
    for t in range(NEW):
        fresh = r2[request * NEW + t].astype(F32)
        score = jnp.sum(row_queries * fresh[HEADS : HEADS + 1], axis=1, keepdims=True)
        score = jnp.broadcast_to(score, (HEADS, LANES))
        own_scores.append(jnp.where(t <= place, score, FLOOR_SCORE))
        own_values.append(fresh[HEADS + 1 : HEADS + 2])
    top = functools.reduce(jnp.maximum, own_scores)

    wait_bytes(r4.at[pl.ds(0, members - 1)], recv_sem.at[2])
    tops, wholes = [], []
    for j in range(members):
        both = r4[j, HEADS:, :]
        swapped = pltpu.roll(both, LANES // 2, 1)
        tops.append(jnp.where(lane_tile < LANES // 2, both, swapped))
        wholes.append(jnp.where(lane_tile < LANES // 2, swapped, both))
    top = functools.reduce(jnp.maximum, tops, top)
    mix, whole = jnp.zeros((HEADS, LANES), F32), jnp.zeros((HEADS, LANES), F32)
    for t in range(NEW):
        weight = jnp.exp2((own_scores[t] - top) * factor)
        whole = whole + weight
        mix = mix + weight * own_values[t]
    for j in range(members):
        shrink = jnp.exp2((tops[j] - top) * factor)
        whole = whole + wholes[j] * shrink
        mix = mix + r4[j, :HEADS, :] * shrink
    s5[...] = mix / whole
    own_rows = pl.ds(pl.multiple_of(me * HEADS, HEADS), HEADS)
    r5[own_rows, :] = s5[...]
    send_members(3, lambda other: s5, r5.at[own_rows])
    ready("wout")
    wait_bytes(r5.at[pl.ds(0, (members - 1) * HEADS)], recv_sem.at[3])

    attended = jnp.concatenate(
        [r5[pl.ds(h, rows, stride=HEADS), :].astype(BF16) for h in range(HEADS)], axis=1
    )
    partial = jnp.dot(attended, wout[...], preferred_element_type=F32)
    after_f = (token_f + sum_peers(4, partial, s5b, r5b)).astype(BF16).astype(F32)
    ready("wgate", "wup")

    scaled_mid = (after_f * gain_two[...].astype(F32)[None, :]).astype(BF16)
    square_mid = jnp.sum(after_f * after_f, axis=1, keepdims=True)
    square_code = code_of(square_mid)
    square_whole = jnp.floor(square_code)
    square_rest = jnp.floor((square_code - square_whole) * STEPS + 0.5)
    lane_rows = lax.broadcasted_iota(jnp.int32, (rows, LANES), 1)
    square_line = jnp.where(lane_rows < LANES // 2, square_whole, square_rest)

    quarter, group = me // GROUPS, lax.rem(me, GROUPS)
    span = wgate.shape[1] // GROUPS
    chunks = span // LANES
    tall = rows * LINES
    short = tall // GROUPS
    for k in (2, 1, 3, 0):
        target = lax.rem(group + k, GROUPS)
        columns = pl.ds(pl.multiple_of(target * span, LANES), span)
        parts = [
            jnp.dot(scaled_mid, weight[:, columns], preferred_element_type=F32)
            for weight in (wgate, wup)
        ]
        largest = jnp.maximum(jnp.abs(parts[0]), jnp.abs(parts[1]))
        unit_code = jnp.ceil(code_of(jnp.max(largest, axis=1, keepdims=True)))
        to_steps = STEPS / value_of(unit_code)
        unit_line = jnp.broadcast_to(unit_code, (rows, LANES))
        for index, (part, extra) in enumerate(zip(parts, (unit_line, square_line))):
            base = (2 * k + index) * tall
            steps = jnp.floor(part * to_steps + 0.5)
            for c in range(chunks):
                g6[pl.ds(base + c, rows, stride=LINES), :] = steps[:, c * LANES : (c + 1) * LANES]
            g6[pl.ds(base + chunks, rows, stride=LINES), :] = extra
            for q in range(GROUPS):
                piece = g6[base + q * short : base + (q + 1) * short, :]
                s6[k, q, index * short : (index + 1) * short, :] = piece.astype(jnp.int32).astype(
                    jnp.int16
                )
        for j in range(1 if k == 0 else 0, GROUPS):
            other = lax.rem(quarter + j, GROUPS)
            pltpu.make_async_remote_copy(
                src_ref=s6.at[k, other],
                dst_ref=r6.at[me],
                send_sem=send_sem.at[5],
                recv_sem=recv_sem.at[5],
                device_id={"mem": other * GROUPS + target},
                device_id_type=MESH,
            ).start()
    r6[me] = s6[0, quarter]

    wait_bytes(r6.at[pl.ds(0, members - 1)], recv_sem.at[5])
    gates = [jnp.zeros((LINES, LANES), F32)] * GROUPS
    ups = [jnp.zeros((LINES, LANES), F32)] * GROUPS
    square = jnp.zeros((GROUPS, LANES), F32)
    lane_codes = lax.broadcasted_iota(jnp.int32, (GROUPS, LANES), 1)
    for j in range(members):
        part = r6[j].astype(jnp.int32).astype(F32)
        units, squares = (
            jnp.concatenate(
                [
                    part[start + r * LINES + chunks : start + r * LINES + chunks + 1]
                    for r in range(GROUPS)
                ],
                axis=0,
            )
            for start in (0, short)
        )
        units = value_of(units) * (1.0 / STEPS)
        squares = jnp.where(lane_codes < LANES // 2, squares, squares * (1.0 / STEPS))
        square = square + value_of(squares + pltpu.roll(squares, LANES // 2, 1))
        for r in range(GROUPS):
            own = slice(r * LINES, (r + 1) * LINES)
            gates[r] = gates[r] + part[:short][own] * units[r : r + 1]
            ups[r] = ups[r] + part[short:][own] * units[r : r + 1]
    inverse_two = 1.0 / jnp.sqrt(square / model_width + EPSILON)
    hidden = []
    for r in range(GROUPS):
        gate = gates[r] * inverse_two[r : r + 1]
        hidden.append(gate / (1.0 + jnp.exp(-gate)) * (ups[r] * inverse_two[r : r + 1]))
    s7[...] = jnp.concatenate(hidden, axis=0).astype(BF16)
    r7[me] = s7[...]
    for k in range(1, members):
        other = lax.rem(me + k, members)
        pltpu.make_async_remote_copy(
            src_ref=s7,
            dst_ref=r7.at[me],
            send_sem=send_sem.at[6],
            recv_sem=group_sem.at[group],
            device_id={"mem": other},
            device_id_type=MESH,
        ).start()
    ready("wdown")

    down = jnp.zeros((rows, wdown.shape[1]), F32)
    for k in (0, 1, 3, 2):
        source = lax.rem(group + k, GROUPS)
        arriving = GROUPS - 1 if k == 0 else GROUPS
        wait_bytes(r7.at[pl.ds(0, arriving)], group_sem.at[source])
        for q in range(GROUPS):
            line = k * tall + q * short
            g7[line : line + short, :] = r7[q * GROUPS + source].astype(F32)
        piece = jnp.concatenate(
            [
                g7[pl.ds(k * tall + c, rows, stride=LINES), :].astype(BF16)
                for c in range(chunks)
            ],
            axis=1,
        )
        down = down + jnp.dot(
            piece,
            wdown[pl.ds(pl.multiple_of(source * span, LANES), span), :],
            preferred_element_type=F32,
        )
    out_ref[...] = (after_f + sum_peers(7, down, s7b, r7b)).astype(BF16)

    wait_bytes(r1.at[pl.ds(0, members - 1), pl.ds(0, used)], send_sem.at[0])
    wait_bytes(r2.at[pl.ds(0, members - 1)], send_sem.at[1])
    wait_bytes(r4.at[pl.ds(0, members - 1)], send_sem.at[2])
    wait_bytes(r5.at[pl.ds(0, (members - 1) * HEADS)], send_sem.at[3])
    for phase, landed in ((4, r5b), (7, r7b)):
        wait_bytes(landed.at[pl.ds(0, peers - 1)], send_sem.at[phase])
    for phase, landed in ((5, r6), (6, r7)):
        wait_bytes(landed.at[pl.ds(0, members - 1)], send_sem.at[phase])


def local(
    members,
    peers,
    tokens,
    attn_gain,
    query_key_value_weight,
    paged_key_store,
    paged_value_store,
    lengths,
    block_table,
    out_weight,
    mlp_gain,
    gate_weight,
    up_weight,
    down_weight,
):
    rows, width_part = tokens.shape
    slots, _, block_len, head_dim = paged_key_store.shape
    short = rows * LINES // GROUPS
    exponents = np.arange(head_dim // 2, dtype=np.float32) * np.float32(
        -2.0 * math.log(ROPE_BASE) / head_dim
    )
    inverse = np.exp(exponents.astype(np.float64)).astype(np.float32)
    freq = jnp.asarray(np.concatenate([inverse, inverse])[None, :])

    any_spec = pl.BlockSpec(memory_space=pl.ANY)
    vmem_spec = pl.BlockSpec(memory_space=pltpu.VMEM)
    scratch = [
        pltpu.VMEM(tokens.shape, BF16),
        pltpu.VMEM(freq.shape, F32),
        pltpu.VMEM(block_table.shape, jnp.int32),
        pltpu.VMEM(query_key_value_weight.shape, BF16),
        pltpu.VMEM((slots, block_len, head_dim), BF16),
        pltpu.VMEM((slots, block_len, head_dim), BF16),
        pltpu.VMEM(out_weight.shape, BF16),
        pltpu.VMEM(gate_weight.shape, BF16),
        pltpu.VMEM(up_weight.shape, BF16),
        pltpu.VMEM(down_weight.shape, BF16),
        pltpu.VMEM((REQUESTS, GROUP, head_dim), BF16),
        pltpu.VMEM((8, slots), jnp.int32),
        pltpu.SMEM((8, slots), jnp.int32),
        pltpu.VMEM((REQUESTS, GROUP, LANES), F32),
        pltpu.VMEM((slots, GROUP, LANES), F32),
        pltpu.VMEM((rows * rows, LANES), F32),
        pltpu.VMEM((members, rows, LANES), F32),
        pltpu.VMEM((16, LANES), BF16),
        pltpu.VMEM((members, 16, LANES), BF16),
        pltpu.VMEM((members, 2 * HEADS, LANES), F32),
        pltpu.VMEM((members, 2 * HEADS, LANES), F32),
        pltpu.VMEM((HEADS, LANES), F32),
        pltpu.VMEM((members * HEADS, LANES), F32),
        pltpu.VMEM((rows, width_part + LANES), jnp.int16),
        pltpu.VMEM((peers, rows, width_part + LANES), jnp.int16),
        pltpu.VMEM((2 * GROUPS * rows * LINES, LANES), F32),
        pltpu.VMEM((GROUPS, GROUPS, 2 * short, LANES), jnp.int16),
        pltpu.VMEM((members, 2 * short, LANES), jnp.int16),
        pltpu.VMEM((short, LANES), BF16),
        pltpu.VMEM((members, short, LANES), BF16),
        pltpu.VMEM((GROUPS * rows * LINES, LANES), F32),
        pltpu.VMEM((rows, width_part + LANES), jnp.int16),
        pltpu.VMEM((peers, rows, width_part + LANES), jnp.int16),
        pltpu.SemaphoreType.DMA,
        pltpu.SemaphoreType.DMA((3 + 6 * PIECES + 2,)),
        pltpu.SemaphoreType.DMA((8,)),
        pltpu.SemaphoreType.DMA((8,)),
        pltpu.SemaphoreType.DMA((GROUPS,)),
    ]
    return pl.pallas_call(
        functools.partial(kernel, members, peers, width_part * members),
        out_shape=jax.ShapeDtypeStruct(tokens.shape, BF16),
        in_specs=[
            pl.BlockSpec(memory_space=pltpu.SMEM),
            any_spec,
            vmem_spec,
            vmem_spec,
        ]
        + [any_spec] * 9,
        out_specs=vmem_spec,
        scratch_shapes=scratch,
        compiler_params=pltpu.CompilerParams(
            collective_id=0, has_side_effects=True, vmem_limit_bytes=56 * 1024 * 1024
        ),
        name="decoder_layer",
    )(
        lengths,
        tokens,
        attn_gain,
        mlp_gain,
        freq,
        block_table,
        query_key_value_weight,
        paged_key_store,
        paged_value_store,
        out_weight,
        gate_weight,
        up_weight,
        down_weight,
    )


def solution(mesh):
    return jax.shard_map(
        functools.partial(local, mesh.shape["mem"], mesh.shape["mp"]),
        mesh=mesh,
        in_specs=(
            P(None, "mem"),
            P("mem"),
            P("mem", "mp"),
            P("mem", "mp", None, None),
            P("mem", "mp", None, None),
            P(),
            P(),
            P("mp", "mem"),
            P("mem"),
            P("mem", "mp"),
            P("mem", "mp"),
            P("mp", "mem"),
        ),
        out_specs=P(None, "mem"),
        check_vma=False,
    )
```

```python
import functools
import math

import jax
import jax.numpy as jnp
import numpy as np
from jax import lax
from jax.experimental import pallas as pl
from jax.experimental.pallas import tpu as pltpu
from jax.sharding import PartitionSpec as P

MESH = pl.DeviceIdType.MESH
F32 = jnp.float32
BF16 = jnp.bfloat16

EPSILON = 1e-05
ROPE_BASE = 500000.0
FLOOR_SCORE = -1e30
LANES = 128
HEADS = 8
NEW = 4
REQUESTS = 4
GROUP = NEW * HEADS
OWNER = 256
TILE = 16
GROUPS = 4
LINES = 8
PIECES = 4

HALF_PI = (1.5703125, 0.000484466552734375, -6.397578377557687e-07)


def sine_cosine(angle):
    turns = jnp.floor(angle * (2.0 / math.pi) + 0.5)
    r = ((angle - turns * HALF_PI[0]) - turns * HALF_PI[1]) - turns * HALF_PI[2]
    z = r * r
    sine = r + r * z * (-1.6666654611e-1 + z * (8.3321608736e-3 + z * (-1.9515295891e-4)))
    cosine = 1.0 - 0.5 * z + z * z * (
        4.166664568298827e-2 + z * (-1.388731625493765e-3 + z * 2.443315711809948e-5)
    )
    quadrant = turns - 4.0 * jnp.floor(turns * 0.25)
    odd = (quadrant == 1.0) | (quadrant == 3.0)
    s, c = jnp.where(odd, cosine, sine), jnp.where(odd, sine, cosine)
    s = jnp.where(quadrant >= 2.0, -s, s)
    c = jnp.where((quadrant == 1.0) | (quadrant == 2.0), -c, c)
    return s, c


STEPS = 32000.0
FINE = 256.0


def code_of(value):
    return jnp.log(jnp.maximum(value, 1e-30)) * (FINE / math.log(2.0))


def value_of(code):
    return jnp.exp2(code * (1.0 / FINE))


def kernel(
    members,
    peers,
    model_width,
    lengths_hbm,
    tokens_hbm,
    gain_one_hbm,
    gain_two_hbm,
    freq_hbm,
    table_hbm,
    wqkv_hbm,
    keys_hbm,
    values_hbm,
    wout_hbm,
    wgate_hbm,
    wup_hbm,
    wdown_hbm,
    out_ref,
    lengths,
    tokens,
    gain_one,
    gain_two,
    freq,
    table,
    wqkv,
    keys,
    values,
    wout,
    wgate,
    wup,
    wdown,
    queries,
    codes,
    slot_codes,
    tops_ref,
    scores,
    s1,
    r1,
    s2,
    r2,
    s4,
    r4,
    s5,
    r5,
    s5b,
    r5b,
    g6,
    s6,
    r6,
    s7,
    r7,
    g7,
    s7b,
    r7b,
    code_sem,
    fetch_sem,
    send_sem,
    recv_sem,
    group_sem,
):
    me = lax.axis_index("mem")
    mine = lax.axis_index("mp")
    rows = tokens.shape[0]
    slots = keys.shape[0]
    block_len = keys.shape[1]

    side = math.isqrt(members)
    z, x = me // side, lax.rem(me, side)
    steps_of = lambda d, n: min(d, n - d)
    offsets = sorted(
        ((dz, dx) for dz in range(side) for dx in range(side) if dz or dx),
        key=lambda d: -steps_of(d[0], side) - steps_of(d[1], side),
    )
    member_order = [lax.rem(z + dz, side) * side + lax.rem(x + dx, side) for dz, dx in offsets]
    ring, cores = peers // 2, 2
    y, core = mine // cores, lax.rem(mine, cores)
    offsets = sorted(
        ((dy, dc) for dy in range(ring) for dc in range(cores) if dy or dc),
        key=lambda d: -steps_of(d[0], ring),
    )
    peer_order = [lax.rem(y + dy, ring) * cores + lax.rem(core + dc, cores) for dy, dc in offsets]

    fetched = {}

    def fetch(name, source, target, pieces=1):
        size = target.shape[0] // pieces
        fetched[name] = []
        for p in range(pieces):
            index = sum(len(v) for v in fetched.values())
            if pieces > 1:
                part = pl.ds(p * size, size)
                copy = pltpu.make_async_copy(source.at[part], target.at[part], fetch_sem.at[index])
            else:
                copy = pltpu.make_async_copy(source, target, fetch_sem.at[index])
            copy.start()
            fetched[name].append(copy)

    def ready(*names):
        for name in names:
            for copy in fetched[name]:
                copy.wait()

    fetch("tokens", tokens_hbm, tokens)
    fetch("gain_one", gain_one_hbm, gain_one)
    fetch("wqkv", wqkv_hbm, wqkv, PIECES)

    barrier = pltpu.get_barrier_semaphore()
    for other in member_order:
        pl.semaphore_signal(barrier, inc=1, device_id={"mem": other}, device_id_type=MESH)
    for other in peer_order:
        pl.semaphore_signal(barrier, inc=1, device_id={"mp": other}, device_id_type=MESH)

    fetch("lengths", lengths_hbm, lengths)
    fetch("freq", freq_hbm, freq)
    fetch("table", table_hbm, table)
    fetch("gain_two", gain_two_hbm, gain_two)

    def send_members(phase, source_of, target):
        for other in member_order:
            pltpu.make_async_remote_copy(
                src_ref=source_of(other),
                dst_ref=target,
                send_sem=send_sem.at[phase],
                recv_sem=recv_sem.at[phase],
                device_id={"mem": other},
                device_id_type=MESH,
            ).start()

    def send_peers(phase, source, target):
        for other in peer_order:
            pltpu.make_async_remote_copy(
                src_ref=source,
                dst_ref=target,
                send_sem=send_sem.at[phase],
                recv_sem=recv_sem.at[phase],
                device_id={"mp": other},
                device_id_type=MESH,
            ).start()

    width = tokens.shape[1]

    def sum_peers(phase, partial, staged, landed):
        unit_code = jnp.ceil(code_of(jnp.max(jnp.abs(partial), axis=1, keepdims=True)))
        steps = jnp.floor(partial * (STEPS / value_of(unit_code)) + 0.5)
        staged[:, :width] = steps.astype(jnp.int32).astype(jnp.int16)
        staged[:, width:] = (
            jnp.broadcast_to(unit_code, (rows, LANES)).astype(jnp.int32).astype(jnp.int16)
        )
        send_peers(phase, staged, landed.at[mine])
        landed[mine] = staged[...]
        wait_bytes(landed.at[pl.ds(0, peers - 1)], recv_sem.at[phase])
        total = jnp.zeros((rows, width), F32)
        for j in range(peers):
            part = landed[j].astype(jnp.int32).astype(F32)
            unit = value_of(part[:, width:]) * (1.0 / STEPS)
            total = total + part[:, :width] * jnp.concatenate([unit] * (width // LANES), axis=1)
        return total

    def wait_bytes(window, semaphore):
        pltpu.make_async_copy(window, window, semaphore).wait()

    ready("tokens", "gain_one")
    token_f = tokens[...].astype(F32)
    scaled_in = (token_f * gain_one[...].astype(F32)[None, :]).astype(BF16)
    square_one = jnp.sum(token_f * token_f, axis=1, keepdims=True)
    ready("wqkv")
    projected = jnp.dot(scaled_in, wqkv[...], preferred_element_type=F32)
    for c in range(HEADS + 2):
        s1[pl.ds(c, rows, stride=rows), :] = projected[:, c * LANES : (c + 1) * LANES]
    s1[pl.ds(HEADS + 2, rows, stride=rows), :] = jnp.broadcast_to(square_one, (rows, LANES))

    pl.semaphore_wait(barrier, members - 1 + peers - 1)

    used = HEADS + 3
    send_members(
        0, lambda other: s1.at[pl.ds(other * rows, used)], r1.at[me, pl.ds(0, used)]
    )
    r1[me] = s1[pl.ds(pl.multiple_of(me * rows, rows), rows), :]

    fetch("keys", keys_hbm.at[:, 0], keys, PIECES)
    fetch("values", values_hbm.at[:, 0], values, PIECES)

    request, place = me // NEW, lax.rem(me, NEW)
    ready("lengths", "freq")
    position = (lengths[request] + place).astype(F32)
    sine, cosine = sine_cosine(position * freq[...])
    lane_row = lax.broadcasted_iota(jnp.int32, (1, LANES), 1)
    sine = jnp.where(lane_row < LANES // 2, -sine, sine)

    wait_bytes(r1.at[pl.ds(0, members - 1), pl.ds(0, used)], recv_sem.at[0])
    total = r1[0]
    for j in range(1, members):
        total = total + r1[j]
    inverse_one = 1.0 / jnp.sqrt(total[HEADS + 2 : HEADS + 3, :] / model_width + EPSILON)
    total = total * inverse_one
    turned = total * cosine + pltpu.roll(total, LANES // 2, 1) * sine
    head_row = lax.broadcasted_iota(jnp.int32, total.shape, 0)
    s2[...] = jnp.where(head_row <= HEADS, turned, total).astype(BF16)
    r2[me] = s2[...]
    send_members(1, lambda other: s2, r2.at[me])
    fetch("wout", wout_hbm, wout, 2)
    fetch("wgate", wgate_hbm, wgate, PIECES)
    fetch("wup", wup_hbm, wup, PIECES)
    fetch("wdown", wdown_hbm, wdown, PIECES)

    ready("table")
    first_slot = me * slots
    max_blocks = table.shape[1]
    block_start = lax.broadcasted_iota(jnp.int32, (1, max_blocks), 1) * block_len
    slot_ids = first_slot + lax.broadcasted_iota(jnp.int32, (slots, max_blocks), 0)
    code = jnp.zeros((slots, max_blocks), jnp.int32)
    for r in range(REQUESTS):
        held = jnp.clip(lengths[r] - block_start, 0, block_len)
        held = jnp.where(held > 0, held + r * OWNER, 0)
        code = code + jnp.where(table[r : r + 1, :] == slot_ids, held, 0)
    code = jnp.sum(code, axis=1, keepdims=True)
    diagonal = lax.broadcasted_iota(jnp.int32, (slots, slots), 0) == lax.broadcasted_iota(
        jnp.int32, (slots, slots), 1
    )
    code = jnp.sum(jnp.where(diagonal, code, 0), axis=0, keepdims=True)
    owner_row = code // OWNER
    codes[0:1, :] = code
    to_scalars = pltpu.make_async_copy(codes, slot_codes, code_sem)
    to_scalars.start()

    wait_bytes(r2.at[pl.ds(0, members - 1)], recv_sem.at[1])

    for r in range(REQUESTS):
        queries[r] = jnp.concatenate(
            [r2[r * NEW + t].astype(F32)[:HEADS] for t in range(NEW)], axis=0
        ).astype(BF16)
    factor = math.log2(math.e) / math.sqrt(LANES)
    lane_group = lax.broadcasted_iota(jnp.int32, (GROUP, LANES), 1)
    to_scalars.wait()
    ready("keys")

    def slot_of(slot):
        value = slot_codes[0, slot]
        return value // OWNER, lax.rem(value, OWNER)

    def score_step(step, best):
        for j in range(TILE):
            slot = step * TILE + j
            owner, count = slot_of(slot)
            score = lax.dot_general(
                queries[owner],
                keys[slot],
                (((1,), (1,)), ((), ())),
                preferred_element_type=F32,
            )
            score = jnp.where(lane_group < count, score, FLOOR_SCORE)
            scores[slot] = score
            best = jnp.where(lane_group == slot, jnp.max(score, axis=1, keepdims=True), best)
        return best

    floor = jnp.full((GROUP, LANES), FLOOR_SCORE, F32)
    slot_best = lax.fori_loop(0, slots // TILE, score_step, floor)
    best = []
    for r in range(REQUESTS):
        own = jnp.where(owner_row == r, slot_best, FLOOR_SCORE)
        best.append(jnp.broadcast_to(jnp.max(own, axis=1, keepdims=True), (GROUP, LANES)))
        tops_ref[r] = best[r]
    ready("values")

    def value_step(step, carry):
        sums, mixed = carry[0], list(carry[1])
        for j in range(TILE):
            slot = step * TILE + j
            owner, _ = slot_of(slot)
            weight = jnp.exp2((scores[slot] - tops_ref[owner]) * factor)
            sums = jnp.where(lane_group == slot, jnp.sum(weight, axis=1, keepdims=True), sums)
            high = weight.astype(BF16)
            low = (weight - high.astype(F32)).astype(BF16)
            both = jnp.dot(
                jnp.concatenate([high, low], axis=0), values[slot], preferred_element_type=F32
            )
            both = both[:GROUP] + both[GROUP:]
            for r in range(REQUESTS):
                mixed[r] = mixed[r] + jnp.where(owner == r, both, 0.0)
        return sums, tuple(mixed)

    zero = jnp.zeros((GROUP, LANES), F32)
    slot_sums, mixed = lax.fori_loop(0, slots // TILE, value_step, (zero, (zero,) * REQUESTS))
    lane_tile = lax.broadcasted_iota(jnp.int32, (HEADS, LANES), 1)
    for r in range(REQUESTS):
        own = jnp.where(owner_row == r, slot_sums, 0.0)
        whole = jnp.broadcast_to(jnp.sum(own, axis=1, keepdims=True), (GROUP, LANES))
        for t in range(NEW):
            part = slice(t * HEADS, (t + 1) * HEADS)
            i = r * NEW + t
            s4[i, :HEADS, :] = mixed[r][part]
            s4[i, HEADS:, :] = jnp.where(lane_tile < LANES // 2, best[r][part], whole[part])
    send_members(2, lambda other: s4.at[other], r4.at[me])
    r4[me] = s4[me]

    row_queries = r2[me].astype(F32)[:HEADS]
    own_scores, own_values = [], []
    for t in range(NEW):
        fresh = r2[request * NEW + t].astype(F32)
        score = jnp.sum(row_queries * fresh[HEADS : HEADS + 1], axis=1, keepdims=True)
        score = jnp.broadcast_to(score, (HEADS, LANES))
        own_scores.append(jnp.where(t <= place, score, FLOOR_SCORE))
        own_values.append(fresh[HEADS + 1 : HEADS + 2])
    top = functools.reduce(jnp.maximum, own_scores)

    wait_bytes(r4.at[pl.ds(0, members - 1)], recv_sem.at[2])
    tops, wholes = [], []
    for j in range(members):
        both = r4[j, HEADS:, :]
        swapped = pltpu.roll(both, LANES // 2, 1)
        tops.append(jnp.where(lane_tile < LANES // 2, both, swapped))
        wholes.append(jnp.where(lane_tile < LANES // 2, swapped, both))
    top = functools.reduce(jnp.maximum, tops, top)
    mix, whole = jnp.zeros((HEADS, LANES), F32), jnp.zeros((HEADS, LANES), F32)
    for t in range(NEW):
        weight = jnp.exp2((own_scores[t] - top) * factor)
        whole = whole + weight
        mix = mix + weight * own_values[t]
    for j in range(members):
        shrink = jnp.exp2((tops[j] - top) * factor)
        whole = whole + wholes[j] * shrink
        mix = mix + r4[j, :HEADS, :] * shrink
    s5[...] = mix / whole
    own_rows = pl.ds(pl.multiple_of(me * HEADS, HEADS), HEADS)
    r5[own_rows, :] = s5[...]
    send_members(3, lambda other: s5, r5.at[own_rows])
    ready("wout")
    wait_bytes(r5.at[pl.ds(0, (members - 1) * HEADS)], recv_sem.at[3])

    attended = jnp.concatenate(
        [r5[pl.ds(h, rows, stride=HEADS), :].astype(BF16) for h in range(HEADS)], axis=1
    )
    partial = jnp.dot(attended, wout[...], preferred_element_type=F32)
    after_f = (token_f + sum_peers(4, partial, s5b, r5b)).astype(BF16).astype(F32)
    ready("gain_two", "wgate", "wup")

    scaled_mid = (after_f * gain_two[...].astype(F32)[None, :]).astype(BF16)
    square_mid = jnp.sum(after_f * after_f, axis=1, keepdims=True)
    square_code = code_of(square_mid)
    square_whole = jnp.floor(square_code)
    square_rest = jnp.floor((square_code - square_whole) * STEPS + 0.5)
    lane_rows = lax.broadcasted_iota(jnp.int32, (rows, LANES), 1)
    square_line = jnp.where(lane_rows < LANES // 2, square_whole, square_rest)

    quarter, group = me // GROUPS, lax.rem(me, GROUPS)
    span = wgate.shape[1] // GROUPS
    chunks = span // LANES
    tall = rows * LINES
    short = tall // GROUPS

    def multiply(k):
        columns = pl.ds(pl.multiple_of(lax.rem(group + k, GROUPS) * span, LANES), span)
        return [
            jnp.dot(scaled_mid, weight[:, columns], preferred_element_type=F32)
            for weight in (wgate, wup)
        ]

    def ship(k, parts):
        target = lax.rem(group + k, GROUPS)
        largest = jnp.maximum(jnp.abs(parts[0]), jnp.abs(parts[1]))
        unit_code = jnp.ceil(code_of(jnp.max(largest, axis=1, keepdims=True)))
        to_steps = STEPS / value_of(unit_code)
        unit_line = jnp.broadcast_to(unit_code, (rows, LANES))
        for index, (part, extra) in enumerate(zip(parts, (unit_line, square_line))):
            base = (2 * k + index) * tall
            steps = jnp.floor(part * to_steps + 0.5)
            for c in range(chunks):
                g6[pl.ds(base + c, rows, stride=LINES), :] = steps[:, c * LANES : (c + 1) * LANES]
            g6[pl.ds(base + chunks, rows, stride=LINES), :] = extra
            for q in range(GROUPS):
                piece = g6[base + q * short : base + (q + 1) * short, :]
                s6[k, q, index * short : (index + 1) * short, :] = piece.astype(jnp.int32).astype(
                    jnp.int16
                )
        for j in (2, 1, 3, 0) if k else (2, 1, 3):
            other = lax.rem(quarter + j, GROUPS)
            pltpu.make_async_remote_copy(
                src_ref=s6.at[k, other],
                dst_ref=r6.at[me],
                send_sem=send_sem.at[5],
                recv_sem=recv_sem.at[5],
                device_id={"mem": other * GROUPS + target},
                device_id_type=MESH,
            ).start()

    order = (2, 1, 3, 0)
    parts = multiply(order[0])
    for index, k in enumerate(order):
        later = multiply(order[index + 1]) if index + 1 < GROUPS else None
        ship(k, parts)
        parts = later
    r6[me] = s6[0, quarter]

    wait_bytes(r6.at[pl.ds(0, members - 1)], recv_sem.at[5])
    gates = [jnp.zeros((LINES, LANES), F32)] * GROUPS
    ups = [jnp.zeros((LINES, LANES), F32)] * GROUPS
    square = jnp.zeros((GROUPS, LANES), F32)
    lane_codes = lax.broadcasted_iota(jnp.int32, (GROUPS, LANES), 1)
    for j in range(members):
        part = r6[j].astype(jnp.int32).astype(F32)
        units, squares = (
            jnp.concatenate(
                [
                    part[start + r * LINES + chunks : start + r * LINES + chunks + 1]
                    for r in range(GROUPS)
                ],
                axis=0,
            )
            for start in (0, short)
        )
        units = value_of(units) * (1.0 / STEPS)
        squares = jnp.where(lane_codes < LANES // 2, squares, squares * (1.0 / STEPS))
        square = square + value_of(squares + pltpu.roll(squares, LANES // 2, 1))
        for r in range(GROUPS):
            own = slice(r * LINES, (r + 1) * LINES)
            gates[r] = gates[r] + part[:short][own] * units[r : r + 1]
            ups[r] = ups[r] + part[short:][own] * units[r : r + 1]
    inverse_two = 1.0 / jnp.sqrt(square / model_width + EPSILON)
    hidden = []
    for r in range(GROUPS):
        gate = gates[r] * inverse_two[r : r + 1]
        hidden.append(gate / (1.0 + jnp.exp(-gate)) * (ups[r] * inverse_two[r : r + 1]))
    s7[...] = jnp.concatenate(hidden, axis=0).astype(BF16)
    r7[me] = s7[...]
    for other in member_order:
        pltpu.make_async_remote_copy(
            src_ref=s7,
            dst_ref=r7.at[me],
            send_sem=send_sem.at[6],
            recv_sem=group_sem.at[group],
            device_id={"mem": other},
            device_id_type=MESH,
        ).start()
    ready("wdown")

    down = jnp.zeros((rows, wdown.shape[1]), F32)
    for k in (0, 1, 3, 2):
        source = lax.rem(group + k, GROUPS)
        arriving = GROUPS - 1 if k == 0 else GROUPS
        wait_bytes(r7.at[pl.ds(0, arriving)], group_sem.at[source])
        for q in range(GROUPS):
            line = k * tall + q * short
            g7[line : line + short, :] = r7[q * GROUPS + source].astype(F32)
        piece = jnp.concatenate(
            [
                g7[pl.ds(k * tall + c, rows, stride=LINES), :].astype(BF16)
                for c in range(chunks)
            ],
            axis=1,
        )
        down = down + jnp.dot(
            piece,
            wdown[pl.ds(pl.multiple_of(source * span, LANES), span), :],
            preferred_element_type=F32,
        )
    out_ref[...] = (after_f + sum_peers(7, down, s7b, r7b)).astype(BF16)

    wait_bytes(r1.at[pl.ds(0, members - 1), pl.ds(0, used)], send_sem.at[0])
    wait_bytes(r2.at[pl.ds(0, members - 1)], send_sem.at[1])
    wait_bytes(r4.at[pl.ds(0, members - 1)], send_sem.at[2])
    wait_bytes(r5.at[pl.ds(0, (members - 1) * HEADS)], send_sem.at[3])
    for phase, landed in ((4, r5b), (7, r7b)):
        wait_bytes(landed.at[pl.ds(0, peers - 1)], send_sem.at[phase])
    for phase, landed in ((5, r6), (6, r7)):
        wait_bytes(landed.at[pl.ds(0, members - 1)], send_sem.at[phase])


def local(
    members,
    peers,
    tokens,
    attn_gain,
    query_key_value_weight,
    paged_key_store,
    paged_value_store,
    lengths,
    block_table,
    out_weight,
    mlp_gain,
    gate_weight,
    up_weight,
    down_weight,
):
    rows, width_part = tokens.shape
    slots, _, block_len, head_dim = paged_key_store.shape
    short = rows * LINES // GROUPS
    exponents = np.arange(head_dim // 2, dtype=np.float32) * np.float32(
        -2.0 * math.log(ROPE_BASE) / head_dim
    )
    inverse = np.exp(exponents.astype(np.float64)).astype(np.float32)
    freq = jnp.asarray(np.concatenate([inverse, inverse])[None, :])

    any_spec = pl.BlockSpec(memory_space=pl.ANY)
    vmem_spec = pl.BlockSpec(memory_space=pltpu.VMEM)
    scratch = [
        pltpu.SMEM(lengths.shape, jnp.int32),
        pltpu.VMEM(tokens.shape, BF16),
        pltpu.VMEM(attn_gain.shape, BF16),
        pltpu.VMEM(mlp_gain.shape, BF16),
        pltpu.VMEM(freq.shape, F32),
        pltpu.VMEM(block_table.shape, jnp.int32),
        pltpu.VMEM(query_key_value_weight.shape, BF16),
        pltpu.VMEM((slots, block_len, head_dim), BF16),
        pltpu.VMEM((slots, block_len, head_dim), BF16),
        pltpu.VMEM(out_weight.shape, BF16),
        pltpu.VMEM(gate_weight.shape, BF16),
        pltpu.VMEM(up_weight.shape, BF16),
        pltpu.VMEM(down_weight.shape, BF16),
        pltpu.VMEM((REQUESTS, GROUP, head_dim), BF16),
        pltpu.VMEM((8, slots), jnp.int32),
        pltpu.SMEM((8, slots), jnp.int32),
        pltpu.VMEM((REQUESTS, GROUP, LANES), F32),
        pltpu.VMEM((slots, GROUP, LANES), F32),
        pltpu.VMEM((rows * rows, LANES), F32),
        pltpu.VMEM((members, rows, LANES), F32),
        pltpu.VMEM((16, LANES), BF16),
        pltpu.VMEM((members, 16, LANES), BF16),
        pltpu.VMEM((members, 2 * HEADS, LANES), F32),
        pltpu.VMEM((members, 2 * HEADS, LANES), F32),
        pltpu.VMEM((HEADS, LANES), F32),
        pltpu.VMEM((members * HEADS, LANES), F32),
        pltpu.VMEM((rows, width_part + LANES), jnp.int16),
        pltpu.VMEM((peers, rows, width_part + LANES), jnp.int16),
        pltpu.VMEM((2 * GROUPS * rows * LINES, LANES), F32),
        pltpu.VMEM((GROUPS, GROUPS, 2 * short, LANES), jnp.int16),
        pltpu.VMEM((members, 2 * short, LANES), jnp.int16),
        pltpu.VMEM((short, LANES), BF16),
        pltpu.VMEM((members, short, LANES), BF16),
        pltpu.VMEM((GROUPS * rows * LINES, LANES), F32),
        pltpu.VMEM((rows, width_part + LANES), jnp.int16),
        pltpu.VMEM((peers, rows, width_part + LANES), jnp.int16),
        pltpu.SemaphoreType.DMA,
        pltpu.SemaphoreType.DMA((6 + 6 * PIECES + 2,)),
        pltpu.SemaphoreType.DMA((8,)),
        pltpu.SemaphoreType.DMA((8,)),
        pltpu.SemaphoreType.DMA((GROUPS,)),
    ]
    return pl.pallas_call(
        functools.partial(kernel, members, peers, width_part * members),
        out_shape=jax.ShapeDtypeStruct(tokens.shape, BF16),
        in_specs=[any_spec] * 13,
        out_specs=vmem_spec,
        scratch_shapes=scratch,
        compiler_params=pltpu.CompilerParams(
            collective_id=0, has_side_effects=True, vmem_limit_bytes=56 * 1024 * 1024
        ),
        name="decoder_layer",
    )(
        lengths,
        tokens,
        attn_gain,
        mlp_gain,
        freq,
        block_table,
        query_key_value_weight,
        paged_key_store,
        paged_value_store,
        out_weight,
        gate_weight,
        up_weight,
        down_weight,
    )


def solution(mesh):
    return jax.shard_map(
        functools.partial(local, mesh.shape["mem"], mesh.shape["mp"]),
        mesh=mesh,
        in_specs=(
            P(None, "mem"),
            P("mem"),
            P("mem", "mp"),
            P("mem", "mp", None, None),
            P("mem", "mp", None, None),
            P(),
            P(),
            P("mp", "mem"),
            P("mem"),
            P("mem", "mp"),
            P("mem", "mp"),
            P("mp", "mem"),
        ),
        out_specs=P(None, "mem"),
        check_vma=False,
    )
```

```python
import functools
import math

import jax
import jax.numpy as jnp
import numpy as np
from jax import lax
from jax.experimental import pallas as pl
from jax.experimental.pallas import tpu as pltpu
from jax.sharding import PartitionSpec as P

MESH = pl.DeviceIdType.MESH
F32 = jnp.float32
BF16 = jnp.bfloat16

EPSILON = 1e-05
ROPE_BASE = 500000.0
FLOOR_SCORE = -1e30
LANES = 128
HEADS = 8
NEW = 4
REQUESTS = 4
GROUP = NEW * HEADS
OWNER = 256
TILE = 32
PARTIAL = 16
GROUPS = 4
LINES = 8
PIECES = 4

HALF_PI = (1.5703125, 0.000484466552734375, -6.397578377557687e-07)


def sine_cosine(angle):
    turns = jnp.floor(angle * (2.0 / math.pi) + 0.5)
    r = ((angle - turns * HALF_PI[0]) - turns * HALF_PI[1]) - turns * HALF_PI[2]
    z = r * r
    sine = r + r * z * (-1.6666654611e-1 + z * (8.3321608736e-3 + z * (-1.9515295891e-4)))
    cosine = 1.0 - 0.5 * z + z * z * (
        4.166664568298827e-2 + z * (-1.388731625493765e-3 + z * 2.443315711809948e-5)
    )
    quadrant = turns - 4.0 * jnp.floor(turns * 0.25)
    odd = (quadrant == 1.0) | (quadrant == 3.0)
    s, c = jnp.where(odd, cosine, sine), jnp.where(odd, sine, cosine)
    s = jnp.where(quadrant >= 2.0, -s, s)
    c = jnp.where((quadrant == 1.0) | (quadrant == 2.0), -c, c)
    return s, c


STEPS = 32000.0
FINE = 256.0


def code_of(value):
    return jnp.log(jnp.maximum(value, 1e-30)) * (FINE / math.log(2.0))


def value_of(code):
    return jnp.exp2(code * (1.0 / FINE))


def kernel(
    members,
    peers,
    model_width,
    lengths_hbm,
    tokens_hbm,
    gain_one_hbm,
    gain_two_hbm,
    freq_hbm,
    table_hbm,
    wqkv_hbm,
    keys_hbm,
    values_hbm,
    wout_hbm,
    wgate_hbm,
    wup_hbm,
    wdown_hbm,
    out_ref,
    lengths,
    tokens,
    gain_one,
    gain_two,
    freq,
    table,
    wqkv,
    keys,
    values,
    wout,
    wgate,
    wup,
    wdown,
    queries,
    codes,
    slot_codes,
    tops_ref,
    scores,
    s1,
    r1,
    s2,
    r2,
    s4,
    r4,
    s5,
    r5,
    s5b,
    r5b,
    g6,
    s6,
    r6,
    s7,
    r7,
    g7,
    s7b,
    r7b,
    code_sem,
    fetch_sem,
    send_sem,
    recv_sem,
    quarter_sem,
    group_sem,
):
    me = lax.axis_index("mem")
    mine = lax.axis_index("mp")
    rows = tokens.shape[0]
    slots = keys.shape[0]
    block_len = keys.shape[1]

    side = math.isqrt(members)
    z, x = me // side, lax.rem(me, side)
    steps_of = lambda d, n: min(d, n - d)
    offsets = sorted(
        ((dz, dx) for dz in range(side) for dx in range(side) if dz or dx),
        key=lambda d: -steps_of(d[0], side) - steps_of(d[1], side),
    )
    member_order = [lax.rem(z + dz, side) * side + lax.rem(x + dx, side) for dz, dx in offsets]
    ring, cores = peers // 2, 2
    y, core = mine // cores, lax.rem(mine, cores)
    offsets = sorted(
        ((dy, dc) for dy in range(ring) for dc in range(cores) if dy or dc),
        key=lambda d: -steps_of(d[0], ring),
    )
    peer_order = [lax.rem(y + dy, ring) * cores + lax.rem(core + dc, cores) for dy, dc in offsets]

    fetched = {}

    def fetch(name, source, target, pieces=1):
        size = target.shape[0] // pieces
        fetched[name] = []
        for p in range(pieces):
            index = sum(len(v) for v in fetched.values())
            if pieces > 1:
                part = pl.ds(p * size, size)
                copy = pltpu.make_async_copy(source.at[part], target.at[part], fetch_sem.at[index])
            else:
                copy = pltpu.make_async_copy(source, target, fetch_sem.at[index])
            copy.start()
            fetched[name].append(copy)

    def ready(*names):
        for name in names:
            for copy in fetched[name]:
                copy.wait()

    fetch("tokens", tokens_hbm, tokens)
    fetch("gain_one", gain_one_hbm, gain_one)
    fetch("wqkv", wqkv_hbm, wqkv, PIECES)

    barrier = pltpu.get_barrier_semaphore()
    for other in member_order:
        pl.semaphore_signal(barrier, inc=1, device_id={"mem": other}, device_id_type=MESH)
    for other in peer_order:
        pl.semaphore_signal(barrier, inc=1, device_id={"mp": other}, device_id_type=MESH)

    fetch("lengths", lengths_hbm, lengths)
    fetch("freq", freq_hbm, freq)
    fetch("table", table_hbm, table)
    fetch("gain_two", gain_two_hbm, gain_two)

    def send_members(phase, source_of, target):
        for other in member_order:
            pltpu.make_async_remote_copy(
                src_ref=source_of(other),
                dst_ref=target,
                send_sem=send_sem.at[phase],
                recv_sem=recv_sem.at[phase],
                device_id={"mem": other},
                device_id_type=MESH,
            ).start()

    def send_peers(phase, source, target):
        for other in peer_order:
            pltpu.make_async_remote_copy(
                src_ref=source,
                dst_ref=target,
                send_sem=send_sem.at[phase],
                recv_sem=recv_sem.at[phase],
                device_id={"mp": other},
                device_id_type=MESH,
            ).start()

    width = tokens.shape[1]

    def sum_peers(phase, partial, staged, landed):
        unit_code = jnp.ceil(code_of(jnp.max(jnp.abs(partial), axis=1, keepdims=True)))
        steps = jnp.floor(partial * (STEPS / value_of(unit_code)) + 0.5)
        staged[:, :width] = steps.astype(jnp.int32).astype(jnp.int16)
        staged[:, width:] = (
            jnp.broadcast_to(unit_code, (rows, LANES)).astype(jnp.int32).astype(jnp.int16)
        )
        send_peers(phase, staged, landed.at[mine])
        landed[mine] = staged[...]
        wait_bytes(landed.at[pl.ds(0, peers - 1)], recv_sem.at[phase])
        total = jnp.zeros((rows, width), F32)
        for j in range(peers):
            part = landed[j].astype(jnp.int32).astype(F32)
            unit = value_of(part[:, width:]) * (1.0 / STEPS)
            total = total + part[:, :width] * jnp.concatenate([unit] * (width // LANES), axis=1)
        return total

    def wait_bytes(window, semaphore):
        pltpu.make_async_copy(window, window, semaphore).wait()

    ready("tokens", "gain_one")
    token_f = tokens[...].astype(F32)
    scaled_in = (token_f * gain_one[...].astype(F32)[None, :]).astype(BF16)
    square_one = jnp.sum(token_f * token_f, axis=1, keepdims=True)
    ready("wqkv")
    projected = jnp.dot(scaled_in, wqkv[...], preferred_element_type=F32)
    for c in range(HEADS + 2):
        s1[pl.ds(c, rows, stride=rows), :] = projected[:, c * LANES : (c + 1) * LANES]
    s1[pl.ds(HEADS + 2, rows, stride=rows), :] = jnp.broadcast_to(square_one, (rows, LANES))

    pl.semaphore_wait(barrier, members - 1 + peers - 1)

    used = HEADS + 3
    send_members(
        0, lambda other: s1.at[pl.ds(other * rows, used)], r1.at[me, pl.ds(0, used)]
    )
    r1[me] = s1[pl.ds(pl.multiple_of(me * rows, rows), rows), :]

    fetch("keys", keys_hbm.at[:, 0], keys, PIECES)
    fetch("values", values_hbm.at[:, 0], values, PIECES)

    request, place = me // NEW, lax.rem(me, NEW)
    ready("lengths", "freq")
    position = (lengths[request] + place).astype(F32)
    sine, cosine = sine_cosine(position * freq[...])
    lane_row = lax.broadcasted_iota(jnp.int32, (1, LANES), 1)
    sine = jnp.where(lane_row < LANES // 2, -sine, sine)

    wait_bytes(r1.at[pl.ds(0, members - 1), pl.ds(0, used)], recv_sem.at[0])
    total = r1[0]
    for j in range(1, members):
        total = total + r1[j]
    inverse_one = 1.0 / jnp.sqrt(total[HEADS + 2 : HEADS + 3, :] / model_width + EPSILON)
    total = total * inverse_one
    turned = total * cosine + pltpu.roll(total, LANES // 2, 1) * sine
    head_row = lax.broadcasted_iota(jnp.int32, total.shape, 0)
    s2[...] = jnp.where(head_row <= HEADS, turned, total).astype(BF16)
    r2[me] = s2[...]
    send_members(1, lambda other: s2, r2.at[me])
    fetch("wout", wout_hbm, wout, 2)
    fetch("wgate", wgate_hbm, wgate, PIECES)
    fetch("wup", wup_hbm, wup, PIECES)
    fetch("wdown", wdown_hbm, wdown, PIECES)

    ready("table")
    first_slot = me * slots
    max_blocks = table.shape[1]
    block_start = lax.broadcasted_iota(jnp.int32, (1, max_blocks), 1) * block_len
    slot_ids = first_slot + lax.broadcasted_iota(jnp.int32, (slots, max_blocks), 0)
    code = jnp.zeros((slots, max_blocks), jnp.int32)
    for r in range(REQUESTS):
        held = jnp.clip(lengths[r] - block_start, 0, block_len)
        held = jnp.where(held > 0, held + r * OWNER, 0)
        code = code + jnp.where(table[r : r + 1, :] == slot_ids, held, 0)
    code = jnp.sum(code, axis=1, keepdims=True)
    diagonal = lax.broadcasted_iota(jnp.int32, (slots, slots), 0) == lax.broadcasted_iota(
        jnp.int32, (slots, slots), 1
    )
    code = jnp.sum(jnp.where(diagonal, code, 0), axis=0, keepdims=True)
    owner_row = code // OWNER
    codes[0:1, :] = code
    to_scalars = pltpu.make_async_copy(codes, slot_codes, code_sem)
    to_scalars.start()

    wait_bytes(r2.at[pl.ds(0, members - 1)], recv_sem.at[1])

    for r in range(REQUESTS):
        queries[r] = jnp.concatenate(
            [r2[r * NEW + t].astype(F32)[:HEADS] for t in range(NEW)], axis=0
        ).astype(BF16)
    factor = math.log2(math.e) / math.sqrt(LANES)
    lane_group = lax.broadcasted_iota(jnp.int32, (GROUP, LANES), 1)
    to_scalars.wait()
    ready("keys")

    def slot_of(slot):
        value = slot_codes[0, slot]
        return value // OWNER, lax.rem(value, OWNER)

    def score_step(step, best):
        for j in range(TILE):
            slot = step * TILE + j
            owner, count = slot_of(slot)
            score = lax.dot_general(
                queries[owner],
                keys[slot],
                (((1,), (1,)), ((), ())),
                preferred_element_type=F32,
            )
            score = jnp.where(lane_group < count, score, FLOOR_SCORE)
            scores[slot] = score
            best = jnp.where(lane_group == slot, jnp.max(score, axis=1, keepdims=True), best)
        return best

    floor = jnp.full((GROUP, LANES), FLOOR_SCORE, F32)
    slot_best = lax.fori_loop(0, slots // TILE, score_step, floor)
    best = []
    for r in range(REQUESTS):
        own = jnp.where(owner_row == r, slot_best, FLOOR_SCORE)
        best.append(jnp.broadcast_to(jnp.max(own, axis=1, keepdims=True), (GROUP, LANES)))
        tops_ref[r] = best[r]
    ready("values")

    def value_step(step, carry):
        sums, mixed = carry[0], list(carry[1])
        for j in range(TILE):
            slot = step * TILE + j
            owner, _ = slot_of(slot)
            weight = jnp.exp2((scores[slot] - tops_ref[owner]) * factor)
            sums = jnp.where(lane_group == slot, jnp.sum(weight, axis=1, keepdims=True), sums)
            high = weight.astype(BF16)
            low = (weight - high.astype(F32)).astype(BF16)
            both = jnp.dot(
                jnp.concatenate([high, low], axis=0), values[slot], preferred_element_type=F32
            )
            both = both[:GROUP] + both[GROUP:]
            for r in range(REQUESTS):
                mixed[r] = mixed[r] + jnp.where(owner == r, both, 0.0)
        return sums, tuple(mixed)

    zero = jnp.zeros((GROUP, LANES), F32)
    slot_sums, mixed = lax.fori_loop(0, slots // TILE, value_step, (zero, (zero,) * REQUESTS))
    lane_head = lax.broadcasted_iota(jnp.int32, (HEADS, LANES), 1) // (LANES // HEADS)
    by_head = lane_head == lax.broadcasted_iota(jnp.int32, (HEADS, LANES), 0)

    def to_line(column):
        return jnp.sum(jnp.where(by_head, column, 0.0), axis=0, keepdims=True)

    def to_column(line):
        column = jnp.max(jnp.where(by_head, line, -jnp.inf), axis=1, keepdims=True)
        return jnp.broadcast_to(column, (HEADS, LANES))

    for r in range(REQUESTS):
        own = jnp.where(owner_row == r, slot_sums, 0.0)
        whole = jnp.broadcast_to(jnp.sum(own, axis=1, keepdims=True), (GROUP, LANES))
        for t in range(NEW):
            part = slice(t * HEADS, (t + 1) * HEADS)
            line = (r * NEW + t) * PARTIAL
            s4[line : line + HEADS, :] = mixed[r][part]
            s4[line + HEADS : line + HEADS + 1, :] = to_line(best[r][part])
            s4[line + HEADS + 1 : line + HEADS + 2, :] = to_line(whole[part])
    mine_4 = pl.ds(pl.multiple_of(me * PARTIAL, PARTIAL), PARTIAL)
    sent = HEADS + 2
    send_members(
        2,
        lambda other: s4.at[pl.ds(other * PARTIAL, sent)],
        r4.at[pl.ds(me * PARTIAL, sent)],
    )
    r4[mine_4, :] = s4[mine_4, :]

    row_queries = r2[me].astype(F32)[:HEADS]
    own_scores, own_values = [], []
    for t in range(NEW):
        fresh = r2[request * NEW + t].astype(F32)
        score = jnp.sum(row_queries * fresh[HEADS : HEADS + 1], axis=1, keepdims=True)
        score = jnp.broadcast_to(score, (HEADS, LANES))
        own_scores.append(jnp.where(t <= place, score, FLOOR_SCORE))
        own_values.append(fresh[HEADS + 1 : HEADS + 2])
    top = to_line(functools.reduce(jnp.maximum, own_scores))

    wait_bytes(r4.at[pl.ds(0, (members - 1) * sent)], recv_sem.at[2])
    tops = r4[pl.ds(HEADS, members, stride=PARTIAL), :]
    wholes = r4[pl.ds(HEADS + 1, members, stride=PARTIAL), :]
    top = jnp.maximum(top, jnp.max(tops, axis=0, keepdims=True))
    shrink = jnp.exp2((tops - top) * factor)
    whole = to_column(jnp.sum(wholes * shrink, axis=0, keepdims=True))
    top = to_column(top)
    mix = jnp.zeros((HEADS, LANES), F32)
    for t in range(NEW):
        weight = jnp.exp2((own_scores[t] - top) * factor)
        whole = whole + weight
        mix = mix + weight * own_values[t]
    for j in range(members):
        mix = mix + r4[j * PARTIAL : j * PARTIAL + HEADS, :] * to_column(shrink[j : j + 1])
    s5[...] = mix / whole
    own_rows = pl.ds(pl.multiple_of(me * HEADS, HEADS), HEADS)
    r5[own_rows, :] = s5[...]
    send_members(3, lambda other: s5, r5.at[own_rows])
    ready("wout")
    wait_bytes(r5.at[pl.ds(0, (members - 1) * HEADS)], recv_sem.at[3])

    attended = jnp.concatenate(
        [r5[pl.ds(h, rows, stride=HEADS), :].astype(BF16) for h in range(HEADS)], axis=1
    )
    partial = jnp.dot(attended, wout[...], preferred_element_type=F32)
    after_f = (token_f + sum_peers(4, partial, s5b, r5b)).astype(BF16).astype(F32)
    ready("gain_two", "wgate", "wup")

    scaled_mid = (after_f * gain_two[...].astype(F32)[None, :]).astype(BF16)
    square_mid = jnp.sum(after_f * after_f, axis=1, keepdims=True)
    square_code = code_of(square_mid)
    square_whole = jnp.floor(square_code)
    square_rest = jnp.floor((square_code - square_whole) * STEPS + 0.5)
    lane_rows = lax.broadcasted_iota(jnp.int32, (rows, LANES), 1)
    square_line = jnp.where(lane_rows < LANES // 2, square_whole, square_rest)

    quarter, group = me // GROUPS, lax.rem(me, GROUPS)
    span = wgate.shape[1] // GROUPS
    chunks = span // LANES
    tall = rows * LINES
    short = tall // GROUPS

    def multiply(k):
        columns = pl.ds(pl.multiple_of(lax.rem(group + k, GROUPS) * span, LANES), span)
        return [
            jnp.dot(scaled_mid, weight[:, columns], preferred_element_type=F32)
            for weight in (wgate, wup)
        ]

    def ship(k, parts):
        target = lax.rem(group + k, GROUPS)
        largest = jnp.maximum(jnp.abs(parts[0]), jnp.abs(parts[1]))
        unit_code = jnp.ceil(code_of(jnp.max(largest, axis=1, keepdims=True)))
        to_steps = STEPS / value_of(unit_code)
        unit_line = jnp.broadcast_to(unit_code, (rows, LANES))
        for index, (part, extra) in enumerate(zip(parts, (unit_line, square_line))):
            base = (2 * k + index) * tall
            steps = jnp.floor(part * to_steps + 0.5)
            for c in range(chunks):
                g6[pl.ds(base + c, rows, stride=LINES), :] = steps[:, c * LANES : (c + 1) * LANES]
            g6[pl.ds(base + chunks, rows, stride=LINES), :] = extra
            for q in range(GROUPS):
                piece = g6[base + q * short : base + (q + 1) * short, :]
                s6[k, q, index * short : (index + 1) * short, :] = piece.astype(jnp.int32).astype(
                    jnp.int16
                )
        for j in (2, 1, 3, 0) if k else (2, 1, 3):
            other = lax.rem(quarter + j, GROUPS)
            pltpu.make_async_remote_copy(
                src_ref=s6.at[k, other],
                dst_ref=r6.at[me],
                send_sem=send_sem.at[5],
                recv_sem=quarter_sem.at[k],
                device_id={"mem": other * GROUPS + target},
                device_id_type=MESH,
            ).start()

    order = (2, 1, 3, 0)
    parts = multiply(order[0])
    for index, k in enumerate(order):
        later = multiply(order[index + 1]) if index + 1 < GROUPS else None
        ship(k, parts)
        parts = later
    r6[me] = s6[0, quarter]

    gates = [jnp.zeros((LINES, LANES), F32)] * GROUPS
    ups = [jnp.zeros((LINES, LANES), F32)] * GROUPS
    square = jnp.zeros((GROUPS, LANES), F32)
    lane_codes = lax.broadcasted_iota(jnp.int32, (GROUPS, LANES), 1)
    for k, q in [(k, q) for k in order for q in range(GROUPS)]:
        if q == 0:
            arriving = GROUPS if k else GROUPS - 1
            wait_bytes(r6.at[pl.ds(0, arriving)], quarter_sem.at[k])
        sender = q * GROUPS + lax.rem(group + GROUPS - k, GROUPS)
        part = r6[sender].astype(jnp.int32).astype(F32)
        units, squares = (
            jnp.concatenate(
                [
                    part[start + r * LINES + chunks : start + r * LINES + chunks + 1]
                    for r in range(GROUPS)
                ],
                axis=0,
            )
            for start in (0, short)
        )
        units = value_of(units) * (1.0 / STEPS)
        squares = jnp.where(lane_codes < LANES // 2, squares, squares * (1.0 / STEPS))
        square = square + value_of(squares + pltpu.roll(squares, LANES // 2, 1))
        for r in range(GROUPS):
            own = slice(r * LINES, (r + 1) * LINES)
            gates[r] = gates[r] + part[:short][own] * units[r : r + 1]
            ups[r] = ups[r] + part[short:][own] * units[r : r + 1]
    inverse_two = 1.0 / jnp.sqrt(square / model_width + EPSILON)
    hidden = []
    for r in range(GROUPS):
        gate = gates[r] * inverse_two[r : r + 1]
        hidden.append(gate / (1.0 + jnp.exp(-gate)) * (ups[r] * inverse_two[r : r + 1]))
    s7[...] = jnp.concatenate(hidden, axis=0).astype(BF16)
    r7[me] = s7[...]
    for other in member_order:
        pltpu.make_async_remote_copy(
            src_ref=s7,
            dst_ref=r7.at[me],
            send_sem=send_sem.at[6],
            recv_sem=group_sem.at[group],
            device_id={"mem": other},
            device_id_type=MESH,
        ).start()
    ready("wdown")

    down = jnp.zeros((rows, wdown.shape[1]), F32)
    for k in (0, 1, 3, 2):
        source = lax.rem(group + k, GROUPS)
        arriving = GROUPS - 1 if k == 0 else GROUPS
        wait_bytes(r7.at[pl.ds(0, arriving)], group_sem.at[source])
        for q in range(GROUPS):
            line = k * tall + q * short
            g7[line : line + short, :] = r7[q * GROUPS + source].astype(F32)
        piece = jnp.concatenate(
            [
                g7[pl.ds(k * tall + c, rows, stride=LINES), :].astype(BF16)
                for c in range(chunks)
            ],
            axis=1,
        )
        down = down + jnp.dot(
            piece,
            wdown[pl.ds(pl.multiple_of(source * span, LANES), span), :],
            preferred_element_type=F32,
        )
    out_ref[...] = (after_f + sum_peers(7, down, s7b, r7b)).astype(BF16)

    wait_bytes(r1.at[pl.ds(0, members - 1), pl.ds(0, used)], send_sem.at[0])
    wait_bytes(r2.at[pl.ds(0, members - 1)], send_sem.at[1])
    wait_bytes(r4.at[pl.ds(0, (members - 1) * sent)], send_sem.at[2])
    wait_bytes(r5.at[pl.ds(0, (members - 1) * HEADS)], send_sem.at[3])
    for phase, landed in ((4, r5b), (7, r7b)):
        wait_bytes(landed.at[pl.ds(0, peers - 1)], send_sem.at[phase])
    for phase, landed in ((5, r6), (6, r7)):
        wait_bytes(landed.at[pl.ds(0, members - 1)], send_sem.at[phase])


def local(
    members,
    peers,
    tokens,
    attn_gain,
    query_key_value_weight,
    paged_key_store,
    paged_value_store,
    lengths,
    block_table,
    out_weight,
    mlp_gain,
    gate_weight,
    up_weight,
    down_weight,
):
    rows, width_part = tokens.shape
    slots, _, block_len, head_dim = paged_key_store.shape
    short = rows * LINES // GROUPS
    exponents = np.arange(head_dim // 2, dtype=np.float32) * np.float32(
        -2.0 * math.log(ROPE_BASE) / head_dim
    )
    inverse = np.exp(exponents.astype(np.float64)).astype(np.float32)
    freq = jnp.asarray(np.concatenate([inverse, inverse])[None, :])

    any_spec = pl.BlockSpec(memory_space=pl.ANY)
    vmem_spec = pl.BlockSpec(memory_space=pltpu.VMEM)
    scratch = [
        pltpu.SMEM(lengths.shape, jnp.int32),
        pltpu.VMEM(tokens.shape, BF16),
        pltpu.VMEM(attn_gain.shape, BF16),
        pltpu.VMEM(mlp_gain.shape, BF16),
        pltpu.VMEM(freq.shape, F32),
        pltpu.VMEM(block_table.shape, jnp.int32),
        pltpu.VMEM(query_key_value_weight.shape, BF16),
        pltpu.VMEM((slots, block_len, head_dim), BF16),
        pltpu.VMEM((slots, block_len, head_dim), BF16),
        pltpu.VMEM(out_weight.shape, BF16),
        pltpu.VMEM(gate_weight.shape, BF16),
        pltpu.VMEM(up_weight.shape, BF16),
        pltpu.VMEM(down_weight.shape, BF16),
        pltpu.VMEM((REQUESTS, GROUP, head_dim), BF16),
        pltpu.VMEM((8, slots), jnp.int32),
        pltpu.SMEM((8, slots), jnp.int32),
        pltpu.VMEM((REQUESTS, GROUP, LANES), F32),
        pltpu.VMEM((slots, GROUP, LANES), F32),
        pltpu.VMEM((rows * rows, LANES), F32),
        pltpu.VMEM((members, rows, LANES), F32),
        pltpu.VMEM((16, LANES), BF16),
        pltpu.VMEM((members, 16, LANES), BF16),
        pltpu.VMEM((members * PARTIAL, LANES), F32),
        pltpu.VMEM((members * PARTIAL, LANES), F32),
        pltpu.VMEM((HEADS, LANES), F32),
        pltpu.VMEM((members * HEADS, LANES), F32),
        pltpu.VMEM((rows, width_part + LANES), jnp.int16),
        pltpu.VMEM((peers, rows, width_part + LANES), jnp.int16),
        pltpu.VMEM((2 * GROUPS * rows * LINES, LANES), F32),
        pltpu.VMEM((GROUPS, GROUPS, 2 * short, LANES), jnp.int16),
        pltpu.VMEM((members, 2 * short, LANES), jnp.int16),
        pltpu.VMEM((short, LANES), BF16),
        pltpu.VMEM((members, short, LANES), BF16),
        pltpu.VMEM((GROUPS * rows * LINES, LANES), F32),
        pltpu.VMEM((rows, width_part + LANES), jnp.int16),
        pltpu.VMEM((peers, rows, width_part + LANES), jnp.int16),
        pltpu.SemaphoreType.DMA,
        pltpu.SemaphoreType.DMA((6 + 6 * PIECES + 2,)),
        pltpu.SemaphoreType.DMA((8,)),
        pltpu.SemaphoreType.DMA((8,)),
        pltpu.SemaphoreType.DMA((GROUPS,)),
        pltpu.SemaphoreType.DMA((GROUPS,)),
    ]
    return pl.pallas_call(
        functools.partial(kernel, members, peers, width_part * members),
        out_shape=jax.ShapeDtypeStruct(tokens.shape, BF16),
        in_specs=[any_spec] * 13,
        out_specs=vmem_spec,
        scratch_shapes=scratch,
        compiler_params=pltpu.CompilerParams(
            collective_id=0, has_side_effects=True, vmem_limit_bytes=56 * 1024 * 1024
        ),
        name="decoder_layer",
    )(
        lengths,
        tokens,
        attn_gain,
        mlp_gain,
        freq,
        block_table,
        query_key_value_weight,
        paged_key_store,
        paged_value_store,
        out_weight,
        gate_weight,
        up_weight,
        down_weight,
    )


def solution(mesh):
    return jax.shard_map(
        functools.partial(local, mesh.shape["mem"], mesh.shape["mp"]),
        mesh=mesh,
        in_specs=(
            P(None, "mem"),
            P("mem"),
            P("mem", "mp"),
            P("mem", "mp", None, None),
            P("mem", "mp", None, None),
            P(),
            P(),
            P("mp", "mem"),
            P("mem"),
            P("mem", "mp"),
            P("mem", "mp"),
            P("mp", "mem"),
        ),
        out_specs=P(None, "mem"),
        check_vma=False,
    )
```

```python
import functools
import math

import jax
import jax.numpy as jnp
import numpy as np
from jax import lax
from jax.experimental import pallas as pl
from jax.experimental.pallas import tpu as pltpu
from jax.sharding import PartitionSpec as P

MESH = pl.DeviceIdType.MESH
F32 = jnp.float32
BF16 = jnp.bfloat16

EPSILON = 1e-05
ROPE_BASE = 500000.0
FLOOR_SCORE = -1e30
LANES = 128
HEADS = 8
NEW = 4
REQUESTS = 4
GROUP = NEW * HEADS
OWNER = 256
TILE = 32
PARTIAL = 16
GROUPS = 4
LINES = 8
PIECES = 4

HALF_PI = (1.5703125, 0.000484466552734375, -6.397578377557687e-07)


def sine_cosine(angle):
    turns = jnp.floor(angle * (2.0 / math.pi) + 0.5)
    r = ((angle - turns * HALF_PI[0]) - turns * HALF_PI[1]) - turns * HALF_PI[2]
    z = r * r
    sine = r + r * z * (-1.6666654611e-1 + z * (8.3321608736e-3 + z * (-1.9515295891e-4)))
    cosine = 1.0 - 0.5 * z + z * z * (
        4.166664568298827e-2 + z * (-1.388731625493765e-3 + z * 2.443315711809948e-5)
    )
    quadrant = turns - 4.0 * jnp.floor(turns * 0.25)
    odd = (quadrant == 1.0) | (quadrant == 3.0)
    s, c = jnp.where(odd, cosine, sine), jnp.where(odd, sine, cosine)
    s = jnp.where(quadrant >= 2.0, -s, s)
    c = jnp.where((quadrant == 1.0) | (quadrant == 2.0), -c, c)
    return s, c


STEPS = 32000.0
FINE = 256.0


def code_of(value):
    return jnp.log(jnp.maximum(value, 1e-30)) * (FINE / math.log(2.0))


def value_of(code):
    return jnp.exp2(code * (1.0 / FINE))


def kernel(
    members,
    peers,
    model_width,
    lengths_hbm,
    tokens_hbm,
    gain_one_hbm,
    gain_two_hbm,
    freq_hbm,
    table_hbm,
    wqkv_hbm,
    keys_hbm,
    values_hbm,
    wout_hbm,
    wgate_hbm,
    wup_hbm,
    wdown_hbm,
    out_ref,
    lengths,
    tokens,
    gain_one,
    gain_two,
    freq,
    table,
    wqkv,
    keys,
    values,
    wout,
    wgate,
    wup,
    wdown,
    queries,
    codes,
    slot_codes,
    tops_ref,
    scores,
    s1,
    r1,
    s2,
    r2,
    s4,
    r4,
    s5,
    r5,
    s5b,
    r5b,
    s5c,
    r5c,
    g6,
    s6,
    r6,
    s7,
    r7,
    g7,
    s7b,
    r7b,
    s7c,
    r7c,
    code_sem,
    fetch_sem,
    send_sem,
    recv_sem,
    quarter_sem,
    group_sem,
):
    me = lax.axis_index("mem")
    mine = lax.axis_index("mp")
    rows = tokens.shape[0]
    slots = keys.shape[0]
    block_len = keys.shape[1]

    side = math.isqrt(members)
    z, x = me // side, lax.rem(me, side)
    steps_of = lambda d, n: min(d, n - d)
    offsets = sorted(
        ((dz, dx) for dz in range(side) for dx in range(side) if dz or dx),
        key=lambda d: -steps_of(d[0], side) - steps_of(d[1], side),
    )
    member_order = [lax.rem(z + dz, side) * side + lax.rem(x + dx, side) for dz, dx in offsets]
    ring, cores = peers // 2, 2
    y, core = mine // cores, lax.rem(mine, cores)
    peer_order = [lax.rem(y + dy, ring) * cores + core for dy in (ring // 2, 1, ring - 1)]
    partner = y * cores + 1 - core

    fetched = {}

    def fetch(name, source, target, pieces=1):
        size = target.shape[0] // pieces
        fetched[name] = []
        for p in range(pieces):
            index = sum(len(v) for v in fetched.values())
            if pieces > 1:
                part = pl.ds(p * size, size)
                copy = pltpu.make_async_copy(source.at[part], target.at[part], fetch_sem.at[index])
            else:
                copy = pltpu.make_async_copy(source, target, fetch_sem.at[index])
            copy.start()
            fetched[name].append(copy)

    def ready(*names):
        for name in names:
            for copy in fetched[name]:
                copy.wait()

    fetch("tokens", tokens_hbm, tokens)
    fetch("gain_one", gain_one_hbm, gain_one)
    fetch("wqkv", wqkv_hbm, wqkv, PIECES)

    barrier = pltpu.get_barrier_semaphore()
    for other in member_order:
        pl.semaphore_signal(barrier, inc=1, device_id={"mem": other}, device_id_type=MESH)
    for other in peer_order + [partner]:
        pl.semaphore_signal(barrier, inc=1, device_id={"mp": other}, device_id_type=MESH)

    fetch("lengths", lengths_hbm, lengths)
    fetch("freq", freq_hbm, freq)
    fetch("table", table_hbm, table)
    fetch("gain_two", gain_two_hbm, gain_two)

    def send_members(phase, source_of, target):
        for other in member_order:
            pltpu.make_async_remote_copy(
                src_ref=source_of(other),
                dst_ref=target,
                send_sem=send_sem.at[phase],
                recv_sem=recv_sem.at[phase],
                device_id={"mem": other},
                device_id_type=MESH,
            ).start()

    width = tokens.shape[1]

    def send_peer(phase, source, target, other):
        pltpu.make_async_remote_copy(
            src_ref=source,
            dst_ref=target,
            send_sem=send_sem.at[phase],
            recv_sem=recv_sem.at[phase],
            device_id={"mp": other},
            device_id_type=MESH,
        ).start()

    def sum_peers(phase, partial, staged, landed, summed, paired):
        unit_code = jnp.ceil(code_of(jnp.max(jnp.abs(partial), axis=1, keepdims=True)))
        steps = jnp.floor(partial * (STEPS / value_of(unit_code)) + 0.5)
        staged[:, :width] = steps.astype(jnp.int32).astype(jnp.int16)
        staged[:, width:] = (
            jnp.broadcast_to(unit_code, (rows, LANES)).astype(jnp.int32).astype(jnp.int16)
        )
        for other in peer_order:
            send_peer(phase, staged, landed.at[y], other)
        landed[y] = staged[...]
        wait_bytes(landed.at[pl.ds(0, ring - 1)], recv_sem.at[phase])
        total = jnp.zeros((rows, width), F32)
        for j in range(ring):
            part = landed[j].astype(jnp.int32).astype(F32)
            unit = value_of(part[:, width:]) * (1.0 / STEPS)
            total = total + part[:, :width] * jnp.concatenate([unit] * (width // LANES), axis=1)
        summed[...] = total
        send_peer(phase + 1, summed, paired, partner)
        wait_bytes(paired, recv_sem.at[phase + 1])
        return total + paired[...]

    def wait_bytes(window, semaphore):
        pltpu.make_async_copy(window, window, semaphore).wait()

    ready("tokens", "gain_one")
    token_f = tokens[...].astype(F32)
    scaled_in = (token_f * gain_one[...].astype(F32)[None, :]).astype(BF16)
    square_one = jnp.sum(token_f * token_f, axis=1, keepdims=True)
    ready("wqkv")
    projected = jnp.dot(scaled_in, wqkv[...], preferred_element_type=F32)
    for c in range(HEADS + 2):
        s1[pl.ds(c, rows, stride=rows), :] = projected[:, c * LANES : (c + 1) * LANES]
    s1[pl.ds(HEADS + 2, rows, stride=rows), :] = jnp.broadcast_to(square_one, (rows, LANES))

    pl.semaphore_wait(barrier, len(member_order) + len(peer_order) + 1)

    used = HEADS + 3
    send_members(
        0, lambda other: s1.at[pl.ds(other * rows, used)], r1.at[me, pl.ds(0, used)]
    )
    r1[me] = s1[pl.ds(pl.multiple_of(me * rows, rows), rows), :]

    fetch("keys", keys_hbm.at[:, 0], keys, PIECES)
    fetch("values", values_hbm.at[:, 0], values, PIECES)

    request, place = me // NEW, lax.rem(me, NEW)
    ready("lengths", "freq")
    position = (lengths[request] + place).astype(F32)
    sine, cosine = sine_cosine(position * freq[...])
    lane_row = lax.broadcasted_iota(jnp.int32, (1, LANES), 1)
    sine = jnp.where(lane_row < LANES // 2, -sine, sine)

    wait_bytes(r1.at[pl.ds(0, members - 1), pl.ds(0, used)], recv_sem.at[0])
    total = r1[0]
    for j in range(1, members):
        total = total + r1[j]
    inverse_one = 1.0 / jnp.sqrt(total[HEADS + 2 : HEADS + 3, :] / model_width + EPSILON)
    total = total * inverse_one
    turned = total * cosine + pltpu.roll(total, LANES // 2, 1) * sine
    head_row = lax.broadcasted_iota(jnp.int32, total.shape, 0)
    s2[...] = jnp.where(head_row <= HEADS, turned, total).astype(BF16)
    r2[me] = s2[...]
    send_members(1, lambda other: s2, r2.at[me])
    fetch("wout", wout_hbm, wout, 2)
    fetch("wgate", wgate_hbm, wgate, PIECES)
    fetch("wup", wup_hbm, wup, PIECES)
    fetch("wdown", wdown_hbm, wdown, PIECES)

    ready("table")
    first_slot = me * slots
    max_blocks = table.shape[1]
    block_start = lax.broadcasted_iota(jnp.int32, (1, max_blocks), 1) * block_len
    slot_ids = first_slot + lax.broadcasted_iota(jnp.int32, (slots, max_blocks), 0)
    code = jnp.zeros((slots, max_blocks), jnp.int32)
    for r in range(REQUESTS):
        held = jnp.clip(lengths[r] - block_start, 0, block_len)
        held = jnp.where(held > 0, held + r * OWNER, 0)
        code = code + jnp.where(table[r : r + 1, :] == slot_ids, held, 0)
    code = jnp.sum(code, axis=1, keepdims=True)
    diagonal = lax.broadcasted_iota(jnp.int32, (slots, slots), 0) == lax.broadcasted_iota(
        jnp.int32, (slots, slots), 1
    )
    code = jnp.sum(jnp.where(diagonal, code, 0), axis=0, keepdims=True)
    owner_row = code // OWNER
    codes[0:1, :] = code
    to_scalars = pltpu.make_async_copy(codes, slot_codes, code_sem)
    to_scalars.start()

    wait_bytes(r2.at[pl.ds(0, members - 1)], recv_sem.at[1])

    for r in range(REQUESTS):
        queries[r] = jnp.concatenate(
            [r2[r * NEW + t].astype(F32)[:HEADS] for t in range(NEW)], axis=0
        ).astype(BF16)
    factor = math.log2(math.e) / math.sqrt(LANES)
    lane_group = lax.broadcasted_iota(jnp.int32, (GROUP, LANES), 1)
    to_scalars.wait()
    ready("keys")

    def slot_of(slot):
        value = slot_codes[0, slot]
        return value // OWNER, lax.rem(value, OWNER)

    def score_step(step, best):
        for j in range(TILE):
            slot = step * TILE + j
            owner, count = slot_of(slot)
            score = lax.dot_general(
                queries[owner],
                keys[slot],
                (((1,), (1,)), ((), ())),
                preferred_element_type=F32,
            )
            score = jnp.where(lane_group < count, score, FLOOR_SCORE)
            scores[slot] = score
            best = jnp.where(lane_group == slot, jnp.max(score, axis=1, keepdims=True), best)
        return best

    floor = jnp.full((GROUP, LANES), FLOOR_SCORE, F32)
    slot_best = lax.fori_loop(0, slots // TILE, score_step, floor)
    best = []
    for r in range(REQUESTS):
        own = jnp.where(owner_row == r, slot_best, FLOOR_SCORE)
        best.append(jnp.broadcast_to(jnp.max(own, axis=1, keepdims=True), (GROUP, LANES)))
        tops_ref[r] = best[r]
    ready("values")

    def value_step(step, carry):
        sums, mixed = carry[0], list(carry[1])
        for j in range(TILE):
            slot = step * TILE + j
            owner, _ = slot_of(slot)
            weight = jnp.exp2((scores[slot] - tops_ref[owner]) * factor)
            sums = jnp.where(lane_group == slot, jnp.sum(weight, axis=1, keepdims=True), sums)
            high = weight.astype(BF16)
            low = (weight - high.astype(F32)).astype(BF16)
            both = jnp.dot(
                jnp.concatenate([high, low], axis=0), values[slot], preferred_element_type=F32
            )
            both = both[:GROUP] + both[GROUP:]
            for r in range(REQUESTS):
                mixed[r] = mixed[r] + jnp.where(owner == r, both, 0.0)
        return sums, tuple(mixed)

    zero = jnp.zeros((GROUP, LANES), F32)
    slot_sums, mixed = lax.fori_loop(0, slots // TILE, value_step, (zero, (zero,) * REQUESTS))
    lane_head = lax.broadcasted_iota(jnp.int32, (HEADS, LANES), 1) // (LANES // HEADS)
    by_head = lane_head == lax.broadcasted_iota(jnp.int32, (HEADS, LANES), 0)

    def to_line(column):
        return jnp.sum(jnp.where(by_head, column, 0.0), axis=0, keepdims=True)

    def to_column(line):
        column = jnp.max(jnp.where(by_head, line, -jnp.inf), axis=1, keepdims=True)
        return jnp.broadcast_to(column, (HEADS, LANES))

    for r in range(REQUESTS):
        own = jnp.where(owner_row == r, slot_sums, 0.0)
        whole = jnp.broadcast_to(jnp.sum(own, axis=1, keepdims=True), (GROUP, LANES))
        for t in range(NEW):
            part = slice(t * HEADS, (t + 1) * HEADS)
            line = (r * NEW + t) * PARTIAL
            s4[line : line + HEADS, :] = mixed[r][part]
            s4[line + HEADS : line + HEADS + 1, :] = to_line(best[r][part])
            s4[line + HEADS + 1 : line + HEADS + 2, :] = to_line(whole[part])
    mine_4 = pl.ds(pl.multiple_of(me * PARTIAL, PARTIAL), PARTIAL)
    sent = HEADS + 2
    send_members(
        2,
        lambda other: s4.at[pl.ds(other * PARTIAL, sent)],
        r4.at[pl.ds(me * PARTIAL, sent)],
    )
    r4[mine_4, :] = s4[mine_4, :]

    row_queries = r2[me].astype(F32)[:HEADS]
    own_scores, own_values = [], []
    for t in range(NEW):
        fresh = r2[request * NEW + t].astype(F32)
        score = jnp.sum(row_queries * fresh[HEADS : HEADS + 1], axis=1, keepdims=True)
        score = jnp.broadcast_to(score, (HEADS, LANES))
        own_scores.append(jnp.where(t <= place, score, FLOOR_SCORE))
        own_values.append(fresh[HEADS + 1 : HEADS + 2])
    top = to_line(functools.reduce(jnp.maximum, own_scores))

    wait_bytes(r4.at[pl.ds(0, (members - 1) * sent)], recv_sem.at[2])
    tops = r4[pl.ds(HEADS, members, stride=PARTIAL), :]
    wholes = r4[pl.ds(HEADS + 1, members, stride=PARTIAL), :]
    top = jnp.maximum(top, jnp.max(tops, axis=0, keepdims=True))
    shrink = jnp.exp2((tops - top) * factor)
    whole = to_column(jnp.sum(wholes * shrink, axis=0, keepdims=True))
    top = to_column(top)
    mix = jnp.zeros((HEADS, LANES), F32)
    for t in range(NEW):
        weight = jnp.exp2((own_scores[t] - top) * factor)
        whole = whole + weight
        mix = mix + weight * own_values[t]
    for j in range(members):
        mix = mix + r4[j * PARTIAL : j * PARTIAL + HEADS, :] * to_column(shrink[j : j + 1])
    s5[...] = mix / whole
    own_rows = pl.ds(pl.multiple_of(me * HEADS, HEADS), HEADS)
    r5[own_rows, :] = s5[...]
    send_members(3, lambda other: s5, r5.at[own_rows])
    ready("wout")
    wait_bytes(r5.at[pl.ds(0, (members - 1) * HEADS)], recv_sem.at[3])

    attended = jnp.concatenate(
        [r5[pl.ds(h, rows, stride=HEADS), :].astype(BF16) for h in range(HEADS)], axis=1
    )
    partial = jnp.dot(attended, wout[...], preferred_element_type=F32)
    after_f = (token_f + sum_peers(4, partial, s5b, r5b, s5c, r5c)).astype(BF16).astype(F32)
    ready("gain_two", "wgate", "wup")

    scaled_mid = (after_f * gain_two[...].astype(F32)[None, :]).astype(BF16)
    square_mid = jnp.sum(after_f * after_f, axis=1, keepdims=True)
    square_code = code_of(square_mid)
    square_whole = jnp.floor(square_code)
    square_rest = jnp.floor((square_code - square_whole) * STEPS + 0.5)
    lane_rows = lax.broadcasted_iota(jnp.int32, (rows, LANES), 1)
    square_line = jnp.where(lane_rows < LANES // 2, square_whole, square_rest)

    quarter, group = me // GROUPS, lax.rem(me, GROUPS)
    span = wgate.shape[1] // GROUPS
    chunks = span // LANES
    tall = rows * LINES
    short = tall // GROUPS

    def multiply(k):
        columns = pl.ds(pl.multiple_of(lax.rem(group + k, GROUPS) * span, LANES), span)
        return [
            jnp.dot(scaled_mid, weight[:, columns], preferred_element_type=F32)
            for weight in (wgate, wup)
        ]

    def ship(k, parts):
        target = lax.rem(group + k, GROUPS)
        largest = jnp.maximum(jnp.abs(parts[0]), jnp.abs(parts[1]))
        unit_code = jnp.ceil(code_of(jnp.max(largest, axis=1, keepdims=True)))
        to_steps = STEPS / value_of(unit_code)
        unit_line = jnp.broadcast_to(unit_code, (rows, LANES))
        for index, (part, extra) in enumerate(zip(parts, (unit_line, square_line))):
            base = (2 * k + index) * tall
            steps = jnp.floor(part * to_steps + 0.5)
            for c in range(chunks):
                g6[pl.ds(base + c, rows, stride=LINES), :] = steps[:, c * LANES : (c + 1) * LANES]
            g6[pl.ds(base + chunks, rows, stride=LINES), :] = extra
            for q in range(GROUPS):
                piece = g6[base + q * short : base + (q + 1) * short, :]
                s6[k, q, index * short : (index + 1) * short, :] = piece.astype(jnp.int32).astype(
                    jnp.int16
                )
        for j in (2, 1, 3, 0) if k else (2, 1, 3):
            other = lax.rem(quarter + j, GROUPS)
            pltpu.make_async_remote_copy(
                src_ref=s6.at[k, other],
                dst_ref=r6.at[me],
                send_sem=send_sem.at[6],
                recv_sem=quarter_sem.at[k],
                device_id={"mem": other * GROUPS + target},
                device_id_type=MESH,
            ).start()

    order = (2, 1, 3, 0)
    parts = multiply(order[0])
    for index, k in enumerate(order):
        later = multiply(order[index + 1]) if index + 1 < GROUPS else None
        ship(k, parts)
        parts = later
    r6[me] = s6[0, quarter]

    gates = [jnp.zeros((LINES, LANES), F32)] * GROUPS
    ups = [jnp.zeros((LINES, LANES), F32)] * GROUPS
    square = jnp.zeros((GROUPS, LANES), F32)
    lane_codes = lax.broadcasted_iota(jnp.int32, (GROUPS, LANES), 1)
    for k, q in [(k, q) for k in order for q in range(GROUPS)]:
        if q == 0:
            arriving = GROUPS if k else GROUPS - 1
            wait_bytes(r6.at[pl.ds(0, arriving)], quarter_sem.at[k])
        sender = q * GROUPS + lax.rem(group + GROUPS - k, GROUPS)
        part = r6[sender].astype(jnp.int32).astype(F32)
        units, squares = (
            jnp.concatenate(
                [
                    part[start + r * LINES + chunks : start + r * LINES + chunks + 1]
                    for r in range(GROUPS)
                ],
                axis=0,
            )
            for start in (0, short)
        )
        units = value_of(units) * (1.0 / STEPS)
        squares = jnp.where(lane_codes < LANES // 2, squares, squares * (1.0 / STEPS))
        square = square + value_of(squares + pltpu.roll(squares, LANES // 2, 1))
        for r in range(GROUPS):
            own = slice(r * LINES, (r + 1) * LINES)
            gates[r] = gates[r] + part[:short][own] * units[r : r + 1]
            ups[r] = ups[r] + part[short:][own] * units[r : r + 1]
    inverse_two = 1.0 / jnp.sqrt(square / model_width + EPSILON)
    hidden = []
    for r in range(GROUPS):
        gate = gates[r] * inverse_two[r : r + 1]
        hidden.append(gate / (1.0 + jnp.exp(-gate)) * (ups[r] * inverse_two[r : r + 1]))
    s7[...] = jnp.concatenate(hidden, axis=0).astype(BF16)
    r7[me] = s7[...]
    for other in member_order:
        pltpu.make_async_remote_copy(
            src_ref=s7,
            dst_ref=r7.at[me],
            send_sem=send_sem.at[7],
            recv_sem=group_sem.at[group],
            device_id={"mem": other},
            device_id_type=MESH,
        ).start()
    ready("wdown")

    down = jnp.zeros((rows, wdown.shape[1]), F32)
    for k in (0, 1, 3, 2):
        source = lax.rem(group + k, GROUPS)
        arriving = GROUPS - 1 if k == 0 else GROUPS
        wait_bytes(r7.at[pl.ds(0, arriving)], group_sem.at[source])
        for q in range(GROUPS):
            line = k * tall + q * short
            g7[line : line + short, :] = r7[q * GROUPS + source].astype(F32)
        piece = jnp.concatenate(
            [
                g7[pl.ds(k * tall + c, rows, stride=LINES), :].astype(BF16)
                for c in range(chunks)
            ],
            axis=1,
        )
        down = down + jnp.dot(
            piece,
            wdown[pl.ds(pl.multiple_of(source * span, LANES), span), :],
            preferred_element_type=F32,
        )
    out_ref[...] = (after_f + sum_peers(8, down, s7b, r7b, s7c, r7c)).astype(BF16)

    wait_bytes(r1.at[pl.ds(0, members - 1), pl.ds(0, used)], send_sem.at[0])
    wait_bytes(r2.at[pl.ds(0, members - 1)], send_sem.at[1])
    wait_bytes(r4.at[pl.ds(0, (members - 1) * sent)], send_sem.at[2])
    wait_bytes(r5.at[pl.ds(0, (members - 1) * HEADS)], send_sem.at[3])
    for phase, landed, paired in ((4, r5b, r5c), (8, r7b, r7c)):
        wait_bytes(landed.at[pl.ds(0, ring - 1)], send_sem.at[phase])
        wait_bytes(paired, send_sem.at[phase + 1])
    for phase, landed in ((6, r6), (7, r7)):
        wait_bytes(landed.at[pl.ds(0, members - 1)], send_sem.at[phase])


def local(
    members,
    peers,
    tokens,
    attn_gain,
    query_key_value_weight,
    paged_key_store,
    paged_value_store,
    lengths,
    block_table,
    out_weight,
    mlp_gain,
    gate_weight,
    up_weight,
    down_weight,
):
    rows, width_part = tokens.shape
    slots, _, block_len, head_dim = paged_key_store.shape
    short = rows * LINES // GROUPS
    exponents = np.arange(head_dim // 2, dtype=np.float32) * np.float32(
        -2.0 * math.log(ROPE_BASE) / head_dim
    )
    inverse = np.exp(exponents.astype(np.float64)).astype(np.float32)
    freq = jnp.asarray(np.concatenate([inverse, inverse])[None, :])

    any_spec = pl.BlockSpec(memory_space=pl.ANY)
    vmem_spec = pl.BlockSpec(memory_space=pltpu.VMEM)
    scratch = [
        pltpu.SMEM(lengths.shape, jnp.int32),
        pltpu.VMEM(tokens.shape, BF16),
        pltpu.VMEM(attn_gain.shape, BF16),
        pltpu.VMEM(mlp_gain.shape, BF16),
        pltpu.VMEM(freq.shape, F32),
        pltpu.VMEM(block_table.shape, jnp.int32),
        pltpu.VMEM(query_key_value_weight.shape, BF16),
        pltpu.VMEM((slots, block_len, head_dim), BF16),
        pltpu.VMEM((slots, block_len, head_dim), BF16),
        pltpu.VMEM(out_weight.shape, BF16),
        pltpu.VMEM(gate_weight.shape, BF16),
        pltpu.VMEM(up_weight.shape, BF16),
        pltpu.VMEM(down_weight.shape, BF16),
        pltpu.VMEM((REQUESTS, GROUP, head_dim), BF16),
        pltpu.VMEM((8, slots), jnp.int32),
        pltpu.SMEM((8, slots), jnp.int32),
        pltpu.VMEM((REQUESTS, GROUP, LANES), F32),
        pltpu.VMEM((slots, GROUP, LANES), F32),
        pltpu.VMEM((rows * rows, LANES), F32),
        pltpu.VMEM((members, rows, LANES), F32),
        pltpu.VMEM((16, LANES), BF16),
        pltpu.VMEM((members, 16, LANES), BF16),
        pltpu.VMEM((members * PARTIAL, LANES), F32),
        pltpu.VMEM((members * PARTIAL, LANES), F32),
        pltpu.VMEM((HEADS, LANES), F32),
        pltpu.VMEM((members * HEADS, LANES), F32),
        pltpu.VMEM((rows, width_part + LANES), jnp.int16),
        pltpu.VMEM((peers // 2, rows, width_part + LANES), jnp.int16),
        pltpu.VMEM((rows, width_part), F32),
        pltpu.VMEM((rows, width_part), F32),
        pltpu.VMEM((2 * GROUPS * rows * LINES, LANES), F32),
        pltpu.VMEM((GROUPS, GROUPS, 2 * short, LANES), jnp.int16),
        pltpu.VMEM((members, 2 * short, LANES), jnp.int16),
        pltpu.VMEM((short, LANES), BF16),
        pltpu.VMEM((members, short, LANES), BF16),
        pltpu.VMEM((GROUPS * rows * LINES, LANES), F32),
        pltpu.VMEM((rows, width_part + LANES), jnp.int16),
        pltpu.VMEM((peers // 2, rows, width_part + LANES), jnp.int16),
        pltpu.VMEM((rows, width_part), F32),
        pltpu.VMEM((rows, width_part), F32),
        pltpu.SemaphoreType.DMA,
        pltpu.SemaphoreType.DMA((6 + 6 * PIECES + 2,)),
        pltpu.SemaphoreType.DMA((10,)),
        pltpu.SemaphoreType.DMA((10,)),
        pltpu.SemaphoreType.DMA((GROUPS,)),
        pltpu.SemaphoreType.DMA((GROUPS,)),
    ]
    return pl.pallas_call(
        functools.partial(kernel, members, peers, width_part * members),
        out_shape=jax.ShapeDtypeStruct(tokens.shape, BF16),
        in_specs=[any_spec] * 13,
        out_specs=vmem_spec,
        scratch_shapes=scratch,
        compiler_params=pltpu.CompilerParams(
            collective_id=0, has_side_effects=True, vmem_limit_bytes=56 * 1024 * 1024
        ),
        name="decoder_layer",
    )(
        lengths,
        tokens,
        attn_gain,
        mlp_gain,
        freq,
        block_table,
        query_key_value_weight,
        paged_key_store,
        paged_value_store,
        out_weight,
        gate_weight,
        up_weight,
        down_weight,
    )


def solution(mesh):
    return jax.shard_map(
        functools.partial(local, mesh.shape["mem"], mesh.shape["mp"]),
        mesh=mesh,
        in_specs=(
            P(None, "mem"),
            P("mem"),
            P("mem", "mp"),
            P("mem", "mp", None, None),
            P("mem", "mp", None, None),
            P(),
            P(),
            P("mp", "mem"),
            P("mem"),
            P("mem", "mp"),
            P("mem", "mp"),
            P("mp", "mem"),
        ),
        out_specs=P(None, "mem"),
        check_vma=False,
    )
```

```python
import functools
import math

import jax
import jax.numpy as jnp
import numpy as np
from jax import lax
from jax.experimental import pallas as pl
from jax.experimental.pallas import tpu as pltpu
from jax.sharding import PartitionSpec as P

MESH = pl.DeviceIdType.MESH
F32 = jnp.float32
BF16 = jnp.bfloat16

EPSILON = 1e-05
ROPE_BASE = 500000.0
FLOOR_SCORE = -1e30
LANES = 128
HEADS = 8
NEW = 4
REQUESTS = 4
GROUP = NEW * HEADS
OWNER = 256
RUN = 4
TILE = 9
PARTIAL = 16
GROUPS = 4
LINES = 8
PIECES = 4

HALF_PI = (1.5703125, 0.000484466552734375, -6.397578377557687e-07)


def sine_cosine(angle):
    turns = jnp.floor(angle * (2.0 / math.pi) + 0.5)
    r = ((angle - turns * HALF_PI[0]) - turns * HALF_PI[1]) - turns * HALF_PI[2]
    z = r * r
    sine = r + r * z * (-1.6666654611e-1 + z * (8.3321608736e-3 + z * (-1.9515295891e-4)))
    cosine = 1.0 - 0.5 * z + z * z * (
        4.166664568298827e-2 + z * (-1.388731625493765e-3 + z * 2.443315711809948e-5)
    )
    quadrant = turns - 4.0 * jnp.floor(turns * 0.25)
    odd = (quadrant == 1.0) | (quadrant == 3.0)
    s, c = jnp.where(odd, cosine, sine), jnp.where(odd, sine, cosine)
    s = jnp.where(quadrant >= 2.0, -s, s)
    c = jnp.where((quadrant == 1.0) | (quadrant == 2.0), -c, c)
    return s, c


STEPS = 32000.0
FINE = 256.0


def code_of(value):
    return jnp.log(jnp.maximum(value, 1e-30)) * (FINE / math.log(2.0))


def value_of(code):
    return jnp.exp2(code * (1.0 / FINE))


def kernel(
    members,
    peers,
    model_width,
    lengths_hbm,
    tokens_hbm,
    gain_one_hbm,
    gain_two_hbm,
    freq_hbm,
    table_hbm,
    wqkv_hbm,
    keys_hbm,
    values_hbm,
    wout_hbm,
    wgate_hbm,
    wup_hbm,
    wdown_hbm,
    out_ref,
    lengths,
    tokens,
    gain_one,
    gain_two,
    freq,
    table,
    wqkv,
    keys,
    values,
    wout,
    wgate,
    wup,
    wdown,
    queries,
    codes,
    slot_codes,
    tops_ref,
    scores,
    s1,
    r1,
    s2,
    r2,
    s4,
    r4,
    s5,
    r5,
    s5b,
    r5b,
    g6,
    s6,
    r6,
    s7,
    r7,
    g7,
    s7b,
    r7b,
    code_sem,
    fetch_sem,
    send_sem,
    recv_sem,
    quarter_sem,
    group_sem,
):
    me = lax.axis_index("mem")
    mine = lax.axis_index("mp")
    rows = tokens.shape[0]
    slots = keys.shape[0]
    block_len = keys.shape[1]

    side = math.isqrt(members)
    z, x = me // side, lax.rem(me, side)
    steps_of = lambda d, n: min(d, n - d)
    offsets = sorted(
        ((dz, dx) for dz in range(side) for dx in range(side) if dz or dx),
        key=lambda d: -steps_of(d[0], side) - steps_of(d[1], side),
    )
    member_order = [lax.rem(z + dz, side) * side + lax.rem(x + dx, side) for dz, dx in offsets]
    ring, cores = peers // 2, 2
    y, core = mine // cores, lax.rem(mine, cores)
    offsets = sorted(
        ((dy, dc) for dy in range(ring) for dc in range(cores) if dy or dc),
        key=lambda d: -steps_of(d[0], ring),
    )
    peer_order = [lax.rem(y + dy, ring) * cores + lax.rem(core + dc, cores) for dy, dc in offsets]

    fetched = {}

    def fetch(name, source, target, pieces=1):
        size = target.shape[0] // pieces
        fetched[name] = []
        for p in range(pieces):
            index = sum(len(v) for v in fetched.values())
            if pieces > 1:
                part = pl.ds(p * size, size)
                copy = pltpu.make_async_copy(source.at[part], target.at[part], fetch_sem.at[index])
            else:
                copy = pltpu.make_async_copy(source, target, fetch_sem.at[index])
            copy.start()
            fetched[name].append(copy)

    def ready(*names):
        for name in names:
            for copy in fetched[name]:
                copy.wait()

    fetch("tokens", tokens_hbm, tokens)
    fetch("gain_one", gain_one_hbm, gain_one)
    fetch("wqkv", wqkv_hbm, wqkv, PIECES)

    barrier = pltpu.get_barrier_semaphore()
    for other in member_order:
        pl.semaphore_signal(barrier, inc=1, device_id={"mem": other}, device_id_type=MESH)
    for other in peer_order:
        pl.semaphore_signal(barrier, inc=1, device_id={"mp": other}, device_id_type=MESH)

    fetch("lengths", lengths_hbm, lengths)
    fetch("freq", freq_hbm, freq)
    fetch("table", table_hbm, table)
    fetch("gain_two", gain_two_hbm, gain_two)

    def send_members(phase, source_of, target):
        for other in member_order:
            pltpu.make_async_remote_copy(
                src_ref=source_of(other),
                dst_ref=target,
                send_sem=send_sem.at[phase],
                recv_sem=recv_sem.at[phase],
                device_id={"mem": other},
                device_id_type=MESH,
            ).start()

    def send_peers(phase, source, target):
        for other in peer_order:
            pltpu.make_async_remote_copy(
                src_ref=source,
                dst_ref=target,
                send_sem=send_sem.at[phase],
                recv_sem=recv_sem.at[phase],
                device_id={"mp": other},
                device_id_type=MESH,
            ).start()

    width = tokens.shape[1]

    def sum_peers(phase, partial, staged, landed):
        unit_code = jnp.ceil(code_of(jnp.max(jnp.abs(partial), axis=1, keepdims=True)))
        steps = jnp.floor(partial * (STEPS / value_of(unit_code)) + 0.5)
        staged[:, :width] = steps.astype(jnp.int32).astype(jnp.int16)
        staged[:, width:] = (
            jnp.broadcast_to(unit_code, (rows, LANES)).astype(jnp.int32).astype(jnp.int16)
        )
        send_peers(phase, staged, landed.at[mine])
        landed[mine] = staged[...]
        wait_bytes(landed.at[pl.ds(0, peers - 1)], recv_sem.at[phase])
        total = jnp.zeros((rows, width), F32)
        for j in range(peers):
            part = landed[j].astype(jnp.int32).astype(F32)
            unit = value_of(part[:, width:]) * (1.0 / STEPS)
            total = total + part[:, :width] * jnp.concatenate([unit] * (width // LANES), axis=1)
        return total

    def wait_bytes(window, semaphore):
        pltpu.make_async_copy(window, window, semaphore).wait()

    ready("tokens", "gain_one")
    token_f = tokens[...].astype(F32)
    scaled_in = (token_f * gain_one[...].astype(F32)[None, :]).astype(BF16)
    square_one = jnp.sum(token_f * token_f, axis=1, keepdims=True)
    ready("wqkv")
    projected = jnp.dot(scaled_in, wqkv[...], preferred_element_type=F32)
    for c in range(HEADS + 2):
        s1[pl.ds(c, rows, stride=rows), :] = projected[:, c * LANES : (c + 1) * LANES]
    s1[pl.ds(HEADS + 2, rows, stride=rows), :] = jnp.broadcast_to(square_one, (rows, LANES))

    pl.semaphore_wait(barrier, members - 1 + peers - 1)

    used = HEADS + 3
    send_members(
        0, lambda other: s1.at[pl.ds(other * rows, used)], r1.at[me, pl.ds(0, used)]
    )
    r1[me] = s1[pl.ds(pl.multiple_of(me * rows, rows), rows), :]

    fetch("keys", keys_hbm.at[:, 0], keys, PIECES)
    fetch("values", values_hbm.at[:, 0], values, PIECES)

    request, place = me // NEW, lax.rem(me, NEW)
    ready("lengths", "freq")
    position = (lengths[request] + place).astype(F32)
    sine, cosine = sine_cosine(position * freq[...])
    lane_row = lax.broadcasted_iota(jnp.int32, (1, LANES), 1)
    sine = jnp.where(lane_row < LANES // 2, -sine, sine)

    wait_bytes(r1.at[pl.ds(0, members - 1), pl.ds(0, used)], recv_sem.at[0])
    total = r1[0]
    for j in range(1, members):
        total = total + r1[j]
    inverse_one = 1.0 / jnp.sqrt(total[HEADS + 2 : HEADS + 3, :] / model_width + EPSILON)
    total = total * inverse_one
    turned = total * cosine + pltpu.roll(total, LANES // 2, 1) * sine
    head_row = lax.broadcasted_iota(jnp.int32, total.shape, 0)
    s2[...] = jnp.where(head_row <= HEADS, turned, total).astype(BF16)
    r2[me] = s2[...]
    send_members(1, lambda other: s2, r2.at[me])
    fetch("wout", wout_hbm, wout, 2)
    fetch("wgate", wgate_hbm, wgate, PIECES)
    fetch("wup", wup_hbm, wup, PIECES)
    fetch("wdown", wdown_hbm, wdown, PIECES)

    ready("table")
    first_slot = me * slots
    max_blocks = table.shape[1]
    block_start = lax.broadcasted_iota(jnp.int32, (1, max_blocks), 1) * block_len
    slot_ids = first_slot + lax.broadcasted_iota(jnp.int32, (slots, max_blocks), 0)
    code = jnp.zeros((slots, max_blocks), jnp.int32)
    for r in range(REQUESTS):
        held = jnp.clip(lengths[r] - block_start, 0, block_len)
        held = jnp.where(held > 0, held + r * OWNER, 0)
        code = code + jnp.where(table[r : r + 1, :] == slot_ids, held, 0)
    code = jnp.sum(code, axis=1, keepdims=True)
    sub = lax.broadcasted_iota(jnp.int32, (slots, slots), 0)
    lane = lax.broadcasted_iota(jnp.int32, (slots, slots), 1)
    code_line = jnp.sum(jnp.where(sub == lane, code, 0), axis=0, keepdims=True)
    owner_column = jnp.where(code > 0, code >> 8, REQUESTS)
    owner_line = jnp.where(code_line > 0, code_line >> 8, REQUESTS)
    ahead = jnp.where((owner_line == owner_column) & (lane < sub), 1, 0)
    place_column = jnp.sum(ahead, axis=1, keepdims=True)
    positions = codes.shape[1]
    run_ids = lax.broadcasted_iota(jnp.int32, (1, positions), 1) * RUN
    run_owner = jnp.zeros((1, positions), jnp.int32)
    start = jnp.zeros((1, 1), jnp.int32)
    for r in range(REQUESTS):
        if r > 0:
            run_owner = run_owner + jnp.where(run_ids >= start, 1, 0)
        place_column = place_column + jnp.where(owner_column == r, start, 0)
        number = jnp.sum(jnp.where(owner_line == r, 1, 0), axis=1, keepdims=True)
        start = start + ((number + (RUN - 1)) & -RUN)
    place_column = jnp.where(code > 0, place_column, -1)
    position_ids = lax.broadcasted_iota(jnp.int32, (slots, positions), 1)
    entry = lax.broadcasted_iota(jnp.int32, (slots, positions), 0) * OWNER + (code & (OWNER - 1))
    entry = jnp.where(position_ids == place_column, entry, 0)
    codes[0:1, :] = jnp.sum(entry, axis=0, keepdims=True)
    codes[1:2, :] = run_owner
    owner_row = run_owner[:, :LANES]
    to_scalars = pltpu.make_async_copy(codes, slot_codes, code_sem)
    to_scalars.start()

    wait_bytes(r2.at[pl.ds(0, members - 1)], recv_sem.at[1])

    for r in range(REQUESTS):
        queries[r] = jnp.concatenate(
            [r2[r * NEW + t].astype(F32)[:HEADS] for t in range(NEW)], axis=0
        ).astype(BF16)
    factor = math.log2(math.e) / math.sqrt(LANES)
    lane_group = lax.broadcasted_iota(jnp.int32, (GROUP, LANES), 1)
    to_scalars.wait()
    ready("keys")

    def run_of(run):
        entries = [slot_codes[0, run * RUN + i] for i in range(RUN)]
        return slot_codes[1, run], [(e >> 8, e & (OWNER - 1)) for e in entries]

    def score_step(step, best):
        for j in range(TILE):
            run = step * TILE + j
            owner, members_of = run_of(run)
            score = lax.dot_general(
                queries[owner],
                jnp.concatenate([keys[slot] for slot, _ in members_of], axis=0),
                (((1,), (1,)), ((), ())),
                preferred_element_type=F32,
            )
            tops = []
            for i, (_, count) in enumerate(members_of):
                part = slice(i * LANES, (i + 1) * LANES)
                tops.append(jnp.where(lane_group < count, score[:, part], FLOOR_SCORE))
                scores[run, :, part] = tops[-1]
            top = jnp.max(functools.reduce(jnp.maximum, tops), axis=1, keepdims=True)
            best = jnp.where(lane_group == run, top, best)
        return best

    floor = jnp.full((GROUP, LANES), FLOOR_SCORE, F32)
    runs = scores.shape[0]
    run_best = lax.fori_loop(0, runs // TILE, score_step, floor)
    best = []
    for r in range(REQUESTS):
        own = jnp.where(owner_row == r, run_best, FLOOR_SCORE)
        best.append(jnp.broadcast_to(jnp.max(own, axis=1, keepdims=True), (GROUP, LANES)))
        tops_ref[r] = best[r]
    ready("values")

    def value_step(step, carry):
        sums, mixed = carry[0], list(carry[1])
        for j in range(TILE):
            run = step * TILE + j
            owner, members_of = run_of(run)
            top = tops_ref[owner]
            weights, highs, lows = [], [], []
            for i in range(RUN):
                weight = jnp.exp2((scores[run, :, i * LANES : (i + 1) * LANES] - top) * factor)
                weights.append(weight)
                highs.append(weight.astype(BF16))
                lows.append((weight - highs[-1].astype(F32)).astype(BF16))
            total = jnp.sum(functools.reduce(jnp.add, weights), axis=1, keepdims=True)
            sums = jnp.where(lane_group == run, total, sums)
            both = jnp.dot(
                jnp.concatenate(
                    [jnp.concatenate(highs, axis=1), jnp.concatenate(lows, axis=1)], axis=0
                ),
                jnp.concatenate([values[slot] for slot, _ in members_of], axis=0),
                preferred_element_type=F32,
            )
            both = both[:GROUP] + both[GROUP:]
            for r in range(REQUESTS):
                mixed[r] = mixed[r] + jnp.where(owner == r, both, 0.0)
        return sums, tuple(mixed)

    zero = jnp.zeros((GROUP, LANES), F32)
    run_sums, mixed = lax.fori_loop(0, runs // TILE, value_step, (zero, (zero,) * REQUESTS))
    lane_head = lax.broadcasted_iota(jnp.int32, (HEADS, LANES), 1) // (LANES // HEADS)
    by_head = lane_head == lax.broadcasted_iota(jnp.int32, (HEADS, LANES), 0)

    def to_line(column):
        return jnp.sum(jnp.where(by_head, column, 0.0), axis=0, keepdims=True)

    def to_column(line):
        column = jnp.max(jnp.where(by_head, line, -jnp.inf), axis=1, keepdims=True)
        return jnp.broadcast_to(column, (HEADS, LANES))

    for r in range(REQUESTS):
        own = jnp.where(owner_row == r, run_sums, 0.0)
        whole = jnp.broadcast_to(jnp.sum(own, axis=1, keepdims=True), (GROUP, LANES))
        for t in range(NEW):
            part = slice(t * HEADS, (t + 1) * HEADS)
            line = (r * NEW + t) * PARTIAL
            s4[line : line + HEADS, :] = mixed[r][part]
            s4[line + HEADS : line + HEADS + 1, :] = to_line(best[r][part])
            s4[line + HEADS + 1 : line + HEADS + 2, :] = to_line(whole[part])
    mine_4 = pl.ds(pl.multiple_of(me * PARTIAL, PARTIAL), PARTIAL)
    sent = HEADS + 2
    send_members(
        2,
        lambda other: s4.at[pl.ds(other * PARTIAL, sent)],
        r4.at[pl.ds(me * PARTIAL, sent)],
    )
    r4[mine_4, :] = s4[mine_4, :]

    row_queries = r2[me].astype(F32)[:HEADS]
    own_scores, own_values = [], []
    for t in range(NEW):
        fresh = r2[request * NEW + t].astype(F32)
        score = jnp.sum(row_queries * fresh[HEADS : HEADS + 1], axis=1, keepdims=True)
        score = jnp.broadcast_to(score, (HEADS, LANES))
        own_scores.append(jnp.where(t <= place, score, FLOOR_SCORE))
        own_values.append(fresh[HEADS + 1 : HEADS + 2])
    top = to_line(functools.reduce(jnp.maximum, own_scores))

    wait_bytes(r4.at[pl.ds(0, (members - 1) * sent)], recv_sem.at[2])
    tops = r4[pl.ds(HEADS, members, stride=PARTIAL), :]
    wholes = r4[pl.ds(HEADS + 1, members, stride=PARTIAL), :]
    top = jnp.maximum(top, jnp.max(tops, axis=0, keepdims=True))
    shrink = jnp.exp2((tops - top) * factor)
    whole = to_column(jnp.sum(wholes * shrink, axis=0, keepdims=True))
    top = to_column(top)
    mix = jnp.zeros((HEADS, LANES), F32)
    for t in range(NEW):
        weight = jnp.exp2((own_scores[t] - top) * factor)
        whole = whole + weight
        mix = mix + weight * own_values[t]
    for j in range(members):
        mix = mix + r4[j * PARTIAL : j * PARTIAL + HEADS, :] * to_column(shrink[j : j + 1])
    s5[...] = mix / whole
    own_rows = pl.ds(pl.multiple_of(me * HEADS, HEADS), HEADS)
    r5[own_rows, :] = s5[...]
    send_members(3, lambda other: s5, r5.at[own_rows])
    ready("wout")
    wait_bytes(r5.at[pl.ds(0, (members - 1) * HEADS)], recv_sem.at[3])

    attended = jnp.concatenate(
        [r5[pl.ds(h, rows, stride=HEADS), :].astype(BF16) for h in range(HEADS)], axis=1
    )
    partial = jnp.dot(attended, wout[...], preferred_element_type=F32)
    after_f = (token_f + sum_peers(4, partial, s5b, r5b)).astype(BF16).astype(F32)
    ready("gain_two", "wgate", "wup")

    scaled_mid = (after_f * gain_two[...].astype(F32)[None, :]).astype(BF16)
    square_mid = jnp.sum(after_f * after_f, axis=1, keepdims=True)
    square_code = code_of(square_mid)
    square_whole = jnp.floor(square_code)
    square_rest = jnp.floor((square_code - square_whole) * STEPS + 0.5)
    lane_rows = lax.broadcasted_iota(jnp.int32, (rows, LANES), 1)
    square_line = jnp.where(lane_rows < LANES // 2, square_whole, square_rest)

    quarter, group = me // GROUPS, lax.rem(me, GROUPS)
    span = wgate.shape[1] // GROUPS
    chunks = span // LANES
    tall = rows * LINES
    short = tall // GROUPS

    def multiply(k):
        columns = pl.ds(pl.multiple_of(lax.rem(group + k, GROUPS) * span, LANES), span)
        return [
            jnp.dot(scaled_mid, weight[:, columns], preferred_element_type=F32)
            for weight in (wgate, wup)
        ]

    def ship(k, parts):
        target = lax.rem(group + k, GROUPS)
        largest = jnp.maximum(jnp.abs(parts[0]), jnp.abs(parts[1]))
        unit_code = jnp.ceil(code_of(jnp.max(largest, axis=1, keepdims=True)))
        to_steps = STEPS / value_of(unit_code)
        unit_line = jnp.broadcast_to(unit_code, (rows, LANES))
        for index, (part, extra) in enumerate(zip(parts, (unit_line, square_line))):
            base = (2 * k + index) * tall
            steps = jnp.floor(part * to_steps + 0.5)
            for c in range(chunks):
                g6[pl.ds(base + c, rows, stride=LINES), :] = steps[:, c * LANES : (c + 1) * LANES]
            g6[pl.ds(base + chunks, rows, stride=LINES), :] = extra
            for q in range(GROUPS):
                piece = g6[base + q * short : base + (q + 1) * short, :]
                s6[k, q, index * short : (index + 1) * short, :] = piece.astype(jnp.int32).astype(
                    jnp.int16
                )
        for j in (2, 1, 3, 0) if k else (2, 1, 3):
            other = lax.rem(quarter + j, GROUPS)
            pltpu.make_async_remote_copy(
                src_ref=s6.at[k, other],
                dst_ref=r6.at[me],
                send_sem=send_sem.at[5],
                recv_sem=quarter_sem.at[k],
                device_id={"mem": other * GROUPS + target},
                device_id_type=MESH,
            ).start()

    order = (2, 1, 3, 0)
    parts = multiply(order[0])
    for index, k in enumerate(order):
        later = multiply(order[index + 1]) if index + 1 < GROUPS else None
        ship(k, parts)
        parts = later
    r6[me] = s6[0, quarter]

    gates = [jnp.zeros((LINES, LANES), F32)] * GROUPS
    ups = [jnp.zeros((LINES, LANES), F32)] * GROUPS
    square = jnp.zeros((GROUPS, LANES), F32)
    lane_codes = lax.broadcasted_iota(jnp.int32, (GROUPS, LANES), 1)
    for k, q in [(k, q) for k in order for q in range(GROUPS)]:
        if q == 0:
            arriving = GROUPS if k else GROUPS - 1
            wait_bytes(r6.at[pl.ds(0, arriving)], quarter_sem.at[k])
        sender = q * GROUPS + lax.rem(group + GROUPS - k, GROUPS)
        part = r6[sender].astype(jnp.int32).astype(F32)
        units, squares = (
            jnp.concatenate(
                [
                    part[start + r * LINES + chunks : start + r * LINES + chunks + 1]
                    for r in range(GROUPS)
                ],
                axis=0,
            )
            for start in (0, short)
        )
        units = value_of(units) * (1.0 / STEPS)
        squares = jnp.where(lane_codes < LANES // 2, squares, squares * (1.0 / STEPS))
        square = square + value_of(squares + pltpu.roll(squares, LANES // 2, 1))
        for r in range(GROUPS):
            own = slice(r * LINES, (r + 1) * LINES)
            gates[r] = gates[r] + part[:short][own] * units[r : r + 1]
            ups[r] = ups[r] + part[short:][own] * units[r : r + 1]
    inverse_two = 1.0 / jnp.sqrt(square / model_width + EPSILON)
    hidden = []
    for r in range(GROUPS):
        gate = gates[r] * inverse_two[r : r + 1]
        hidden.append(gate / (1.0 + jnp.exp(-gate)) * (ups[r] * inverse_two[r : r + 1]))
    s7[...] = jnp.concatenate(hidden, axis=0).astype(BF16)
    r7[me] = s7[...]
    for other in member_order:
        pltpu.make_async_remote_copy(
            src_ref=s7,
            dst_ref=r7.at[me],
            send_sem=send_sem.at[6],
            recv_sem=group_sem.at[group],
            device_id={"mem": other},
            device_id_type=MESH,
        ).start()
    ready("wdown")

    down = jnp.zeros((rows, wdown.shape[1]), F32)
    for k in (0, 1, 3, 2):
        source = lax.rem(group + k, GROUPS)
        arriving = GROUPS - 1 if k == 0 else GROUPS
        wait_bytes(r7.at[pl.ds(0, arriving)], group_sem.at[source])
        for q in range(GROUPS):
            line = k * tall + q * short
            g7[line : line + short, :] = r7[q * GROUPS + source].astype(F32)
        piece = jnp.concatenate(
            [
                g7[pl.ds(k * tall + c, rows, stride=LINES), :].astype(BF16)
                for c in range(chunks)
            ],
            axis=1,
        )
        down = down + jnp.dot(
            piece,
            wdown[pl.ds(pl.multiple_of(source * span, LANES), span), :],
            preferred_element_type=F32,
        )
    out_ref[...] = (after_f + sum_peers(7, down, s7b, r7b)).astype(BF16)

    wait_bytes(r1.at[pl.ds(0, members - 1), pl.ds(0, used)], send_sem.at[0])
    wait_bytes(r2.at[pl.ds(0, members - 1)], send_sem.at[1])
    wait_bytes(r4.at[pl.ds(0, (members - 1) * sent)], send_sem.at[2])
    wait_bytes(r5.at[pl.ds(0, (members - 1) * HEADS)], send_sem.at[3])
    for phase, landed in ((4, r5b), (7, r7b)):
        wait_bytes(landed.at[pl.ds(0, peers - 1)], send_sem.at[phase])
    for phase, landed in ((5, r6), (6, r7)):
        wait_bytes(landed.at[pl.ds(0, members - 1)], send_sem.at[phase])


def local(
    members,
    peers,
    tokens,
    attn_gain,
    query_key_value_weight,
    paged_key_store,
    paged_value_store,
    lengths,
    block_table,
    out_weight,
    mlp_gain,
    gate_weight,
    up_weight,
    down_weight,
):
    rows, width_part = tokens.shape
    slots, _, block_len, head_dim = paged_key_store.shape
    short = rows * LINES // GROUPS
    runs = slots // RUN + REQUESTS
    exponents = np.arange(head_dim // 2, dtype=np.float32) * np.float32(
        -2.0 * math.log(ROPE_BASE) / head_dim
    )
    inverse = np.exp(exponents.astype(np.float64)).astype(np.float32)
    freq = jnp.asarray(np.concatenate([inverse, inverse])[None, :])

    any_spec = pl.BlockSpec(memory_space=pl.ANY)
    vmem_spec = pl.BlockSpec(memory_space=pltpu.VMEM)
    scratch = [
        pltpu.SMEM(lengths.shape, jnp.int32),
        pltpu.VMEM(tokens.shape, BF16),
        pltpu.VMEM(attn_gain.shape, BF16),
        pltpu.VMEM(mlp_gain.shape, BF16),
        pltpu.VMEM(freq.shape, F32),
        pltpu.VMEM(block_table.shape, jnp.int32),
        pltpu.VMEM(query_key_value_weight.shape, BF16),
        pltpu.VMEM((slots, block_len, head_dim), BF16),
        pltpu.VMEM((slots, block_len, head_dim), BF16),
        pltpu.VMEM(out_weight.shape, BF16),
        pltpu.VMEM(gate_weight.shape, BF16),
        pltpu.VMEM(up_weight.shape, BF16),
        pltpu.VMEM(down_weight.shape, BF16),
        pltpu.VMEM((REQUESTS, GROUP, head_dim), BF16),
        pltpu.VMEM((8, 2 * LANES), jnp.int32),
        pltpu.SMEM((8, 2 * LANES), jnp.int32),
        pltpu.VMEM((REQUESTS, GROUP, LANES), F32),
        pltpu.VMEM((runs, GROUP, RUN * LANES), F32),
        pltpu.VMEM((rows * rows, LANES), F32),
        pltpu.VMEM((members, rows, LANES), F32),
        pltpu.VMEM((16, LANES), BF16),
        pltpu.VMEM((members, 16, LANES), BF16),
        pltpu.VMEM((members * PARTIAL, LANES), F32),
        pltpu.VMEM((members * PARTIAL, LANES), F32),
        pltpu.VMEM((HEADS, LANES), F32),
        pltpu.VMEM((members * HEADS, LANES), F32),
        pltpu.VMEM((rows, width_part + LANES), jnp.int16),
        pltpu.VMEM((peers, rows, width_part + LANES), jnp.int16),
        pltpu.VMEM((2 * GROUPS * rows * LINES, LANES), F32),
        pltpu.VMEM((GROUPS, GROUPS, 2 * short, LANES), jnp.int16),
        pltpu.VMEM((members, 2 * short, LANES), jnp.int16),
        pltpu.VMEM((short, LANES), BF16),
        pltpu.VMEM((members, short, LANES), BF16),
        pltpu.VMEM((GROUPS * rows * LINES, LANES), F32),
        pltpu.VMEM((rows, width_part + LANES), jnp.int16),
        pltpu.VMEM((peers, rows, width_part + LANES), jnp.int16),
        pltpu.SemaphoreType.DMA,
        pltpu.SemaphoreType.DMA((6 + 6 * PIECES + 2,)),
        pltpu.SemaphoreType.DMA((8,)),
        pltpu.SemaphoreType.DMA((8,)),
        pltpu.SemaphoreType.DMA((GROUPS,)),
        pltpu.SemaphoreType.DMA((GROUPS,)),
    ]
    return pl.pallas_call(
        functools.partial(kernel, members, peers, width_part * members),
        out_shape=jax.ShapeDtypeStruct(tokens.shape, BF16),
        in_specs=[any_spec] * 13,
        out_specs=vmem_spec,
        scratch_shapes=scratch,
        compiler_params=pltpu.CompilerParams(
            collective_id=0, has_side_effects=True, vmem_limit_bytes=56 * 1024 * 1024
        ),
        name="decoder_layer",
    )(
        lengths,
        tokens,
        attn_gain,
        mlp_gain,
        freq,
        block_table,
        query_key_value_weight,
        paged_key_store,
        paged_value_store,
        out_weight,
        gate_weight,
        up_weight,
        down_weight,
    )


def solution(mesh):
    return jax.shard_map(
        functools.partial(local, mesh.shape["mem"], mesh.shape["mp"]),
        mesh=mesh,
        in_specs=(
            P(None, "mem"),
            P("mem"),
            P("mem", "mp"),
            P("mem", "mp", None, None),
            P("mem", "mp", None, None),
            P(),
            P(),
            P("mp", "mem"),
            P("mem"),
            P("mem", "mp"),
            P("mem", "mp"),
            P("mp", "mem"),
        ),
        out_specs=P(None, "mem"),
        check_vma=False,
    )
```

```python
import functools
import math

import jax
import jax.numpy as jnp
import numpy as np
from jax import lax
from jax.experimental import pallas as pl
from jax.experimental.pallas import tpu as pltpu
from jax.sharding import PartitionSpec as P

MESH = pl.DeviceIdType.MESH
F32 = jnp.float32
BF16 = jnp.bfloat16

EPSILON = 1e-05
ROPE_BASE = 500000.0
FLOOR_SCORE = -1e30
LANES = 128
HEADS = 8
NEW = 4
REQUESTS = 4
GROUP = NEW * HEADS
OWNER = 256
RUN = 4
TILE = 18
PARTIAL = 16
GROUPS = 4
LINES = 8
PIECES = 4

HALF_PI = (1.5703125, 0.000484466552734375, -6.397578377557687e-07)


def sine_cosine(angle):
    turns = jnp.floor(angle * (2.0 / math.pi) + 0.5)
    r = ((angle - turns * HALF_PI[0]) - turns * HALF_PI[1]) - turns * HALF_PI[2]
    z = r * r
    sine = r + r * z * (-1.6666654611e-1 + z * (8.3321608736e-3 + z * (-1.9515295891e-4)))
    cosine = 1.0 - 0.5 * z + z * z * (
        4.166664568298827e-2 + z * (-1.388731625493765e-3 + z * 2.443315711809948e-5)
    )
    quadrant = turns - 4.0 * jnp.floor(turns * 0.25)
    odd = (quadrant == 1.0) | (quadrant == 3.0)
    s, c = jnp.where(odd, cosine, sine), jnp.where(odd, sine, cosine)
    s = jnp.where(quadrant >= 2.0, -s, s)
    c = jnp.where((quadrant == 1.0) | (quadrant == 2.0), -c, c)
    return s, c


STEPS = 32000.0
FINE = 256.0


def code_of(value):
    return jnp.log(jnp.maximum(value, 1e-30)) * (FINE / math.log(2.0))


def value_of(code):
    return jnp.exp2(code * (1.0 / FINE))


def kernel(
    members,
    peers,
    model_width,
    lengths_hbm,
    tokens_hbm,
    gain_one_hbm,
    gain_two_hbm,
    freq_hbm,
    table_hbm,
    wqkv_hbm,
    keys_hbm,
    values_hbm,
    wout_hbm,
    wgate_hbm,
    wup_hbm,
    wdown_hbm,
    out_ref,
    lengths,
    tokens,
    gain_one,
    gain_two,
    freq,
    table,
    wqkv,
    keys,
    values,
    wout,
    wgate,
    wup,
    wdown,
    queries,
    codes,
    slot_codes,
    tops_ref,
    scores,
    s1,
    r1,
    s2,
    r2,
    s4,
    r4,
    s5,
    r5,
    s5b,
    r5b,
    g6,
    s6,
    r6,
    s7,
    r7,
    g7,
    s7b,
    r7b,
    code_sem,
    fetch_sem,
    send_sem,
    recv_sem,
    quarter_sem,
    group_sem,
):
    me = lax.axis_index("mem")
    mine = lax.axis_index("mp")
    rows = tokens.shape[0]
    slots = keys.shape[0]
    block_len = keys.shape[1]

    side = math.isqrt(members)
    z, x = me // side, lax.rem(me, side)
    steps_of = lambda d, n: min(d, n - d)
    offsets = sorted(
        ((dz, dx) for dz in range(side) for dx in range(side) if dz or dx),
        key=lambda d: -steps_of(d[0], side) - steps_of(d[1], side),
    )
    member_order = [lax.rem(z + dz, side) * side + lax.rem(x + dx, side) for dz, dx in offsets]
    ring, cores = peers // 2, 2
    y, core = mine // cores, lax.rem(mine, cores)
    offsets = sorted(
        ((dy, dc) for dy in range(ring) for dc in range(cores) if dy or dc),
        key=lambda d: -steps_of(d[0], ring),
    )
    peer_order = [lax.rem(y + dy, ring) * cores + lax.rem(core + dc, cores) for dy, dc in offsets]

    fetched = {}

    def fetch(name, source, target, pieces=1):
        size = target.shape[0] // pieces
        fetched[name] = []
        for p in range(pieces):
            index = sum(len(v) for v in fetched.values())
            if pieces > 1:
                part = pl.ds(p * size, size)
                copy = pltpu.make_async_copy(source.at[part], target.at[part], fetch_sem.at[index])
            else:
                copy = pltpu.make_async_copy(source, target, fetch_sem.at[index])
            copy.start()
            fetched[name].append(copy)

    def ready(*names):
        for name in names:
            for copy in fetched[name]:
                copy.wait()

    fetch("tokens", tokens_hbm, tokens)
    fetch("gain_one", gain_one_hbm, gain_one)
    fetch("wqkv", wqkv_hbm, wqkv, 2 * PIECES)
    fetch("lengths", lengths_hbm, lengths)
    fetch("freq", freq_hbm, freq)

    barrier = pltpu.get_barrier_semaphore()
    for other in member_order:
        pl.semaphore_signal(barrier, inc=1, device_id={"mem": other}, device_id_type=MESH)
    for other in peer_order:
        pl.semaphore_signal(barrier, inc=1, device_id={"mp": other}, device_id_type=MESH)

    fetch("table", table_hbm, table)
    fetch("gain_two", gain_two_hbm, gain_two)

    def send_members(phase, source_of, target):
        for other in member_order:
            pltpu.make_async_remote_copy(
                src_ref=source_of(other),
                dst_ref=target,
                send_sem=send_sem.at[phase],
                recv_sem=recv_sem.at[phase],
                device_id={"mem": other},
                device_id_type=MESH,
            ).start()

    def send_peers(phase, source, target):
        for other in peer_order:
            pltpu.make_async_remote_copy(
                src_ref=source,
                dst_ref=target,
                send_sem=send_sem.at[phase],
                recv_sem=recv_sem.at[phase],
                device_id={"mp": other},
                device_id_type=MESH,
            ).start()

    width = tokens.shape[1]

    def sum_peers(phase, partial, staged, landed):
        unit_code = jnp.ceil(code_of(jnp.max(jnp.abs(partial), axis=1, keepdims=True)))
        steps = jnp.floor(partial * (STEPS / value_of(unit_code)) + 0.5)
        staged[:, :width] = steps.astype(jnp.int32).astype(jnp.int16)
        staged[:, width:] = (
            jnp.broadcast_to(unit_code, (rows, LANES)).astype(jnp.int32).astype(jnp.int16)
        )
        send_peers(phase, staged, landed.at[mine])
        landed[mine] = staged[...]
        wait_bytes(landed.at[pl.ds(0, peers - 1)], recv_sem.at[phase])
        total = jnp.zeros((rows, width), F32)
        for j in range(peers):
            part = landed[j].astype(jnp.int32).astype(F32)
            unit = value_of(part[:, width:]) * (1.0 / STEPS)
            total = total + part[:, :width] * jnp.concatenate([unit] * (width // LANES), axis=1)
        return total

    def wait_bytes(window, semaphore):
        pltpu.make_async_copy(window, window, semaphore).wait()

    ready("tokens", "gain_one")
    token_f = tokens[...].astype(F32)
    scaled_in = (token_f * gain_one[...].astype(F32)[None, :]).astype(BF16)
    square_one = jnp.sum(token_f * token_f, axis=1, keepdims=True)
    request, place = me // NEW, lax.rem(me, NEW)
    ready("lengths", "freq")
    position = (lengths[request] + place).astype(F32)
    sine, cosine = sine_cosine(position * freq[...])
    lane_row = lax.broadcasted_iota(jnp.int32, (1, LANES), 1)
    sine = jnp.where(lane_row < LANES // 2, -sine, sine)
    ready("wqkv")
    projected = jnp.dot(scaled_in, wqkv[...], preferred_element_type=F32)
    for c in range(HEADS + 2):
        s1[pl.ds(c, rows, stride=rows), :] = projected[:, c * LANES : (c + 1) * LANES]
    s1[pl.ds(HEADS + 2, rows, stride=rows), :] = jnp.broadcast_to(square_one, (rows, LANES))

    pl.semaphore_wait(barrier, members - 1 + peers - 1)

    used = HEADS + 3
    send_members(
        0, lambda other: s1.at[pl.ds(other * rows, used)], r1.at[me, pl.ds(0, used)]
    )
    r1[me] = s1[pl.ds(pl.multiple_of(me * rows, rows), rows), :]

    fetch("keys", keys_hbm.at[:, 0], keys, PIECES)
    fetch("values", values_hbm.at[:, 0], values, PIECES)

    wait_bytes(r1.at[pl.ds(0, members - 1), pl.ds(0, used)], recv_sem.at[0])
    total = r1[0]
    for j in range(1, members):
        total = total + r1[j]
    inverse_one = 1.0 / jnp.sqrt(total[HEADS + 2 : HEADS + 3, :] / model_width + EPSILON)
    total = total * inverse_one
    turned = total * cosine + pltpu.roll(total, LANES // 2, 1) * sine
    head_row = lax.broadcasted_iota(jnp.int32, total.shape, 0)
    s2[...] = jnp.where(head_row <= HEADS, turned, total).astype(BF16)
    send_members(1, lambda other: s2, r2.at[me])
    r2[me] = s2[...]
    fetch("wout", wout_hbm, wout, 2)
    fetch("wgate", wgate_hbm, wgate, PIECES)
    fetch("wup", wup_hbm, wup, PIECES)
    fetch("wdown", wdown_hbm, wdown, PIECES)

    ready("table")
    first_slot = me * slots
    max_blocks = table.shape[1]
    block_start = lax.broadcasted_iota(jnp.int32, (1, max_blocks), 1) * block_len
    slot_ids = first_slot + lax.broadcasted_iota(jnp.int32, (slots, max_blocks), 0)
    code = jnp.zeros((slots, max_blocks), jnp.int32)
    for r in range(REQUESTS):
        held = jnp.clip(lengths[r] - block_start, 0, block_len)
        held = jnp.where(held > 0, held + r * OWNER, 0)
        code = code + jnp.where(table[r : r + 1, :] == slot_ids, held, 0)
    code = jnp.sum(code, axis=1, keepdims=True)
    sub = lax.broadcasted_iota(jnp.int32, (slots, slots), 0)
    lane = lax.broadcasted_iota(jnp.int32, (slots, slots), 1)
    code_line = jnp.sum(jnp.where(sub == lane, code, 0), axis=0, keepdims=True)
    owner_column = jnp.where(code > 0, code >> 8, REQUESTS)
    owner_line = jnp.where(code_line > 0, code_line >> 8, REQUESTS)
    ahead = jnp.where((owner_line == owner_column) & (lane < sub), 1, 0)
    place_column = jnp.sum(ahead, axis=1, keepdims=True)
    positions = codes.shape[1]
    run_ids = lax.broadcasted_iota(jnp.int32, (1, positions), 1) * RUN
    run_owner = jnp.zeros((1, positions), jnp.int32)
    start = jnp.zeros((1, 1), jnp.int32)
    for r in range(REQUESTS):
        if r > 0:
            run_owner = run_owner + jnp.where(run_ids >= start, 1, 0)
        place_column = place_column + jnp.where(owner_column == r, start, 0)
        number = jnp.sum(jnp.where(owner_line == r, 1, 0), axis=1, keepdims=True)
        start = start + ((number + (RUN - 1)) & -RUN)
    place_column = jnp.where(code > 0, place_column, -1)
    position_ids = lax.broadcasted_iota(jnp.int32, (slots, positions), 1)
    entry = lax.broadcasted_iota(jnp.int32, (slots, positions), 0) * OWNER + (code & (OWNER - 1))
    entry = jnp.where(position_ids == place_column, entry, 0)
    codes[0:1, :] = jnp.sum(entry, axis=0, keepdims=True)
    codes[1:2, :] = run_owner
    owner_row = run_owner[:, :LANES]
    to_scalars = pltpu.make_async_copy(codes, slot_codes, code_sem)
    to_scalars.start()

    wait_bytes(r2.at[pl.ds(0, members - 1)], recv_sem.at[1])

    for r in range(REQUESTS):
        queries[r] = jnp.concatenate(
            [r2[r * NEW + t].astype(F32)[:HEADS] for t in range(NEW)], axis=0
        ).astype(BF16)
    factor = math.log2(math.e) / math.sqrt(LANES)
    lane_group = lax.broadcasted_iota(jnp.int32, (GROUP, LANES), 1)
    to_scalars.wait()
    ready("keys")

    def run_of(run):
        entries = [slot_codes[0, run * RUN + i] for i in range(RUN)]
        return slot_codes[1, run], [(e >> 8, e & (OWNER - 1)) for e in entries]

    def score_step(step, best):
        for j in range(TILE):
            run = step * TILE + j
            owner, members_of = run_of(run)
            score = lax.dot_general(
                queries[owner],
                jnp.concatenate([keys[slot] for slot, _ in members_of], axis=0),
                (((1,), (1,)), ((), ())),
                preferred_element_type=F32,
            )
            tops = []
            for i, (_, count) in enumerate(members_of):
                part = slice(i * LANES, (i + 1) * LANES)
                tops.append(jnp.where(lane_group < count, score[:, part], FLOOR_SCORE))
                scores[run, :, part] = tops[-1]
            top = jnp.max(functools.reduce(jnp.maximum, tops), axis=1, keepdims=True)
            best = jnp.where(lane_group == run, top, best)
        return best

    floor = jnp.full((GROUP, LANES), FLOOR_SCORE, F32)
    runs = scores.shape[0]
    run_best = lax.fori_loop(0, runs // TILE, score_step, floor)
    best = []
    for r in range(REQUESTS):
        own = jnp.where(owner_row == r, run_best, FLOOR_SCORE)
        best.append(jnp.broadcast_to(jnp.max(own, axis=1, keepdims=True), (GROUP, LANES)))
        tops_ref[r] = best[r]
    ready("values")

    def value_step(step, carry):
        sums, mixed = carry[0], list(carry[1])
        for j in range(TILE):
            run = step * TILE + j
            owner, members_of = run_of(run)
            top = tops_ref[owner]
            weights, highs, lows = [], [], []
            for i in range(RUN):
                weight = jnp.exp2((scores[run, :, i * LANES : (i + 1) * LANES] - top) * factor)
                weights.append(weight)
                highs.append(weight.astype(BF16))
                lows.append((weight - highs[-1].astype(F32)).astype(BF16))
            total = jnp.sum(functools.reduce(jnp.add, weights), axis=1, keepdims=True)
            sums = jnp.where(lane_group == run, total, sums)
            both = jnp.dot(
                jnp.concatenate(
                    [jnp.concatenate(highs, axis=1), jnp.concatenate(lows, axis=1)], axis=0
                ),
                jnp.concatenate([values[slot] for slot, _ in members_of], axis=0),
                preferred_element_type=F32,
            )
            both = both[:GROUP] + both[GROUP:]
            for r in range(REQUESTS):
                mixed[r] = mixed[r] + jnp.where(owner == r, both, 0.0)
        return sums, tuple(mixed)

    zero = jnp.zeros((GROUP, LANES), F32)
    run_sums, mixed = lax.fori_loop(0, runs // TILE, value_step, (zero, (zero,) * REQUESTS))
    lane_head = lax.broadcasted_iota(jnp.int32, (HEADS, LANES), 1) // (LANES // HEADS)
    by_head = lane_head == lax.broadcasted_iota(jnp.int32, (HEADS, LANES), 0)

    def to_line(column):
        return jnp.sum(jnp.where(by_head, column, 0.0), axis=0, keepdims=True)

    def to_column(line):
        column = jnp.max(jnp.where(by_head, line, -jnp.inf), axis=1, keepdims=True)
        return jnp.broadcast_to(column, (HEADS, LANES))

    for r in range(REQUESTS):
        own = jnp.where(owner_row == r, run_sums, 0.0)
        whole = jnp.broadcast_to(jnp.sum(own, axis=1, keepdims=True), (GROUP, LANES))
        for t in range(NEW):
            part = slice(t * HEADS, (t + 1) * HEADS)
            line = (r * NEW + t) * PARTIAL
            s4[line : line + HEADS, :] = mixed[r][part]
            s4[line + HEADS : line + HEADS + 1, :] = to_line(best[r][part])
            s4[line + HEADS + 1 : line + HEADS + 2, :] = to_line(whole[part])
    mine_4 = pl.ds(pl.multiple_of(me * PARTIAL, PARTIAL), PARTIAL)
    sent = HEADS + 2
    send_members(
        2,
        lambda other: s4.at[pl.ds(other * PARTIAL, sent)],
        r4.at[pl.ds(me * PARTIAL, sent)],
    )
    r4[mine_4, :] = s4[mine_4, :]

    row_queries = r2[me].astype(F32)[:HEADS]
    own_scores, own_values = [], []
    for t in range(NEW):
        fresh = r2[request * NEW + t].astype(F32)
        score = jnp.sum(row_queries * fresh[HEADS : HEADS + 1], axis=1, keepdims=True)
        score = jnp.broadcast_to(score, (HEADS, LANES))
        own_scores.append(jnp.where(t <= place, score, FLOOR_SCORE))
        own_values.append(fresh[HEADS + 1 : HEADS + 2])
    top = to_line(functools.reduce(jnp.maximum, own_scores))

    wait_bytes(r4.at[pl.ds(0, (members - 1) * sent)], recv_sem.at[2])
    tops = r4[pl.ds(HEADS, members, stride=PARTIAL), :]
    wholes = r4[pl.ds(HEADS + 1, members, stride=PARTIAL), :]
    top = jnp.maximum(top, jnp.max(tops, axis=0, keepdims=True))
    shrink = jnp.exp2((tops - top) * factor)
    whole = to_column(jnp.sum(wholes * shrink, axis=0, keepdims=True))
    top = to_column(top)
    mix = jnp.zeros((HEADS, LANES), F32)
    for t in range(NEW):
        weight = jnp.exp2((own_scores[t] - top) * factor)
        whole = whole + weight
        mix = mix + weight * own_values[t]
    for j in range(members):
        mix = mix + r4[j * PARTIAL : j * PARTIAL + HEADS, :] * to_column(shrink[j : j + 1])
    s5[...] = mix / whole
    own_rows = pl.ds(pl.multiple_of(me * HEADS, HEADS), HEADS)
    send_members(3, lambda other: s5, r5.at[own_rows])
    r5[own_rows, :] = s5[...]
    ready("wout")
    wait_bytes(r5.at[pl.ds(0, (members - 1) * HEADS)], recv_sem.at[3])

    attended = jnp.concatenate(
        [r5[pl.ds(h, rows, stride=HEADS), :].astype(BF16) for h in range(HEADS)], axis=1
    )
    partial = jnp.dot(attended, wout[...], preferred_element_type=F32)
    after_f = (token_f + sum_peers(4, partial, s5b, r5b)).astype(BF16).astype(F32)
    ready("gain_two", "wgate", "wup")

    scaled_mid = (after_f * gain_two[...].astype(F32)[None, :]).astype(BF16)
    square_mid = jnp.sum(after_f * after_f, axis=1, keepdims=True)
    square_code = code_of(square_mid)
    square_whole = jnp.floor(square_code)
    square_rest = jnp.floor((square_code - square_whole) * STEPS + 0.5)
    lane_rows = lax.broadcasted_iota(jnp.int32, (rows, LANES), 1)
    square_line = jnp.where(lane_rows < LANES // 2, square_whole, square_rest)

    quarter, group = me // GROUPS, lax.rem(me, GROUPS)
    span = wgate.shape[1] // GROUPS
    chunks = span // LANES
    tall = rows * LINES
    short = tall // GROUPS

    def multiply(k):
        columns = pl.ds(pl.multiple_of(lax.rem(group + k, GROUPS) * span, LANES), span)
        return [
            jnp.dot(scaled_mid, weight[:, columns], preferred_element_type=F32)
            for weight in (wgate, wup)
        ]

    def ship(k, parts):
        target = lax.rem(group + k, GROUPS)
        largest = jnp.maximum(jnp.abs(parts[0]), jnp.abs(parts[1]))
        unit_code = jnp.ceil(code_of(jnp.max(largest, axis=1, keepdims=True)))
        to_steps = STEPS / value_of(unit_code)
        unit_line = jnp.broadcast_to(unit_code, (rows, LANES))
        for index, (part, extra) in enumerate(zip(parts, (unit_line, square_line))):
            base = (2 * k + index) * tall
            steps = jnp.floor(part * to_steps + 0.5)
            for c in range(chunks):
                g6[pl.ds(base + c, rows, stride=LINES), :] = steps[:, c * LANES : (c + 1) * LANES]
            g6[pl.ds(base + chunks, rows, stride=LINES), :] = extra
            for q in range(GROUPS):
                piece = g6[base + q * short : base + (q + 1) * short, :]
                s6[k, q, index * short : (index + 1) * short, :] = piece.astype(jnp.int32).astype(
                    jnp.int16
                )
        for j in (2, 1, 3, 0) if k else (2, 1, 3):
            other = lax.rem(quarter + j, GROUPS)
            pltpu.make_async_remote_copy(
                src_ref=s6.at[k, other],
                dst_ref=r6.at[me],
                send_sem=send_sem.at[5],
                recv_sem=quarter_sem.at[k],
                device_id={"mem": other * GROUPS + target},
                device_id_type=MESH,
            ).start()

    order = (2, 1, 3, 0)
    parts = multiply(order[0])
    for index, k in enumerate(order):
        later = multiply(order[index + 1]) if index + 1 < GROUPS else None
        ship(k, parts)
        parts = later
    r6[me] = s6[0, quarter]

    gates = [jnp.zeros((LINES, LANES), F32)] * GROUPS
    ups = [jnp.zeros((LINES, LANES), F32)] * GROUPS
    square = jnp.zeros((GROUPS, LANES), F32)
    lane_codes = lax.broadcasted_iota(jnp.int32, (GROUPS, LANES), 1)
    for k, q in [(k, q) for k in order for q in range(GROUPS)]:
        if q == 0:
            arriving = GROUPS if k else GROUPS - 1
            wait_bytes(r6.at[pl.ds(0, arriving)], quarter_sem.at[k])
        sender = q * GROUPS + lax.rem(group + GROUPS - k, GROUPS)
        part = r6[sender].astype(jnp.int32).astype(F32)
        units, squares = (
            jnp.concatenate(
                [
                    part[start + r * LINES + chunks : start + r * LINES + chunks + 1]
                    for r in range(GROUPS)
                ],
                axis=0,
            )
            for start in (0, short)
        )
        units = value_of(units) * (1.0 / STEPS)
        squares = jnp.where(lane_codes < LANES // 2, squares, squares * (1.0 / STEPS))
        square = square + value_of(squares + pltpu.roll(squares, LANES // 2, 1))
        for r in range(GROUPS):
            own = slice(r * LINES, (r + 1) * LINES)
            gates[r] = gates[r] + part[:short][own] * units[r : r + 1]
            ups[r] = ups[r] + part[short:][own] * units[r : r + 1]
    inverse_two = 1.0 / jnp.sqrt(square / model_width + EPSILON)
    hidden = []
    for r in range(GROUPS):
        gate = gates[r] * inverse_two[r : r + 1]
        hidden.append(gate / (1.0 + jnp.exp(-gate)) * (ups[r] * inverse_two[r : r + 1]))
    s7[...] = jnp.concatenate(hidden, axis=0).astype(BF16)
    for other in member_order:
        pltpu.make_async_remote_copy(
            src_ref=s7,
            dst_ref=r7.at[me],
            send_sem=send_sem.at[6],
            recv_sem=group_sem.at[group],
            device_id={"mem": other},
            device_id_type=MESH,
        ).start()
    r7[me] = s7[...]
    ready("wdown")

    down = jnp.zeros((rows, wdown.shape[1]), F32)
    for k in (0, 1, 3, 2):
        source = lax.rem(group + k, GROUPS)
        arriving = GROUPS - 1 if k == 0 else GROUPS
        wait_bytes(r7.at[pl.ds(0, arriving)], group_sem.at[source])
        for q in range(GROUPS):
            line = k * tall + q * short
            g7[line : line + short, :] = r7[q * GROUPS + source].astype(F32)
        piece = jnp.concatenate(
            [
                g7[pl.ds(k * tall + c, rows, stride=LINES), :].astype(BF16)
                for c in range(chunks)
            ],
            axis=1,
        )
        down = down + jnp.dot(
            piece,
            wdown[pl.ds(pl.multiple_of(source * span, LANES), span), :],
            preferred_element_type=F32,
        )
    out_ref[...] = (after_f + sum_peers(7, down, s7b, r7b)).astype(BF16)

    wait_bytes(r1.at[pl.ds(0, members - 1), pl.ds(0, used)], send_sem.at[0])
    wait_bytes(r2.at[pl.ds(0, members - 1)], send_sem.at[1])
    wait_bytes(r4.at[pl.ds(0, (members - 1) * sent)], send_sem.at[2])
    wait_bytes(r5.at[pl.ds(0, (members - 1) * HEADS)], send_sem.at[3])
    for phase, landed in ((4, r5b), (7, r7b)):
        wait_bytes(landed.at[pl.ds(0, peers - 1)], send_sem.at[phase])
    for phase, landed in ((5, r6), (6, r7)):
        wait_bytes(landed.at[pl.ds(0, members - 1)], send_sem.at[phase])


def local(
    members,
    peers,
    tokens,
    attn_gain,
    query_key_value_weight,
    paged_key_store,
    paged_value_store,
    lengths,
    block_table,
    out_weight,
    mlp_gain,
    gate_weight,
    up_weight,
    down_weight,
):
    rows, width_part = tokens.shape
    slots, _, block_len, head_dim = paged_key_store.shape
    short = rows * LINES // GROUPS
    runs = slots // RUN + REQUESTS
    exponents = np.arange(head_dim // 2, dtype=np.float32) * np.float32(
        -2.0 * math.log(ROPE_BASE) / head_dim
    )
    inverse = np.exp(exponents.astype(np.float64)).astype(np.float32)
    freq = jnp.asarray(np.concatenate([inverse, inverse])[None, :])

    any_spec = pl.BlockSpec(memory_space=pl.ANY)
    vmem_spec = pl.BlockSpec(memory_space=pltpu.VMEM)
    scratch = [
        pltpu.SMEM(lengths.shape, jnp.int32),
        pltpu.VMEM(tokens.shape, BF16),
        pltpu.VMEM(attn_gain.shape, BF16),
        pltpu.VMEM(mlp_gain.shape, BF16),
        pltpu.VMEM(freq.shape, F32),
        pltpu.VMEM(block_table.shape, jnp.int32),
        pltpu.VMEM(query_key_value_weight.shape, BF16),
        pltpu.VMEM((slots, block_len, head_dim), BF16),
        pltpu.VMEM((slots, block_len, head_dim), BF16),
        pltpu.VMEM(out_weight.shape, BF16),
        pltpu.VMEM(gate_weight.shape, BF16),
        pltpu.VMEM(up_weight.shape, BF16),
        pltpu.VMEM(down_weight.shape, BF16),
        pltpu.VMEM((REQUESTS, GROUP, head_dim), BF16),
        pltpu.VMEM((8, 2 * LANES), jnp.int32),
        pltpu.SMEM((8, 2 * LANES), jnp.int32),
        pltpu.VMEM((REQUESTS, GROUP, LANES), F32),
        pltpu.VMEM((runs, GROUP, RUN * LANES), F32),
        pltpu.VMEM((rows * rows, LANES), F32),
        pltpu.VMEM((members, rows, LANES), F32),
        pltpu.VMEM((16, LANES), BF16),
        pltpu.VMEM((members, 16, LANES), BF16),
        pltpu.VMEM((members * PARTIAL, LANES), F32),
        pltpu.VMEM((members * PARTIAL, LANES), F32),
        pltpu.VMEM((HEADS, LANES), F32),
        pltpu.VMEM((members * HEADS, LANES), F32),
        pltpu.VMEM((rows, width_part + LANES), jnp.int16),
        pltpu.VMEM((peers, rows, width_part + LANES), jnp.int16),
        pltpu.VMEM((2 * GROUPS * rows * LINES, LANES), F32),
        pltpu.VMEM((GROUPS, GROUPS, 2 * short, LANES), jnp.int16),
        pltpu.VMEM((members, 2 * short, LANES), jnp.int16),
        pltpu.VMEM((short, LANES), BF16),
        pltpu.VMEM((members, short, LANES), BF16),
        pltpu.VMEM((GROUPS * rows * LINES, LANES), F32),
        pltpu.VMEM((rows, width_part + LANES), jnp.int16),
        pltpu.VMEM((peers, rows, width_part + LANES), jnp.int16),
        pltpu.SemaphoreType.DMA,
        pltpu.SemaphoreType.DMA((6 + 7 * PIECES + 2,)),
        pltpu.SemaphoreType.DMA((8,)),
        pltpu.SemaphoreType.DMA((8,)),
        pltpu.SemaphoreType.DMA((GROUPS,)),
        pltpu.SemaphoreType.DMA((GROUPS,)),
    ]
    return pl.pallas_call(
        functools.partial(kernel, members, peers, width_part * members),
        out_shape=pltpu.VMEM(tokens.shape, BF16),
        in_specs=[any_spec] * 13,
        out_specs=vmem_spec,
        scratch_shapes=scratch,
        compiler_params=pltpu.CompilerParams(
            collective_id=0, has_side_effects=True, vmem_limit_bytes=56 * 1024 * 1024
        ),
        name="decoder_layer",
    )(
        lengths,
        tokens,
        attn_gain,
        mlp_gain,
        freq,
        block_table,
        query_key_value_weight,
        paged_key_store,
        paged_value_store,
        out_weight,
        gate_weight,
        up_weight,
        down_weight,
    )


def solution(mesh):
    return jax.shard_map(
        functools.partial(local, mesh.shape["mem"], mesh.shape["mp"]),
        mesh=mesh,
        in_specs=(
            P(None, "mem"),
            P("mem"),
            P("mem", "mp"),
            P("mem", "mp", None, None),
            P("mem", "mp", None, None),
            P(),
            P(),
            P("mp", "mem"),
            P("mem"),
            P("mem", "mp"),
            P("mem", "mp"),
            P("mp", "mem"),
        ),
        out_specs=P(None, "mem"),
        check_vma=False,
    )
```

```python
import functools
import math

import jax
import jax.numpy as jnp
import numpy as np
from jax import lax
from jax.experimental import pallas as pl
from jax.experimental.pallas import tpu as pltpu
from jax.sharding import PartitionSpec as P

MESH = pl.DeviceIdType.MESH
F32 = jnp.float32
BF16 = jnp.bfloat16

EPSILON = 1e-05
ROPE_BASE = 500000.0
FLOOR_SCORE = -1e30
LANES = 128
HEADS = 8
NEW = 4
REQUESTS = 4
GROUP = NEW * HEADS
OWNER = 256
RUN = 4
TILE = 18
PARTIAL = 16
GROUPS = 4
LINES = 8
PIECES = 4

HALF_PI = (1.5703125, 0.000484466552734375, -6.397578377557687e-07)


def sine_cosine(angle):
    turns = jnp.floor(angle * (2.0 / math.pi) + 0.5)
    r = ((angle - turns * HALF_PI[0]) - turns * HALF_PI[1]) - turns * HALF_PI[2]
    z = r * r
    sine = r + r * z * (-1.6666654611e-1 + z * (8.3321608736e-3 + z * (-1.9515295891e-4)))
    cosine = 1.0 - 0.5 * z + z * z * (
        4.166664568298827e-2 + z * (-1.388731625493765e-3 + z * 2.443315711809948e-5)
    )
    quadrant = turns - 4.0 * jnp.floor(turns * 0.25)
    odd = (quadrant == 1.0) | (quadrant == 3.0)
    s, c = jnp.where(odd, cosine, sine), jnp.where(odd, sine, cosine)
    s = jnp.where(quadrant >= 2.0, -s, s)
    c = jnp.where((quadrant == 1.0) | (quadrant == 2.0), -c, c)
    return s, c


STEPS = 32000.0
FINE = 256.0


def code_of(value):
    return jnp.log(jnp.maximum(value, 1e-30)) * (FINE / math.log(2.0))


def value_of(code):
    return jnp.exp2(code * (1.0 / FINE))


def kernel(
    members,
    peers,
    model_width,
    lengths_hbm,
    tokens_hbm,
    gain_one_hbm,
    gain_two_hbm,
    freq_hbm,
    table_hbm,
    wqkv_hbm,
    keys_hbm,
    values_hbm,
    wout_hbm,
    wgate_hbm,
    wup_hbm,
    wdown_hbm,
    out_ref,
    lengths,
    tokens,
    gain_one,
    gain_two,
    freq,
    table,
    wqkv,
    keys,
    values,
    wout,
    wgate,
    wup,
    wdown,
    queries,
    codes,
    slot_codes,
    tops_ref,
    scores,
    s1,
    r1,
    s2,
    r2,
    s4,
    r4,
    s5,
    r5,
    s5b,
    r5b,
    g6,
    s6,
    r6,
    s7,
    r7,
    g7,
    s7b,
    r7b,
    code_sem,
    fetch_sem,
    send_sem,
    recv_sem,
    quarter_sem,
    group_sem,
):
    me = lax.axis_index("mem")
    mine = lax.axis_index("mp")
    rows = tokens.shape[0]
    slots = keys.shape[0]
    block_len = keys.shape[1]

    side = math.isqrt(members)
    z, x = me // side, lax.rem(me, side)
    steps_of = lambda d, n: min(d, n - d)
    offsets = sorted(
        ((dz, dx) for dz in range(side) for dx in range(side) if dz or dx),
        key=lambda d: -steps_of(d[0], side) - steps_of(d[1], side),
    )
    member_order = [lax.rem(z + dz, side) * side + lax.rem(x + dx, side) for dz, dx in offsets]
    ring, cores = peers // 2, 2
    y, core = mine // cores, lax.rem(mine, cores)
    offsets = sorted(
        ((dy, dc) for dy in range(ring) for dc in range(cores) if dy or dc),
        key=lambda d: -steps_of(d[0], ring),
    )
    peer_order = [lax.rem(y + dy, ring) * cores + lax.rem(core + dc, cores) for dy, dc in offsets]

    fetched = {}

    def fetch(name, source, target, pieces=1):
        size = target.shape[0] // pieces
        fetched[name] = []
        for p in range(pieces):
            index = sum(len(v) for v in fetched.values())
            if pieces > 1:
                part = pl.ds(p * size, size)
                copy = pltpu.make_async_copy(source.at[part], target.at[part], fetch_sem.at[index])
            else:
                copy = pltpu.make_async_copy(source, target, fetch_sem.at[index])
            copy.start()
            fetched[name].append(copy)

    def ready(*names):
        for name in names:
            for copy in fetched[name]:
                copy.wait()

    fetch("tokens", tokens_hbm, tokens)
    fetch("gain_one", gain_one_hbm, gain_one)
    fetch("wqkv", wqkv_hbm, wqkv, 2 * PIECES)
    fetch("lengths", lengths_hbm, lengths)
    fetch("freq", freq_hbm, freq)

    barrier = pltpu.get_barrier_semaphore()
    for other in member_order:
        pl.semaphore_signal(barrier, inc=1, device_id={"mem": other}, device_id_type=MESH)
    for other in peer_order:
        pl.semaphore_signal(barrier, inc=1, device_id={"mp": other}, device_id_type=MESH)

    fetch("table", table_hbm, table)
    fetch("gain_two", gain_two_hbm, gain_two)

    def send_members(phase, source_of, target):
        for other in member_order:
            pltpu.make_async_remote_copy(
                src_ref=source_of(other),
                dst_ref=target,
                send_sem=send_sem.at[phase],
                recv_sem=recv_sem.at[phase],
                device_id={"mem": other},
                device_id_type=MESH,
            ).start()

    def send_peers(phase, source, target):
        for other in peer_order:
            pltpu.make_async_remote_copy(
                src_ref=source,
                dst_ref=target,
                send_sem=send_sem.at[phase],
                recv_sem=recv_sem.at[phase],
                device_id={"mp": other},
                device_id_type=MESH,
            ).start()

    width = tokens.shape[1]

    def sum_peers(phase, partial, staged, landed):
        unit_code = jnp.ceil(code_of(jnp.max(jnp.abs(partial), axis=1, keepdims=True)))
        steps = jnp.floor(partial * (STEPS / value_of(unit_code)) + 0.5)
        staged[:, :width] = steps.astype(jnp.int32).astype(jnp.int16)
        staged[:, width:] = (
            jnp.broadcast_to(unit_code, (rows, LANES)).astype(jnp.int32).astype(jnp.int16)
        )
        send_peers(phase, staged, landed.at[mine])
        landed[mine] = staged[...]
        wait_bytes(landed.at[pl.ds(0, peers - 1)], recv_sem.at[phase])
        total = jnp.zeros((rows, width), F32)
        for j in range(peers):
            part = landed[j].astype(jnp.int32).astype(F32)
            unit = value_of(part[:, width:]) * (1.0 / STEPS)
            total = total + part[:, :width] * jnp.concatenate([unit] * (width // LANES), axis=1)
        return total

    def wait_bytes(window, semaphore):
        pltpu.make_async_copy(window, window, semaphore).wait()

    ready("tokens", "gain_one")
    token_f = tokens[...].astype(F32)
    scaled_in = (token_f * gain_one[...].astype(F32)[None, :]).astype(BF16)
    square_one = jnp.sum(token_f * token_f, axis=1, keepdims=True)
    request, place = me // NEW, lax.rem(me, NEW)
    ready("lengths", "freq")
    position = (lengths[request] + place).astype(F32)
    sine, cosine = sine_cosine(position * freq[...])
    lane_row = lax.broadcasted_iota(jnp.int32, (1, LANES), 1)
    sine = jnp.where(lane_row < LANES // 2, -sine, sine)
    ready("wqkv")
    projected = jnp.dot(scaled_in, wqkv[...], preferred_element_type=F32)
    for c in range(HEADS + 2):
        s1[pl.ds(c, rows, stride=rows), :] = projected[:, c * LANES : (c + 1) * LANES]
    s1[pl.ds(HEADS + 2, rows, stride=rows), :] = jnp.broadcast_to(square_one, (rows, LANES))

    pl.semaphore_wait(barrier, members - 1 + peers - 1)

    used = HEADS + 3
    send_members(
        0, lambda other: s1.at[pl.ds(other * rows, used)], r1.at[me, pl.ds(0, used)]
    )
    r1[me] = s1[pl.ds(pl.multiple_of(me * rows, rows), rows), :]

    fetch("keys", keys_hbm.at[:, 0], keys, PIECES)
    fetch("values", values_hbm.at[:, 0], values, PIECES)

    wait_bytes(r1.at[pl.ds(0, members - 1), pl.ds(0, used)], recv_sem.at[0])
    total = r1[0]
    for j in range(1, members):
        total = total + r1[j]
    inverse_one = 1.0 / jnp.sqrt(total[HEADS + 2 : HEADS + 3, :] / model_width + EPSILON)
    total = total * inverse_one
    turned = total * cosine + pltpu.roll(total, LANES // 2, 1) * sine
    head_row = lax.broadcasted_iota(jnp.int32, total.shape, 0)
    s2[...] = jnp.where(head_row <= HEADS, turned, total).astype(BF16)
    send_members(1, lambda other: s2, r2.at[me])
    r2[me] = s2[...]
    fetch("wout", wout_hbm, wout, 2)
    fetch("wgate", wgate_hbm, wgate, PIECES)
    fetch("wup", wup_hbm, wup, PIECES)
    fetch("wdown", wdown_hbm, wdown, PIECES)

    ready("table")
    first_slot = me * slots
    max_blocks = table.shape[1]
    block_start = lax.broadcasted_iota(jnp.int32, (1, max_blocks), 1) * block_len
    slot_ids = first_slot + lax.broadcasted_iota(jnp.int32, (slots, max_blocks), 0)
    code = jnp.zeros((slots, max_blocks), jnp.int32)
    for r in range(REQUESTS):
        held = jnp.clip(lengths[r] - block_start, 0, block_len)
        held = jnp.where(held > 0, held + r * OWNER, 0)
        code = code + jnp.where(table[r : r + 1, :] == slot_ids, held, 0)
    code = jnp.sum(code, axis=1, keepdims=True)
    sub = lax.broadcasted_iota(jnp.int32, (slots, slots), 0)
    lane = lax.broadcasted_iota(jnp.int32, (slots, slots), 1)
    code_line = jnp.sum(jnp.where(sub == lane, code, 0), axis=0, keepdims=True)
    owner_column = jnp.where(code > 0, code >> 8, REQUESTS)
    owner_line = jnp.where(code_line > 0, code_line >> 8, REQUESTS)
    ahead = jnp.where((owner_line == owner_column) & (lane < sub), 1, 0)
    place_column = jnp.sum(ahead, axis=1, keepdims=True)
    positions = codes.shape[1]
    run_ids = lax.broadcasted_iota(jnp.int32, (1, positions), 1) * RUN
    run_owner = jnp.zeros((1, positions), jnp.int32)
    start = jnp.zeros((1, 1), jnp.int32)
    for r in range(REQUESTS):
        if r > 0:
            run_owner = run_owner + jnp.where(run_ids >= start, 1, 0)
        place_column = place_column + jnp.where(owner_column == r, start, 0)
        number = jnp.sum(jnp.where(owner_line == r, 1, 0), axis=1, keepdims=True)
        start = start + ((number + (RUN - 1)) & -RUN)
    place_column = jnp.where(code > 0, place_column, -1)
    position_ids = lax.broadcasted_iota(jnp.int32, (slots, positions), 1)
    entry = lax.broadcasted_iota(jnp.int32, (slots, positions), 0) * OWNER + (code & (OWNER - 1))
    entry = jnp.where(position_ids == place_column, entry, 0)
    codes[0:1, :] = jnp.sum(entry, axis=0, keepdims=True)
    codes[1:2, :] = run_owner
    owner_row = run_owner[:, :LANES]
    to_scalars = pltpu.make_async_copy(codes, slot_codes, code_sem)
    to_scalars.start()

    wait_bytes(r2.at[pl.ds(0, members - 1)], recv_sem.at[1])

    for r in range(REQUESTS):
        queries[r] = jnp.concatenate(
            [r2[r * NEW + t].astype(F32)[:HEADS] for t in range(NEW)], axis=0
        ).astype(BF16)
    factor = math.log2(math.e) / math.sqrt(LANES)
    lane_group = lax.broadcasted_iota(jnp.int32, (GROUP, LANES), 1)
    to_scalars.wait()
    ready("keys")

    def run_of(run):
        entries = [slot_codes[0, run * RUN + i] for i in range(RUN)]
        return slot_codes[1, run], [(e >> 8, e & (OWNER - 1)) for e in entries]

    blank = jnp.zeros((GROUP, LANES), BF16)

    def score_step(step, best):
        for j in range(0, TILE, 2):
            pair = [(step * TILE + j + i,) + run_of(step * TILE + j + i) for i in range(2)]
            first, second = (queries[owner] for _, owner, _ in pair)
            left = jnp.concatenate(
                [
                    jnp.concatenate([first, blank], axis=1),
                    jnp.concatenate([blank, second], axis=1),
                ],
                axis=0,
            )
            right = jnp.concatenate(
                [
                    jnp.concatenate([keys[slot] for slot, _ in members_of], axis=0)
                    for _, _, members_of in pair
                ],
                axis=1,
            )
            both = lax.dot_general(
                left, right, (((1,), (1,)), ((), ())), preferred_element_type=F32
            )
            for half, (run, _, members_of) in enumerate(pair):
                score = both[half * GROUP : (half + 1) * GROUP]
                tops = []
                for i, (_, count) in enumerate(members_of):
                    part = slice(i * LANES, (i + 1) * LANES)
                    tops.append(jnp.where(lane_group < count, score[:, part], FLOOR_SCORE))
                    scores[run, :, part] = tops[-1]
                top = jnp.max(functools.reduce(jnp.maximum, tops), axis=1, keepdims=True)
                best = jnp.where(lane_group == run, top, best)
        return best

    floor = jnp.full((GROUP, LANES), FLOOR_SCORE, F32)
    runs = scores.shape[0]
    run_best = lax.fori_loop(0, runs // TILE, score_step, floor)
    best = []
    for r in range(REQUESTS):
        own = jnp.where(owner_row == r, run_best, FLOOR_SCORE)
        best.append(jnp.broadcast_to(jnp.max(own, axis=1, keepdims=True), (GROUP, LANES)))
        tops_ref[r] = best[r]
    ready("values")

    def value_step(step, carry):
        sums, mixed = carry[0], list(carry[1])
        for j in range(TILE):
            run = step * TILE + j
            owner, members_of = run_of(run)
            top = tops_ref[owner]
            weights, highs, lows = [], [], []
            for i in range(RUN):
                weight = jnp.exp2((scores[run, :, i * LANES : (i + 1) * LANES] - top) * factor)
                weights.append(weight)
                highs.append(weight.astype(BF16))
                lows.append((weight - highs[-1].astype(F32)).astype(BF16))
            total = jnp.sum(functools.reduce(jnp.add, weights), axis=1, keepdims=True)
            sums = jnp.where(lane_group == run, total, sums)
            both = jnp.dot(
                jnp.concatenate(
                    [jnp.concatenate(highs, axis=1), jnp.concatenate(lows, axis=1)], axis=0
                ),
                jnp.concatenate([values[slot] for slot, _ in members_of], axis=0),
                preferred_element_type=F32,
            )
            both = both[:GROUP] + both[GROUP:]
            for r in range(REQUESTS):
                mixed[r] = mixed[r] + jnp.where(owner == r, both, 0.0)
        return sums, tuple(mixed)

    zero = jnp.zeros((GROUP, LANES), F32)
    run_sums, mixed = lax.fori_loop(0, runs // TILE, value_step, (zero, (zero,) * REQUESTS))
    lane_head = lax.broadcasted_iota(jnp.int32, (HEADS, LANES), 1) // (LANES // HEADS)
    by_head = lane_head == lax.broadcasted_iota(jnp.int32, (HEADS, LANES), 0)

    def to_line(column):
        return jnp.sum(jnp.where(by_head, column, 0.0), axis=0, keepdims=True)

    def to_column(line):
        column = jnp.max(jnp.where(by_head, line, -jnp.inf), axis=1, keepdims=True)
        return jnp.broadcast_to(column, (HEADS, LANES))

    for r in range(REQUESTS):
        own = jnp.where(owner_row == r, run_sums, 0.0)
        whole = jnp.broadcast_to(jnp.sum(own, axis=1, keepdims=True), (GROUP, LANES))
        for t in range(NEW):
            part = slice(t * HEADS, (t + 1) * HEADS)
            line = (r * NEW + t) * PARTIAL
            s4[line : line + HEADS, :] = mixed[r][part]
            s4[line + HEADS : line + HEADS + 1, :] = to_line(best[r][part])
            s4[line + HEADS + 1 : line + HEADS + 2, :] = to_line(whole[part])
    mine_4 = pl.ds(pl.multiple_of(me * PARTIAL, PARTIAL), PARTIAL)
    sent = HEADS + 2
    send_members(
        2,
        lambda other: s4.at[pl.ds(other * PARTIAL, sent)],
        r4.at[pl.ds(me * PARTIAL, sent)],
    )
    r4[mine_4, :] = s4[mine_4, :]

    row_queries = r2[me].astype(F32)[:HEADS]
    own_scores, own_values = [], []
    for t in range(NEW):
        fresh = r2[request * NEW + t].astype(F32)
        score = jnp.sum(row_queries * fresh[HEADS : HEADS + 1], axis=1, keepdims=True)
        score = jnp.broadcast_to(score, (HEADS, LANES))
        own_scores.append(jnp.where(t <= place, score, FLOOR_SCORE))
        own_values.append(fresh[HEADS + 1 : HEADS + 2])
    top = to_line(functools.reduce(jnp.maximum, own_scores))

    wait_bytes(r4.at[pl.ds(0, (members - 1) * sent)], recv_sem.at[2])
    tops = r4[pl.ds(HEADS, members, stride=PARTIAL), :]
    wholes = r4[pl.ds(HEADS + 1, members, stride=PARTIAL), :]
    top = jnp.maximum(top, jnp.max(tops, axis=0, keepdims=True))
    shrink = jnp.exp2((tops - top) * factor)
    whole = to_column(jnp.sum(wholes * shrink, axis=0, keepdims=True))
    top = to_column(top)
    mix = jnp.zeros((HEADS, LANES), F32)
    for t in range(NEW):
        weight = jnp.exp2((own_scores[t] - top) * factor)
        whole = whole + weight
        mix = mix + weight * own_values[t]
    for j in range(members):
        mix = mix + r4[j * PARTIAL : j * PARTIAL + HEADS, :] * to_column(shrink[j : j + 1])
    s5[...] = mix / whole
    own_rows = pl.ds(pl.multiple_of(me * HEADS, HEADS), HEADS)
    send_members(3, lambda other: s5, r5.at[own_rows])
    r5[own_rows, :] = s5[...]
    ready("wout")
    wait_bytes(r5.at[pl.ds(0, (members - 1) * HEADS)], recv_sem.at[3])

    attended = jnp.concatenate(
        [r5[pl.ds(h, rows, stride=HEADS), :].astype(BF16) for h in range(HEADS)], axis=1
    )
    partial = jnp.dot(attended, wout[...], preferred_element_type=F32)
    after_f = (token_f + sum_peers(4, partial, s5b, r5b)).astype(BF16).astype(F32)
    ready("gain_two", "wgate", "wup")

    scaled_mid = (after_f * gain_two[...].astype(F32)[None, :]).astype(BF16)
    square_mid = jnp.sum(after_f * after_f, axis=1, keepdims=True)
    square_code = code_of(square_mid)
    square_whole = jnp.floor(square_code)
    square_rest = jnp.floor((square_code - square_whole) * STEPS + 0.5)
    lane_rows = lax.broadcasted_iota(jnp.int32, (rows, LANES), 1)
    square_line = jnp.where(lane_rows < LANES // 2, square_whole, square_rest)

    quarter, group = me // GROUPS, lax.rem(me, GROUPS)
    span = wgate.shape[1] // GROUPS
    chunks = span // LANES
    tall = rows * LINES
    short = tall // GROUPS

    def multiply(k):
        columns = pl.ds(pl.multiple_of(lax.rem(group + k, GROUPS) * span, LANES), span)
        both = jnp.concatenate([wgate[:, columns], wup[:, columns]], axis=1)
        both = jnp.dot(scaled_mid, both, preferred_element_type=F32)
        return both[:, :span], both[:, span:]

    def ship(k, parts):
        target = lax.rem(group + k, GROUPS)
        largest = jnp.maximum(jnp.abs(parts[0]), jnp.abs(parts[1]))
        unit_code = jnp.ceil(code_of(jnp.max(largest, axis=1, keepdims=True)))
        to_steps = STEPS / value_of(unit_code)
        unit_line = jnp.broadcast_to(unit_code, (rows, LANES))
        for index, (part, extra) in enumerate(zip(parts, (unit_line, square_line))):
            base = (2 * k + index) * tall
            steps = jnp.floor(part * to_steps + 0.5)
            for c in range(chunks):
                g6[pl.ds(base + c, rows, stride=LINES), :] = steps[:, c * LANES : (c + 1) * LANES]
            g6[pl.ds(base + chunks, rows, stride=LINES), :] = extra
            for q in range(GROUPS):
                piece = g6[base + q * short : base + (q + 1) * short, :]
                s6[k, q, index * short : (index + 1) * short, :] = piece.astype(jnp.int32).astype(
                    jnp.int16
                )
        for j in (2, 1, 3, 0) if k else (2, 1, 3):
            other = lax.rem(quarter + j, GROUPS)
            pltpu.make_async_remote_copy(
                src_ref=s6.at[k, other],
                dst_ref=r6.at[me],
                send_sem=send_sem.at[5],
                recv_sem=quarter_sem.at[k],
                device_id={"mem": other * GROUPS + target},
                device_id_type=MESH,
            ).start()

    order = (2, 1, 3, 0)
    parts = multiply(order[0])
    for index, k in enumerate(order):
        later = multiply(order[index + 1]) if index + 1 < GROUPS else None
        ship(k, parts)
        parts = later
    r6[me] = s6[0, quarter]

    gates = [jnp.zeros((LINES, LANES), F32)] * GROUPS
    ups = [jnp.zeros((LINES, LANES), F32)] * GROUPS
    square = jnp.zeros((GROUPS, LANES), F32)
    lane_codes = lax.broadcasted_iota(jnp.int32, (GROUPS, LANES), 1)
    for k, q in [(k, q) for k in order for q in range(GROUPS)]:
        if q == 0:
            arriving = GROUPS if k else GROUPS - 1
            wait_bytes(r6.at[pl.ds(0, arriving)], quarter_sem.at[k])
        sender = q * GROUPS + lax.rem(group + GROUPS - k, GROUPS)
        part = r6[sender].astype(jnp.int32).astype(F32)
        units, squares = (
            jnp.concatenate(
                [
                    part[start + r * LINES + chunks : start + r * LINES + chunks + 1]
                    for r in range(GROUPS)
                ],
                axis=0,
            )
            for start in (0, short)
        )
        units = value_of(units) * (1.0 / STEPS)
        squares = jnp.where(lane_codes < LANES // 2, squares, squares * (1.0 / STEPS))
        square = square + value_of(squares + pltpu.roll(squares, LANES // 2, 1))
        for r in range(GROUPS):
            own = slice(r * LINES, (r + 1) * LINES)
            gates[r] = gates[r] + part[:short][own] * units[r : r + 1]
            ups[r] = ups[r] + part[short:][own] * units[r : r + 1]
    inverse_two = 1.0 / jnp.sqrt(square / model_width + EPSILON)
    hidden = []
    for r in range(GROUPS):
        gate = gates[r] * inverse_two[r : r + 1]
        hidden.append(gate / (1.0 + jnp.exp(-gate)) * (ups[r] * inverse_two[r : r + 1]))
    s7[...] = jnp.concatenate(hidden, axis=0).astype(BF16)
    for other in member_order:
        pltpu.make_async_remote_copy(
            src_ref=s7,
            dst_ref=r7.at[me],
            send_sem=send_sem.at[6],
            recv_sem=group_sem.at[group],
            device_id={"mem": other},
            device_id_type=MESH,
        ).start()
    r7[me] = s7[...]
    ready("wdown")

    down = jnp.zeros((rows, wdown.shape[1]), F32)
    for k in (0, 1, 3, 2):
        source = lax.rem(group + k, GROUPS)
        arriving = GROUPS - 1 if k == 0 else GROUPS
        wait_bytes(r7.at[pl.ds(0, arriving)], group_sem.at[source])
        for q in range(GROUPS):
            line = k * tall + q * short
            g7[line : line + short, :] = r7[q * GROUPS + source].astype(F32)
        piece = jnp.concatenate(
            [
                g7[pl.ds(k * tall + c, rows, stride=LINES), :].astype(BF16)
                for c in range(chunks)
            ],
            axis=1,
        )
        down = down + jnp.dot(
            piece,
            wdown[pl.ds(pl.multiple_of(source * span, LANES), span), :],
            preferred_element_type=F32,
        )
    out_ref[...] = (after_f + sum_peers(7, down, s7b, r7b)).astype(BF16)

    wait_bytes(r1.at[pl.ds(0, members - 1), pl.ds(0, used)], send_sem.at[0])
    wait_bytes(r2.at[pl.ds(0, members - 1)], send_sem.at[1])
    wait_bytes(r4.at[pl.ds(0, (members - 1) * sent)], send_sem.at[2])
    wait_bytes(r5.at[pl.ds(0, (members - 1) * HEADS)], send_sem.at[3])
    for phase, landed in ((4, r5b), (7, r7b)):
        wait_bytes(landed.at[pl.ds(0, peers - 1)], send_sem.at[phase])
    for phase, landed in ((5, r6), (6, r7)):
        wait_bytes(landed.at[pl.ds(0, members - 1)], send_sem.at[phase])


def local(
    members,
    peers,
    tokens,
    attn_gain,
    query_key_value_weight,
    paged_key_store,
    paged_value_store,
    lengths,
    block_table,
    out_weight,
    mlp_gain,
    gate_weight,
    up_weight,
    down_weight,
):
    rows, width_part = tokens.shape
    slots, _, block_len, head_dim = paged_key_store.shape
    short = rows * LINES // GROUPS
    runs = slots // RUN + REQUESTS
    exponents = np.arange(head_dim // 2, dtype=np.float32) * np.float32(
        -2.0 * math.log(ROPE_BASE) / head_dim
    )
    inverse = np.exp(exponents.astype(np.float64)).astype(np.float32)
    freq = jnp.asarray(np.concatenate([inverse, inverse])[None, :])

    any_spec = pl.BlockSpec(memory_space=pl.ANY)
    vmem_spec = pl.BlockSpec(memory_space=pltpu.VMEM)
    scratch = [
        pltpu.SMEM(lengths.shape, jnp.int32),
        pltpu.VMEM(tokens.shape, BF16),
        pltpu.VMEM(attn_gain.shape, BF16),
        pltpu.VMEM(mlp_gain.shape, BF16),
        pltpu.VMEM(freq.shape, F32),
        pltpu.VMEM(block_table.shape, jnp.int32),
        pltpu.VMEM(query_key_value_weight.shape, BF16),
        pltpu.VMEM((slots, block_len, head_dim), BF16),
        pltpu.VMEM((slots, block_len, head_dim), BF16),
        pltpu.VMEM(out_weight.shape, BF16),
        pltpu.VMEM(gate_weight.shape, BF16),
        pltpu.VMEM(up_weight.shape, BF16),
        pltpu.VMEM(down_weight.shape, BF16),
        pltpu.VMEM((REQUESTS, GROUP, head_dim), BF16),
        pltpu.VMEM((8, 2 * LANES), jnp.int32),
        pltpu.SMEM((8, 2 * LANES), jnp.int32),
        pltpu.VMEM((REQUESTS, GROUP, LANES), F32),
        pltpu.VMEM((runs, GROUP, RUN * LANES), F32),
        pltpu.VMEM((rows * rows, LANES), F32),
        pltpu.VMEM((members, rows, LANES), F32),
        pltpu.VMEM((16, LANES), BF16),
        pltpu.VMEM((members, 16, LANES), BF16),
        pltpu.VMEM((members * PARTIAL, LANES), F32),
        pltpu.VMEM((members * PARTIAL, LANES), F32),
        pltpu.VMEM((HEADS, LANES), F32),
        pltpu.VMEM((members * HEADS, LANES), F32),
        pltpu.VMEM((rows, width_part + LANES), jnp.int16),
        pltpu.VMEM((peers, rows, width_part + LANES), jnp.int16),
        pltpu.VMEM((2 * GROUPS * rows * LINES, LANES), F32),
        pltpu.VMEM((GROUPS, GROUPS, 2 * short, LANES), jnp.int16),
        pltpu.VMEM((members, 2 * short, LANES), jnp.int16),
        pltpu.VMEM((short, LANES), BF16),
        pltpu.VMEM((members, short, LANES), BF16),
        pltpu.VMEM((GROUPS * rows * LINES, LANES), F32),
        pltpu.VMEM((rows, width_part + LANES), jnp.int16),
        pltpu.VMEM((peers, rows, width_part + LANES), jnp.int16),
        pltpu.SemaphoreType.DMA,
        pltpu.SemaphoreType.DMA((6 + 7 * PIECES + 2,)),
        pltpu.SemaphoreType.DMA((8,)),
        pltpu.SemaphoreType.DMA((8,)),
        pltpu.SemaphoreType.DMA((GROUPS,)),
        pltpu.SemaphoreType.DMA((GROUPS,)),
    ]
    return pl.pallas_call(
        functools.partial(kernel, members, peers, width_part * members),
        out_shape=pltpu.VMEM(tokens.shape, BF16),
        in_specs=[any_spec] * 13,
        out_specs=vmem_spec,
        scratch_shapes=scratch,
        compiler_params=pltpu.CompilerParams(
            collective_id=0, has_side_effects=True, vmem_limit_bytes=56 * 1024 * 1024
        ),
        name="decoder_layer",
    )(
        lengths,
        tokens,
        attn_gain,
        mlp_gain,
        freq,
        block_table,
        query_key_value_weight,
        paged_key_store,
        paged_value_store,
        out_weight,
        gate_weight,
        up_weight,
        down_weight,
    )


def solution(mesh):
    return jax.shard_map(
        functools.partial(local, mesh.shape["mem"], mesh.shape["mp"]),
        mesh=mesh,
        in_specs=(
            P(None, "mem"),
            P("mem"),
            P("mem", "mp"),
            P("mem", "mp", None, None),
            P("mem", "mp", None, None),
            P(),
            P(),
            P("mp", "mem"),
            P("mem"),
            P("mem", "mp"),
            P("mem", "mp"),
            P("mp", "mem"),
        ),
        out_specs=P(None, "mem"),
        check_vma=False,
    )
```

```python
import functools
import math

import jax
import jax.numpy as jnp
import numpy as np
from jax import lax
from jax.experimental import pallas as pl
from jax.experimental.pallas import tpu as pltpu
from jax.sharding import PartitionSpec as P

MESH = pl.DeviceIdType.MESH
F32 = jnp.float32
BF16 = jnp.bfloat16

EPSILON = 1e-05
ROPE_BASE = 500000.0
FLOOR_SCORE = -1e30
LANES = 128
HEADS = 8
NEW = 4
REQUESTS = 4
GROUP = NEW * HEADS
OWNER = 256
RUN = 4
TILE = 18
PARTIAL = 16
GROUPS = 4
LINES = 8
PIECES = 4

HALF_PI = (1.5703125, 0.000484466552734375, -6.397578377557687e-07)


def sine_cosine(angle):
    turns = jnp.floor(angle * (2.0 / math.pi) + 0.5)
    r = ((angle - turns * HALF_PI[0]) - turns * HALF_PI[1]) - turns * HALF_PI[2]
    z = r * r
    sine = r + r * z * (-1.6666654611e-1 + z * (8.3321608736e-3 + z * (-1.9515295891e-4)))
    cosine = 1.0 - 0.5 * z + z * z * (
        4.166664568298827e-2 + z * (-1.388731625493765e-3 + z * 2.443315711809948e-5)
    )
    quadrant = turns - 4.0 * jnp.floor(turns * 0.25)
    odd = (quadrant == 1.0) | (quadrant == 3.0)
    s, c = jnp.where(odd, cosine, sine), jnp.where(odd, sine, cosine)
    s = jnp.where(quadrant >= 2.0, -s, s)
    c = jnp.where((quadrant == 1.0) | (quadrant == 2.0), -c, c)
    return s, c


STEPS = 32000.0
FINE = 256.0


def code_of(value):
    return jnp.log(jnp.maximum(value, 1e-30)) * (FINE / math.log(2.0))


def value_of(code):
    return jnp.exp2(code * (1.0 / FINE))


def kernel(
    members,
    peers,
    model_width,
    lengths_hbm,
    tokens_hbm,
    gain_one_hbm,
    gain_two_hbm,
    freq_hbm,
    table_hbm,
    wqkv_hbm,
    keys_hbm,
    values_hbm,
    wout_hbm,
    wgate_hbm,
    wup_hbm,
    wdown_hbm,
    out_ref,
    lengths,
    tokens,
    gain_one,
    gain_two,
    freq,
    table,
    wqkv,
    keys,
    values,
    wout,
    wgate,
    wup,
    wdown,
    queries,
    codes,
    slot_codes,
    tops_ref,
    scores,
    s1,
    r1,
    s2,
    r2,
    s4,
    r4,
    s5,
    r5,
    s5b,
    r5b,
    g6,
    s6,
    r6,
    s7,
    r7,
    g7,
    s7b,
    r7b,
    code_sem,
    fetch_sem,
    send_sem,
    recv_sem,
    quarter_sem,
    group_sem,
):
    me = lax.axis_index("mem")
    mine = lax.axis_index("mp")
    rows = tokens.shape[0]
    slots = keys.shape[0]
    block_len = keys.shape[1]

    side = math.isqrt(members)
    z, x = me // side, lax.rem(me, side)
    steps_of = lambda d, n: min(d, n - d)
    offsets = sorted(
        ((dz, dx) for dz in range(side) for dx in range(side) if dz or dx),
        key=lambda d: -steps_of(d[0], side) - steps_of(d[1], side),
    )
    member_order = [lax.rem(z + dz, side) * side + lax.rem(x + dx, side) for dz, dx in offsets]
    ring, cores = peers // 2, 2
    y, core = mine // cores, lax.rem(mine, cores)
    offsets = sorted(
        ((dy, dc) for dy in range(ring) for dc in range(cores) if dy or dc),
        key=lambda d: -steps_of(d[0], ring),
    )
    peer_order = [lax.rem(y + dy, ring) * cores + lax.rem(core + dc, cores) for dy, dc in offsets]

    fetched = {}

    def fetch(name, source, target, pieces=1):
        size = target.shape[0] // pieces
        fetched[name] = []
        for p in range(pieces):
            index = sum(len(v) for v in fetched.values())
            if pieces > 1:
                part = pl.ds(p * size, size)
                copy = pltpu.make_async_copy(source.at[part], target.at[part], fetch_sem.at[index])
            else:
                copy = pltpu.make_async_copy(source, target, fetch_sem.at[index])
            copy.start()
            fetched[name].append(copy)

    def ready(*names):
        for name in names:
            for copy in fetched[name]:
                copy.wait()

    fetch("tokens", tokens_hbm, tokens)
    fetch("gain_one", gain_one_hbm, gain_one)
    fetch("wqkv", wqkv_hbm, wqkv, 2 * PIECES)
    fetch("lengths", lengths_hbm, lengths)
    fetch("freq", freq_hbm, freq)

    barrier = pltpu.get_barrier_semaphore()
    for other in member_order:
        pl.semaphore_signal(barrier, inc=1, device_id={"mem": other}, device_id_type=MESH)
    for other in peer_order:
        pl.semaphore_signal(barrier, inc=1, device_id={"mp": other}, device_id_type=MESH)

    fetch("table", table_hbm, table)
    fetch("gain_two", gain_two_hbm, gain_two)

    def send_members(phase, source_of, target):
        for other in member_order:
            pltpu.make_async_remote_copy(
                src_ref=source_of(other),
                dst_ref=target,
                send_sem=send_sem.at[phase],
                recv_sem=recv_sem.at[phase],
                device_id={"mem": other},
                device_id_type=MESH,
            ).start()

    def send_peers(phase, source, target):
        for other in peer_order:
            pltpu.make_async_remote_copy(
                src_ref=source,
                dst_ref=target,
                send_sem=send_sem.at[phase],
                recv_sem=recv_sem.at[phase],
                device_id={"mp": other},
                device_id_type=MESH,
            ).start()

    width = tokens.shape[1]

    def sum_peers(phase, partial, staged, landed):
        unit_code = jnp.ceil(code_of(jnp.max(jnp.abs(partial), axis=1, keepdims=True)))
        steps = jnp.floor(partial * (STEPS / value_of(unit_code)) + 0.5)
        staged[:, :width] = steps.astype(jnp.int32).astype(jnp.int16)
        staged[:, width:] = (
            jnp.broadcast_to(unit_code, (rows, LANES)).astype(jnp.int32).astype(jnp.int16)
        )
        send_peers(phase, staged, landed.at[mine])
        landed[mine] = staged[...]
        wait_bytes(landed.at[pl.ds(0, peers - 1)], recv_sem.at[phase])
        total = jnp.zeros((rows, width), F32)
        for j in range(peers):
            part = landed[j].astype(jnp.int32).astype(F32)
            unit = value_of(part[:, width:]) * (1.0 / STEPS)
            total = total + part[:, :width] * jnp.concatenate([unit] * (width // LANES), axis=1)
        return total

    def wait_bytes(window, semaphore):
        pltpu.make_async_copy(window, window, semaphore).wait()

    ready("tokens", "gain_one")
    token_f = tokens[...].astype(F32)
    scaled_in = (token_f * gain_one[...].astype(F32)[None, :]).astype(BF16)
    square_one = jnp.sum(token_f * token_f, axis=1, keepdims=True)
    request, place = me // NEW, lax.rem(me, NEW)
    ready("lengths", "freq")
    position = (lengths[request] + place).astype(F32)
    sine, cosine = sine_cosine(position * freq[...])
    lane_row = lax.broadcasted_iota(jnp.int32, (1, LANES), 1)
    sine = jnp.where(lane_row < LANES // 2, -sine, sine)
    ready("wqkv")
    projected = jnp.dot(scaled_in, wqkv[...], preferred_element_type=F32)
    for c in range(HEADS + 2):
        s1[pl.ds(c, rows, stride=rows), :] = projected[:, c * LANES : (c + 1) * LANES]
    s1[pl.ds(HEADS + 2, rows, stride=rows), :] = jnp.broadcast_to(square_one, (rows, LANES))

    pl.semaphore_wait(barrier, members - 1 + peers - 1)

    used = HEADS + 3
    send_members(
        0, lambda other: s1.at[pl.ds(other * rows, used)], r1.at[me, pl.ds(0, used)]
    )
    r1[me] = s1[pl.ds(pl.multiple_of(me * rows, rows), rows), :]

    fetch("keys", keys_hbm.at[:, 0], keys, PIECES)

    wait_bytes(r1.at[pl.ds(0, members - 1), pl.ds(0, used)], recv_sem.at[0])
    total = r1[0]
    for j in range(1, members):
        total = total + r1[j]
    inverse_one = 1.0 / jnp.sqrt(total[HEADS + 2 : HEADS + 3, :] / model_width + EPSILON)
    total = total * inverse_one
    turned = total * cosine + pltpu.roll(total, LANES // 2, 1) * sine
    head_row = lax.broadcasted_iota(jnp.int32, total.shape, 0)
    s2[...] = jnp.where(head_row <= HEADS, turned, total).astype(BF16)
    send_members(1, lambda other: s2, r2.at[me])
    r2[me] = s2[...]
    fetch("values", values_hbm.at[:, 0], values, PIECES)
    fetch("wout", wout_hbm, wout, 2)
    fetch("wgate", wgate_hbm, wgate, PIECES)
    fetch("wup", wup_hbm, wup, PIECES)

    ready("table")
    first_slot = me * slots
    max_blocks = table.shape[1]
    block_start = lax.broadcasted_iota(jnp.int32, (1, max_blocks), 1) * block_len
    slot_ids = first_slot + lax.broadcasted_iota(jnp.int32, (slots, max_blocks), 0)
    code = jnp.zeros((slots, max_blocks), jnp.int32)
    for r in range(REQUESTS):
        held = jnp.clip(lengths[r] - block_start, 0, block_len)
        held = jnp.where(held > 0, held + r * OWNER, 0)
        code = code + jnp.where(table[r : r + 1, :] == slot_ids, held, 0)
    code = jnp.sum(code, axis=1, keepdims=True)
    sub = lax.broadcasted_iota(jnp.int32, (slots, slots), 0)
    lane = lax.broadcasted_iota(jnp.int32, (slots, slots), 1)
    code_line = jnp.sum(jnp.where(sub == lane, code, 0), axis=0, keepdims=True)
    owner_column = jnp.where(code > 0, code >> 8, REQUESTS)
    owner_line = jnp.where(code_line > 0, code_line >> 8, REQUESTS)
    ahead = jnp.where((owner_line == owner_column) & (lane < sub), 1, 0)
    place_column = jnp.sum(ahead, axis=1, keepdims=True)
    positions = codes.shape[1]
    run_ids = lax.broadcasted_iota(jnp.int32, (1, positions), 1) * RUN
    run_owner = jnp.zeros((1, positions), jnp.int32)
    start = jnp.zeros((1, 1), jnp.int32)
    for r in range(REQUESTS):
        if r > 0:
            run_owner = run_owner + jnp.where(run_ids >= start, 1, 0)
        place_column = place_column + jnp.where(owner_column == r, start, 0)
        number = jnp.sum(jnp.where(owner_line == r, 1, 0), axis=1, keepdims=True)
        start = start + ((number + (RUN - 1)) & -RUN)
    place_column = jnp.where(code > 0, place_column, -1)
    position_ids = lax.broadcasted_iota(jnp.int32, (slots, positions), 1)
    entry = lax.broadcasted_iota(jnp.int32, (slots, positions), 0) * OWNER + (code & (OWNER - 1))
    entry = jnp.where(position_ids == place_column, entry, 0)
    codes[0:1, :] = jnp.sum(entry, axis=0, keepdims=True)
    codes[1:2, :] = run_owner
    owner_row = run_owner[:, :LANES]
    to_scalars = pltpu.make_async_copy(codes, slot_codes, code_sem)
    to_scalars.start()

    wait_bytes(r2.at[pl.ds(0, members - 1)], recv_sem.at[1])

    for r in range(REQUESTS):
        queries[r] = jnp.concatenate(
            [r2[r * NEW + t].astype(F32)[:HEADS] for t in range(NEW)], axis=0
        ).astype(BF16)
    factor = math.log2(math.e) / math.sqrt(LANES)
    lane_group = lax.broadcasted_iota(jnp.int32, (GROUP, LANES), 1)
    to_scalars.wait()
    ready("keys")

    def run_of(run):
        entries = [slot_codes[0, run * RUN + i] for i in range(RUN)]
        return slot_codes[1, run], [(e >> 8, e & (OWNER - 1)) for e in entries]

    blank = jnp.zeros((GROUP, LANES), BF16)

    def score_step(step, best):
        for j in range(0, TILE, 2):
            pair = [(step * TILE + j + i,) + run_of(step * TILE + j + i) for i in range(2)]
            first, second = (queries[owner] for _, owner, _ in pair)
            left = jnp.concatenate(
                [
                    jnp.concatenate([first, blank], axis=1),
                    jnp.concatenate([blank, second], axis=1),
                ],
                axis=0,
            )
            right = jnp.concatenate(
                [
                    jnp.concatenate([keys[slot] for slot, _ in members_of], axis=0)
                    for _, _, members_of in pair
                ],
                axis=1,
            )
            both = lax.dot_general(
                left, right, (((1,), (1,)), ((), ())), preferred_element_type=F32
            )
            for half, (run, _, members_of) in enumerate(pair):
                score = both[half * GROUP : (half + 1) * GROUP]
                tops = []
                for i, (_, count) in enumerate(members_of):
                    part = slice(i * LANES, (i + 1) * LANES)
                    tops.append(jnp.where(lane_group < count, score[:, part], FLOOR_SCORE))
                    scores[run, :, part] = tops[-1]
                top = jnp.max(functools.reduce(jnp.maximum, tops), axis=1, keepdims=True)
                best = jnp.where(lane_group == run, top, best)
        return best

    floor = jnp.full((GROUP, LANES), FLOOR_SCORE, F32)
    runs = scores.shape[0]
    run_best = lax.fori_loop(0, runs // TILE, score_step, floor)
    best = []
    for r in range(REQUESTS):
        own = jnp.where(owner_row == r, run_best, FLOOR_SCORE)
        best.append(jnp.broadcast_to(jnp.max(own, axis=1, keepdims=True), (GROUP, LANES)))
        tops_ref[r] = best[r]
    ready("values")

    def value_step(step, carry):
        sums, mixed = carry[0], list(carry[1])
        for j in range(TILE):
            run = step * TILE + j
            owner, members_of = run_of(run)
            top = tops_ref[owner]
            weights, highs, lows = [], [], []
            for i in range(RUN):
                weight = jnp.exp2((scores[run, :, i * LANES : (i + 1) * LANES] - top) * factor)
                weights.append(weight)
                highs.append(weight.astype(BF16))
                lows.append((weight - highs[-1].astype(F32)).astype(BF16))
            total = jnp.sum(functools.reduce(jnp.add, weights), axis=1, keepdims=True)
            sums = jnp.where(lane_group == run, total, sums)
            both = jnp.dot(
                jnp.concatenate(
                    [jnp.concatenate(highs, axis=1), jnp.concatenate(lows, axis=1)], axis=0
                ),
                jnp.concatenate([values[slot] for slot, _ in members_of], axis=0),
                preferred_element_type=F32,
            )
            both = both[:GROUP] + both[GROUP:]
            for r in range(REQUESTS):
                mixed[r] = mixed[r] + jnp.where(owner == r, both, 0.0)
        return sums, tuple(mixed)

    zero = jnp.zeros((GROUP, LANES), F32)
    run_sums, mixed = lax.fori_loop(0, runs // TILE, value_step, (zero, (zero,) * REQUESTS))
    lane_head = lax.broadcasted_iota(jnp.int32, (HEADS, LANES), 1) // (LANES // HEADS)
    by_head = lane_head == lax.broadcasted_iota(jnp.int32, (HEADS, LANES), 0)

    def to_line(column):
        return jnp.sum(jnp.where(by_head, column, 0.0), axis=0, keepdims=True)

    def to_column(line):
        column = jnp.max(jnp.where(by_head, line, -jnp.inf), axis=1, keepdims=True)
        return jnp.broadcast_to(column, (HEADS, LANES))

    for r in range(REQUESTS):
        own = jnp.where(owner_row == r, run_sums, 0.0)
        whole = jnp.broadcast_to(jnp.sum(own, axis=1, keepdims=True), (GROUP, LANES))
        for t in range(NEW):
            part = slice(t * HEADS, (t + 1) * HEADS)
            line = (r * NEW + t) * PARTIAL
            s4[line : line + HEADS, :] = mixed[r][part]
            s4[line + HEADS : line + HEADS + 1, :] = to_line(best[r][part])
            s4[line + HEADS + 1 : line + HEADS + 2, :] = to_line(whole[part])
    mine_4 = pl.ds(pl.multiple_of(me * PARTIAL, PARTIAL), PARTIAL)
    sent = HEADS + 2
    send_members(
        2,
        lambda other: s4.at[pl.ds(other * PARTIAL, sent)],
        r4.at[pl.ds(me * PARTIAL, sent)],
    )
    r4[mine_4, :] = s4[mine_4, :]
    fetch("wdown", wdown_hbm, wdown, PIECES)

    row_queries = r2[me].astype(F32)[:HEADS]
    own_scores, own_values = [], []
    for t in range(NEW):
        fresh = r2[request * NEW + t].astype(F32)
        score = jnp.sum(row_queries * fresh[HEADS : HEADS + 1], axis=1, keepdims=True)
        score = jnp.broadcast_to(score, (HEADS, LANES))
        own_scores.append(jnp.where(t <= place, score, FLOOR_SCORE))
        own_values.append(fresh[HEADS + 1 : HEADS + 2])
    top = to_line(functools.reduce(jnp.maximum, own_scores))

    wait_bytes(r4.at[pl.ds(0, (members - 1) * sent)], recv_sem.at[2])
    tops = r4[pl.ds(HEADS, members, stride=PARTIAL), :]
    wholes = r4[pl.ds(HEADS + 1, members, stride=PARTIAL), :]
    top = jnp.maximum(top, jnp.max(tops, axis=0, keepdims=True))
    shrink = jnp.exp2((tops - top) * factor)
    whole = to_column(jnp.sum(wholes * shrink, axis=0, keepdims=True))
    top = to_column(top)
    mix = jnp.zeros((HEADS, LANES), F32)
    for t in range(NEW):
        weight = jnp.exp2((own_scores[t] - top) * factor)
        whole = whole + weight
        mix = mix + weight * own_values[t]
    for j in range(members):
        mix = mix + r4[j * PARTIAL : j * PARTIAL + HEADS, :] * to_column(shrink[j : j + 1])
    s5[...] = mix / whole
    own_rows = pl.ds(pl.multiple_of(me * HEADS, HEADS), HEADS)
    send_members(3, lambda other: s5, r5.at[own_rows])
    r5[own_rows, :] = s5[...]
    ready("wout")
    wait_bytes(r5.at[pl.ds(0, (members - 1) * HEADS)], recv_sem.at[3])

    attended = jnp.concatenate(
        [r5[pl.ds(h, rows, stride=HEADS), :].astype(BF16) for h in range(HEADS)], axis=1
    )
    partial = jnp.dot(attended, wout[...], preferred_element_type=F32)
    after_f = (token_f + sum_peers(4, partial, s5b, r5b)).astype(BF16).astype(F32)
    ready("gain_two", "wgate", "wup")

    scaled_mid = (after_f * gain_two[...].astype(F32)[None, :]).astype(BF16)
    square_mid = jnp.sum(after_f * after_f, axis=1, keepdims=True)
    square_code = code_of(square_mid)
    square_whole = jnp.floor(square_code)
    square_rest = jnp.floor((square_code - square_whole) * STEPS + 0.5)
    lane_rows = lax.broadcasted_iota(jnp.int32, (rows, LANES), 1)
    square_line = jnp.where(lane_rows < LANES // 2, square_whole, square_rest)

    quarter, group = me // GROUPS, lax.rem(me, GROUPS)
    span = wgate.shape[1] // GROUPS
    chunks = span // LANES
    tall = rows * LINES
    short = tall // GROUPS

    def multiply(k):
        columns = pl.ds(pl.multiple_of(lax.rem(group + k, GROUPS) * span, LANES), span)
        both = jnp.concatenate([wgate[:, columns], wup[:, columns]], axis=1)
        both = jnp.dot(scaled_mid, both, preferred_element_type=F32)
        return both[:, :span], both[:, span:]

    def ship(k, parts):
        target = lax.rem(group + k, GROUPS)
        largest = jnp.maximum(jnp.abs(parts[0]), jnp.abs(parts[1]))
        unit_code = jnp.ceil(code_of(jnp.max(largest, axis=1, keepdims=True)))
        to_steps = STEPS / value_of(unit_code)
        unit_line = jnp.broadcast_to(unit_code, (rows, LANES))
        for index, (part, extra) in enumerate(zip(parts, (unit_line, square_line))):
            base = (2 * k + index) * tall
            steps = jnp.floor(part * to_steps + 0.5)
            for c in range(chunks):
                g6[pl.ds(base + c, rows, stride=LINES), :] = steps[:, c * LANES : (c + 1) * LANES]
            g6[pl.ds(base + chunks, rows, stride=LINES), :] = extra
            for q in range(GROUPS):
                piece = g6[base + q * short : base + (q + 1) * short, :]
                s6[k, q, index * short : (index + 1) * short, :] = piece.astype(jnp.int32).astype(
                    jnp.int16
                )
        for j in (2, 1, 3, 0) if k else (2, 1, 3):
            other = lax.rem(quarter + j, GROUPS)
            pltpu.make_async_remote_copy(
                src_ref=s6.at[k, other],
                dst_ref=r6.at[me],
                send_sem=send_sem.at[5],
                recv_sem=quarter_sem.at[k],
                device_id={"mem": other * GROUPS + target},
                device_id_type=MESH,
            ).start()

    order = (2, 1, 3, 0)
    parts = multiply(order[0])
    for index, k in enumerate(order):
        later = multiply(order[index + 1]) if index + 1 < GROUPS else None
        ship(k, parts)
        parts = later
    r6[me] = s6[0, quarter]

    gates = [jnp.zeros((LINES, LANES), F32)] * GROUPS
    ups = [jnp.zeros((LINES, LANES), F32)] * GROUPS
    square = jnp.zeros((GROUPS, LANES), F32)
    lane_codes = lax.broadcasted_iota(jnp.int32, (GROUPS, LANES), 1)
    for k, q in [(k, q) for k in order for q in range(GROUPS)]:
        if q == 0:
            arriving = GROUPS if k else GROUPS - 1
            wait_bytes(r6.at[pl.ds(0, arriving)], quarter_sem.at[k])
        sender = q * GROUPS + lax.rem(group + GROUPS - k, GROUPS)
        part = r6[sender].astype(jnp.int32).astype(F32)
        units, squares = (
            jnp.concatenate(
                [
                    part[start + r * LINES + chunks : start + r * LINES + chunks + 1]
                    for r in range(GROUPS)
                ],
                axis=0,
            )
            for start in (0, short)
        )
        units = value_of(units) * (1.0 / STEPS)
        squares = jnp.where(lane_codes < LANES // 2, squares, squares * (1.0 / STEPS))
        square = square + value_of(squares + pltpu.roll(squares, LANES // 2, 1))
        for r in range(GROUPS):
            own = slice(r * LINES, (r + 1) * LINES)
            gates[r] = gates[r] + part[:short][own] * units[r : r + 1]
            ups[r] = ups[r] + part[short:][own] * units[r : r + 1]
    inverse_two = 1.0 / jnp.sqrt(square / model_width + EPSILON)
    hidden = []
    for r in range(GROUPS):
        gate = gates[r] * inverse_two[r : r + 1]
        hidden.append(gate / (1.0 + jnp.exp(-gate)) * (ups[r] * inverse_two[r : r + 1]))
    s7[...] = jnp.concatenate(hidden, axis=0).astype(BF16)
    for other in member_order:
        pltpu.make_async_remote_copy(
            src_ref=s7,
            dst_ref=r7.at[me],
            send_sem=send_sem.at[6],
            recv_sem=group_sem.at[group],
            device_id={"mem": other},
            device_id_type=MESH,
        ).start()
    r7[me] = s7[...]
    ready("wdown")

    down = jnp.zeros((rows, wdown.shape[1]), F32)
    for k in (0, 1, 3, 2):
        source = lax.rem(group + k, GROUPS)
        arriving = GROUPS - 1 if k == 0 else GROUPS
        wait_bytes(r7.at[pl.ds(0, arriving)], group_sem.at[source])
        for q in range(GROUPS):
            line = k * tall + q * short
            g7[line : line + short, :] = r7[q * GROUPS + source].astype(F32)
        piece = jnp.concatenate(
            [
                g7[pl.ds(k * tall + c, rows, stride=LINES), :].astype(BF16)
                for c in range(chunks)
            ],
            axis=1,
        )
        down = down + jnp.dot(
            piece,
            wdown[pl.ds(pl.multiple_of(source * span, LANES), span), :],
            preferred_element_type=F32,
        )
    out_ref[...] = (after_f + sum_peers(7, down, s7b, r7b)).astype(BF16)

    wait_bytes(r1.at[pl.ds(0, members - 1), pl.ds(0, used)], send_sem.at[0])
    wait_bytes(r2.at[pl.ds(0, members - 1)], send_sem.at[1])
    wait_bytes(r4.at[pl.ds(0, (members - 1) * sent)], send_sem.at[2])
    wait_bytes(r5.at[pl.ds(0, (members - 1) * HEADS)], send_sem.at[3])
    for phase, landed in ((4, r5b), (7, r7b)):
        wait_bytes(landed.at[pl.ds(0, peers - 1)], send_sem.at[phase])
    for phase, landed in ((5, r6), (6, r7)):
        wait_bytes(landed.at[pl.ds(0, members - 1)], send_sem.at[phase])


def local(
    members,
    peers,
    tokens,
    attn_gain,
    query_key_value_weight,
    paged_key_store,
    paged_value_store,
    lengths,
    block_table,
    out_weight,
    mlp_gain,
    gate_weight,
    up_weight,
    down_weight,
):
    rows, width_part = tokens.shape
    slots, _, block_len, head_dim = paged_key_store.shape
    short = rows * LINES // GROUPS
    runs = slots // RUN + REQUESTS
    exponents = np.arange(head_dim // 2, dtype=np.float32) * np.float32(
        -2.0 * math.log(ROPE_BASE) / head_dim
    )
    inverse = np.exp(exponents.astype(np.float64)).astype(np.float32)
    freq = jnp.asarray(np.concatenate([inverse, inverse])[None, :])

    any_spec = pl.BlockSpec(memory_space=pl.ANY)
    vmem_spec = pl.BlockSpec(memory_space=pltpu.VMEM)
    scratch = [
        pltpu.SMEM(lengths.shape, jnp.int32),
        pltpu.VMEM(tokens.shape, BF16),
        pltpu.VMEM(attn_gain.shape, BF16),
        pltpu.VMEM(mlp_gain.shape, BF16),
        pltpu.VMEM(freq.shape, F32),
        pltpu.VMEM(block_table.shape, jnp.int32),
        pltpu.VMEM(query_key_value_weight.shape, BF16),
        pltpu.VMEM((slots, block_len, head_dim), BF16),
        pltpu.VMEM((slots, block_len, head_dim), BF16),
        pltpu.VMEM(out_weight.shape, BF16),
        pltpu.VMEM(gate_weight.shape, BF16),
        pltpu.VMEM(up_weight.shape, BF16),
        pltpu.VMEM(down_weight.shape, BF16),
        pltpu.VMEM((REQUESTS, GROUP, head_dim), BF16),
        pltpu.VMEM((8, 2 * LANES), jnp.int32),
        pltpu.SMEM((8, 2 * LANES), jnp.int32),
        pltpu.VMEM((REQUESTS, GROUP, LANES), F32),
        pltpu.VMEM((runs, GROUP, RUN * LANES), F32),
        pltpu.VMEM((rows * rows, LANES), F32),
        pltpu.VMEM((members, rows, LANES), F32),
        pltpu.VMEM((16, LANES), BF16),
        pltpu.VMEM((members, 16, LANES), BF16),
        pltpu.VMEM((members * PARTIAL, LANES), F32),
        pltpu.VMEM((members * PARTIAL, LANES), F32),
        pltpu.VMEM((HEADS, LANES), F32),
        pltpu.VMEM((members * HEADS, LANES), F32),
        pltpu.VMEM((rows, width_part + LANES), jnp.int16),
        pltpu.VMEM((peers, rows, width_part + LANES), jnp.int16),
        pltpu.VMEM((2 * GROUPS * rows * LINES, LANES), F32),
        pltpu.VMEM((GROUPS, GROUPS, 2 * short, LANES), jnp.int16),
        pltpu.VMEM((members, 2 * short, LANES), jnp.int16),
        pltpu.VMEM((short, LANES), BF16),
        pltpu.VMEM((members, short, LANES), BF16),
        pltpu.VMEM((GROUPS * rows * LINES, LANES), F32),
        pltpu.VMEM((rows, width_part + LANES), jnp.int16),
        pltpu.VMEM((peers, rows, width_part + LANES), jnp.int16),
        pltpu.SemaphoreType.DMA,
        pltpu.SemaphoreType.DMA((6 + 7 * PIECES + 2,)),
        pltpu.SemaphoreType.DMA((8,)),
        pltpu.SemaphoreType.DMA((8,)),
        pltpu.SemaphoreType.DMA((GROUPS,)),
        pltpu.SemaphoreType.DMA((GROUPS,)),
    ]
    return pl.pallas_call(
        functools.partial(kernel, members, peers, width_part * members),
        out_shape=pltpu.VMEM(tokens.shape, BF16),
        in_specs=[any_spec] * 13,
        out_specs=vmem_spec,
        scratch_shapes=scratch,
        compiler_params=pltpu.CompilerParams(
            collective_id=0, has_side_effects=True, vmem_limit_bytes=56 * 1024 * 1024
        ),
        name="decoder_layer",
    )(
        lengths,
        tokens,
        attn_gain,
        mlp_gain,
        freq,
        block_table,
        query_key_value_weight,
        paged_key_store,
        paged_value_store,
        out_weight,
        gate_weight,
        up_weight,
        down_weight,
    )


def solution(mesh):
    return jax.shard_map(
        functools.partial(local, mesh.shape["mem"], mesh.shape["mp"]),
        mesh=mesh,
        in_specs=(
            P(None, "mem"),
            P("mem"),
            P("mem", "mp"),
            P("mem", "mp", None, None),
            P("mem", "mp", None, None),
            P(),
            P(),
            P("mp", "mem"),
            P("mem"),
            P("mem", "mp"),
            P("mem", "mp"),
            P("mp", "mem"),
        ),
        out_specs=P(None, "mem"),
        check_vma=False,
    )
```

```python
import functools
import math

import jax
import jax.numpy as jnp
import numpy as np
from jax import lax
from jax.experimental import pallas as pl
from jax.experimental.pallas import tpu as pltpu
from jax.sharding import PartitionSpec as P

MESH = pl.DeviceIdType.MESH
F32 = jnp.float32
BF16 = jnp.bfloat16

EPSILON = 1e-05
ROPE_BASE = 500000.0
FLOOR_SCORE = -1e30
LANES = 128
HEADS = 8
NEW = 4
REQUESTS = 4
GROUP = NEW * HEADS
OWNER = 256
RUN = 4
TILE = 36
PARTIAL = 16
GROUPS = 4
LINES = 8
PIECES = 4

HALF_PI = (1.5703125, 0.000484466552734375, -6.397578377557687e-07)


def sine_cosine(angle):
    turns = jnp.floor(angle * (2.0 / math.pi) + 0.5)
    r = ((angle - turns * HALF_PI[0]) - turns * HALF_PI[1]) - turns * HALF_PI[2]
    z = r * r
    sine = r + r * z * (-1.6666654611e-1 + z * (8.3321608736e-3 + z * (-1.9515295891e-4)))
    cosine = 1.0 - 0.5 * z + z * z * (
        4.166664568298827e-2 + z * (-1.388731625493765e-3 + z * 2.443315711809948e-5)
    )
    quadrant = turns - 4.0 * jnp.floor(turns * 0.25)
    odd = (quadrant == 1.0) | (quadrant == 3.0)
    s, c = jnp.where(odd, cosine, sine), jnp.where(odd, sine, cosine)
    s = jnp.where(quadrant >= 2.0, -s, s)
    c = jnp.where((quadrant == 1.0) | (quadrant == 2.0), -c, c)
    return s, c


STEPS = 32000.0
FINE = 256.0


def code_of(value):
    return jnp.log(jnp.maximum(value, 1e-30)) * (FINE / math.log(2.0))


def value_of(code):
    return jnp.exp2(code * (1.0 / FINE))


def kernel(
    members,
    peers,
    model_width,
    lengths_hbm,
    tokens_hbm,
    gain_one_hbm,
    gain_two_hbm,
    freq_hbm,
    table_hbm,
    wqkv_hbm,
    keys_hbm,
    values_hbm,
    wout_hbm,
    wgate_hbm,
    wup_hbm,
    wdown_hbm,
    out_ref,
    lengths,
    tokens,
    gain_one,
    gain_two,
    freq,
    table,
    wqkv,
    keys,
    values,
    wout,
    wgate,
    wup,
    wdown,
    queries,
    codes,
    slot_codes,
    tops_ref,
    scores,
    s1,
    r1,
    s2,
    r2,
    s4,
    r4,
    s5,
    r5,
    s5b,
    r5b,
    g6,
    s6,
    r6,
    s7,
    r7,
    g7,
    s7b,
    r7b,
    code_sem,
    fetch_sem,
    send_sem,
    recv_sem,
    quarter_sem,
    group_sem,
):
    me = lax.axis_index("mem")
    mine = lax.axis_index("mp")
    rows = tokens.shape[0]
    slots = keys.shape[0]
    block_len = keys.shape[1]

    side = math.isqrt(members)
    z, x = me // side, lax.rem(me, side)
    steps_of = lambda d, n: min(d, n - d)
    offsets = sorted(
        ((dz, dx) for dz in range(side) for dx in range(side) if dz or dx),
        key=lambda d: -steps_of(d[0], side) - steps_of(d[1], side),
    )
    member_order = [lax.rem(z + dz, side) * side + lax.rem(x + dx, side) for dz, dx in offsets]
    ring, cores = peers // 2, 2
    y, core = mine // cores, lax.rem(mine, cores)
    offsets = sorted(
        ((dy, dc) for dy in range(ring) for dc in range(cores) if dy or dc),
        key=lambda d: -steps_of(d[0], ring),
    )
    peer_order = [lax.rem(y + dy, ring) * cores + lax.rem(core + dc, cores) for dy, dc in offsets]

    fetched = {}

    def fetch(name, source, target, pieces=1):
        size = target.shape[0] // pieces
        fetched[name] = []
        for p in range(pieces):
            index = sum(len(v) for v in fetched.values())
            if pieces > 1:
                part = pl.ds(p * size, size)
                copy = pltpu.make_async_copy(source.at[part], target.at[part], fetch_sem.at[index])
            else:
                copy = pltpu.make_async_copy(source, target, fetch_sem.at[index])
            copy.start()
            fetched[name].append(copy)

    def ready(*names):
        for name in names:
            for copy in fetched[name]:
                copy.wait()

    fetch("tokens", tokens_hbm, tokens)
    fetch("gain_one", gain_one_hbm, gain_one)
    fetch("wqkv", wqkv_hbm, wqkv, 2 * PIECES)
    fetch("lengths", lengths_hbm, lengths)
    fetch("freq", freq_hbm, freq)

    barrier = pltpu.get_barrier_semaphore()
    for other in member_order:
        pl.semaphore_signal(barrier, inc=1, device_id={"mem": other}, device_id_type=MESH)
    for other in peer_order:
        pl.semaphore_signal(barrier, inc=1, device_id={"mp": other}, device_id_type=MESH)

    fetch("table", table_hbm, table)
    fetch("gain_two", gain_two_hbm, gain_two)

    def send_members(phase, source_of, target):
        for other in member_order:
            pltpu.make_async_remote_copy(
                src_ref=source_of(other),
                dst_ref=target,
                send_sem=send_sem.at[phase],
                recv_sem=recv_sem.at[phase],
                device_id={"mem": other},
                device_id_type=MESH,
            ).start()

    def send_peers(phase, source, target):
        for other in peer_order:
            pltpu.make_async_remote_copy(
                src_ref=source,
                dst_ref=target,
                send_sem=send_sem.at[phase],
                recv_sem=recv_sem.at[phase],
                device_id={"mp": other},
                device_id_type=MESH,
            ).start()

    width = tokens.shape[1]

    def sum_peers(phase, partial, staged, landed):
        unit_code = jnp.ceil(code_of(jnp.max(jnp.abs(partial), axis=1, keepdims=True)))
        steps = jnp.floor(partial * (STEPS / value_of(unit_code)) + 0.5)
        staged[:, :width] = steps.astype(jnp.int32).astype(jnp.int16)
        staged[:, width:] = (
            jnp.broadcast_to(unit_code, (rows, LANES)).astype(jnp.int32).astype(jnp.int16)
        )
        send_peers(phase, staged, landed.at[mine])
        landed[mine] = staged[...]
        wait_bytes(landed.at[pl.ds(0, peers - 1)], recv_sem.at[phase])
        total = jnp.zeros((rows, width), F32)
        for j in range(peers):
            part = landed[j].astype(jnp.int32).astype(F32)
            unit = value_of(part[:, width:]) * (1.0 / STEPS)
            total = total + part[:, :width] * jnp.concatenate([unit] * (width // LANES), axis=1)
        return total

    def wait_bytes(window, semaphore):
        pltpu.make_async_copy(window, window, semaphore).wait()

    ready("tokens", "gain_one")
    token_f = tokens[...].astype(F32)
    scaled_in = (token_f * gain_one[...].astype(F32)[None, :]).astype(BF16)
    square_one = jnp.sum(token_f * token_f, axis=1, keepdims=True)
    request, place = me // NEW, lax.rem(me, NEW)
    ready("lengths", "freq")
    position = (lengths[request] + place).astype(F32)
    sine, cosine = sine_cosine(position * freq[...])
    lane_row = lax.broadcasted_iota(jnp.int32, (1, LANES), 1)
    sine = jnp.where(lane_row < LANES // 2, -sine, sine)
    ready("wqkv")
    projected = jnp.dot(scaled_in, wqkv[...], preferred_element_type=F32)
    for c in range(HEADS + 2):
        s1[pl.ds(c, rows, stride=rows), :] = projected[:, c * LANES : (c + 1) * LANES]
    s1[pl.ds(HEADS + 2, rows, stride=rows), :] = jnp.broadcast_to(square_one, (rows, LANES))

    pl.semaphore_wait(barrier, members - 1 + peers - 1)

    used = HEADS + 3
    send_members(
        0, lambda other: s1.at[pl.ds(other * rows, used)], r1.at[me, pl.ds(0, used)]
    )
    r1[me] = s1[pl.ds(pl.multiple_of(me * rows, rows), rows), :]

    fetch("keys", keys_hbm.at[:, 0], keys, PIECES)

    wait_bytes(r1.at[pl.ds(0, members - 1), pl.ds(0, used)], recv_sem.at[0])
    total = r1[0]
    for j in range(1, members):
        total = total + r1[j]
    inverse_one = 1.0 / jnp.sqrt(total[HEADS + 2 : HEADS + 3, :] / model_width + EPSILON)
    total = total * inverse_one
    turned = total * cosine + pltpu.roll(total, LANES // 2, 1) * sine
    head_row = lax.broadcasted_iota(jnp.int32, total.shape, 0)
    s2[...] = jnp.where(head_row <= HEADS, turned, total).astype(BF16)
    send_members(1, lambda other: s2, r2.at[me])
    r2[me] = s2[...]
    fetch("values", values_hbm.at[:, 0], values, PIECES)
    fetch("wout", wout_hbm, wout, 2)
    fetch("wgate", wgate_hbm, wgate, PIECES)
    fetch("wup", wup_hbm, wup, PIECES)

    ready("table")
    first_slot = me * slots
    max_blocks = table.shape[1]
    block_start = lax.broadcasted_iota(jnp.int32, (1, max_blocks), 1) * block_len
    slot_ids = first_slot + lax.broadcasted_iota(jnp.int32, (slots, max_blocks), 0)
    code = jnp.zeros((slots, max_blocks), jnp.int32)
    for r in range(REQUESTS):
        held = jnp.clip(lengths[r] - block_start, 0, block_len)
        held = jnp.where(held > 0, held + r * OWNER, 0)
        code = code + jnp.where(table[r : r + 1, :] == slot_ids, held, 0)
    code = jnp.sum(code, axis=1, keepdims=True)
    sub = lax.broadcasted_iota(jnp.int32, (slots, slots), 0)
    lane = lax.broadcasted_iota(jnp.int32, (slots, slots), 1)
    code_line = jnp.sum(jnp.where(sub == lane, code, 0), axis=0, keepdims=True)
    owner_column = jnp.where(code > 0, code >> 8, REQUESTS)
    owner_line = jnp.where(code_line > 0, code_line >> 8, REQUESTS)
    ahead = jnp.where((owner_line == owner_column) & (lane < sub), 1, 0)
    place_column = jnp.sum(ahead, axis=1, keepdims=True)
    positions = codes.shape[1]
    run_ids = lax.broadcasted_iota(jnp.int32, (1, positions), 1) * RUN
    run_owner = jnp.zeros((1, positions), jnp.int32)
    start = jnp.zeros((1, 1), jnp.int32)
    for r in range(REQUESTS):
        if r > 0:
            run_owner = run_owner + jnp.where(run_ids >= start, 1, 0)
        place_column = place_column + jnp.where(owner_column == r, start, 0)
        number = jnp.sum(jnp.where(owner_line == r, 1, 0), axis=1, keepdims=True)
        start = start + ((number + (RUN - 1)) & -RUN)
    place_column = jnp.where(code > 0, place_column, -1)
    position_ids = lax.broadcasted_iota(jnp.int32, (slots, positions), 1)
    entry = lax.broadcasted_iota(jnp.int32, (slots, positions), 0) * OWNER + (code & (OWNER - 1))
    entry = jnp.where(position_ids == place_column, entry, 0)
    codes[0:1, :] = jnp.sum(entry, axis=0, keepdims=True)
    codes[1:2, :] = run_owner
    owner_row = run_owner[:, :LANES]
    to_scalars = pltpu.make_async_copy(codes, slot_codes, code_sem)
    to_scalars.start()

    wait_bytes(r2.at[pl.ds(0, members - 1)], recv_sem.at[1])

    for r in range(REQUESTS):
        queries[r] = jnp.concatenate(
            [r2[r * NEW + t].astype(F32)[:HEADS] for t in range(NEW)], axis=0
        ).astype(BF16)
    factor = math.log2(math.e) / math.sqrt(LANES)
    lane_group = lax.broadcasted_iota(jnp.int32, (GROUP, LANES), 1)
    to_scalars.wait()
    ready("keys")

    def run_of(run):
        entries = [slot_codes[0, run * RUN + i] for i in range(RUN)]
        return slot_codes[1, run], [(e >> 8, e & (OWNER - 1)) for e in entries]

    blank = jnp.zeros((GROUP, LANES), BF16)

    def score_step(step, best):
        for j in range(0, TILE, 2):
            pair = [(step * TILE + j + i,) + run_of(step * TILE + j + i) for i in range(2)]
            first, second = (queries[owner] for _, owner, _ in pair)
            left = jnp.concatenate(
                [
                    jnp.concatenate([first, blank], axis=1),
                    jnp.concatenate([blank, second], axis=1),
                ],
                axis=0,
            )
            right = jnp.concatenate(
                [
                    jnp.concatenate([keys[slot] for slot, _ in members_of], axis=0)
                    for _, _, members_of in pair
                ],
                axis=1,
            )
            both = lax.dot_general(
                left, right, (((1,), (1,)), ((), ())), preferred_element_type=F32
            )
            for half, (run, _, members_of) in enumerate(pair):
                score = both[half * GROUP : (half + 1) * GROUP]
                tops = []
                for i, (_, count) in enumerate(members_of):
                    part = slice(i * LANES, (i + 1) * LANES)
                    tops.append(jnp.where(lane_group < count, score[:, part], FLOOR_SCORE))
                    scores[run, :, part] = tops[-1]
                top = jnp.max(functools.reduce(jnp.maximum, tops), axis=1, keepdims=True)
                best = jnp.where(lane_group == run, top, best)
        return best

    floor = jnp.full((GROUP, LANES), FLOOR_SCORE, F32)
    runs = scores.shape[0]
    run_best = lax.fori_loop(0, runs // TILE, score_step, floor)
    best = []
    for r in range(REQUESTS):
        own = jnp.where(owner_row == r, run_best, FLOOR_SCORE)
        best.append(jnp.broadcast_to(jnp.max(own, axis=1, keepdims=True), (GROUP, LANES)))
        tops_ref[r] = best[r]
    ready("values")

    def value_step(step, carry):
        sums, mixed = carry[0], list(carry[1])
        for j in range(TILE):
            run = step * TILE + j
            owner, members_of = run_of(run)
            top = tops_ref[owner]
            weights, highs, lows = [], [], []
            for i in range(RUN):
                weight = jnp.exp2((scores[run, :, i * LANES : (i + 1) * LANES] - top) * factor)
                weights.append(weight)
                highs.append(weight.astype(BF16))
                lows.append((weight - highs[-1].astype(F32)).astype(BF16))
            total = jnp.sum(functools.reduce(jnp.add, weights), axis=1, keepdims=True)
            sums = jnp.where(lane_group == run, total, sums)
            both = jnp.dot(
                jnp.concatenate(
                    [jnp.concatenate(highs, axis=1), jnp.concatenate(lows, axis=1)], axis=0
                ),
                jnp.concatenate([values[slot] for slot, _ in members_of], axis=0),
                preferred_element_type=F32,
            )
            both = both[:GROUP] + both[GROUP:]
            for r in range(REQUESTS):
                mixed[r] = mixed[r] + jnp.where(owner == r, both, 0.0)
        return sums, tuple(mixed)

    zero = jnp.zeros((GROUP, LANES), F32)
    run_sums, mixed = lax.fori_loop(0, runs // TILE, value_step, (zero, (zero,) * REQUESTS))
    lane_head = lax.broadcasted_iota(jnp.int32, (HEADS, LANES), 1) // (LANES // HEADS)
    by_head = lane_head == lax.broadcasted_iota(jnp.int32, (HEADS, LANES), 0)

    def to_line(column):
        return jnp.sum(jnp.where(by_head, column, 0.0), axis=0, keepdims=True)

    def to_column(line):
        column = jnp.max(jnp.where(by_head, line, -jnp.inf), axis=1, keepdims=True)
        return jnp.broadcast_to(column, (HEADS, LANES))

    for r in range(REQUESTS):
        own = jnp.where(owner_row == r, run_sums, 0.0)
        whole = jnp.broadcast_to(jnp.sum(own, axis=1, keepdims=True), (GROUP, LANES))
        for t in range(NEW):
            part = slice(t * HEADS, (t + 1) * HEADS)
            line = (r * NEW + t) * PARTIAL
            s4[line : line + HEADS, :] = mixed[r][part]
            s4[line + HEADS : line + HEADS + 1, :] = to_line(best[r][part])
            s4[line + HEADS + 1 : line + HEADS + 2, :] = to_line(whole[part])
    mine_4 = pl.ds(pl.multiple_of(me * PARTIAL, PARTIAL), PARTIAL)
    sent = HEADS + 2
    send_members(
        2,
        lambda other: s4.at[pl.ds(other * PARTIAL, sent)],
        r4.at[pl.ds(me * PARTIAL, sent)],
    )
    r4[mine_4, :] = s4[mine_4, :]
    fetch("wdown", wdown_hbm, wdown, PIECES)

    row_queries = r2[me].astype(F32)[:HEADS]
    own_scores, own_values = [], []
    for t in range(NEW):
        fresh = r2[request * NEW + t].astype(F32)
        score = jnp.sum(row_queries * fresh[HEADS : HEADS + 1], axis=1, keepdims=True)
        score = jnp.broadcast_to(score, (HEADS, LANES))
        own_scores.append(jnp.where(t <= place, score, FLOOR_SCORE))
        own_values.append(fresh[HEADS + 1 : HEADS + 2])
    top = to_line(functools.reduce(jnp.maximum, own_scores))

    wait_bytes(r4.at[pl.ds(0, (members - 1) * sent)], recv_sem.at[2])
    tops = r4[pl.ds(HEADS, members, stride=PARTIAL), :]
    wholes = r4[pl.ds(HEADS + 1, members, stride=PARTIAL), :]
    top = jnp.maximum(top, jnp.max(tops, axis=0, keepdims=True))
    shrink = jnp.exp2((tops - top) * factor)
    whole = to_column(jnp.sum(wholes * shrink, axis=0, keepdims=True))
    top = to_column(top)
    mix = jnp.zeros((HEADS, LANES), F32)
    for t in range(NEW):
        weight = jnp.exp2((own_scores[t] - top) * factor)
        whole = whole + weight
        mix = mix + weight * own_values[t]
    for j in range(members):
        mix = mix + r4[j * PARTIAL : j * PARTIAL + HEADS, :] * to_column(shrink[j : j + 1])
    s5[...] = mix / whole
    own_rows = pl.ds(pl.multiple_of(me * HEADS, HEADS), HEADS)
    send_members(3, lambda other: s5, r5.at[own_rows])
    r5[own_rows, :] = s5[...]
    ready("wout")
    wait_bytes(r5.at[pl.ds(0, (members - 1) * HEADS)], recv_sem.at[3])

    attended = jnp.concatenate(
        [r5[pl.ds(h, rows, stride=HEADS), :].astype(BF16) for h in range(HEADS)], axis=1
    )
    partial = jnp.dot(attended, wout[...], preferred_element_type=F32)
    after_f = (token_f + sum_peers(4, partial, s5b, r5b)).astype(BF16).astype(F32)
    ready("gain_two", "wgate", "wup")

    scaled_mid = (after_f * gain_two[...].astype(F32)[None, :]).astype(BF16)
    square_mid = jnp.sum(after_f * after_f, axis=1, keepdims=True)
    square_code = code_of(square_mid)
    square_whole = jnp.floor(square_code)
    square_rest = jnp.floor((square_code - square_whole) * STEPS + 0.5)
    lane_rows = lax.broadcasted_iota(jnp.int32, (rows, LANES), 1)
    square_line = jnp.where(lane_rows < LANES // 2, square_whole, square_rest)

    quarter, group = me // GROUPS, lax.rem(me, GROUPS)
    span = wgate.shape[1] // GROUPS
    chunks = span // LANES
    tall = rows * LINES
    short = tall // GROUPS

    def multiply(k):
        columns = pl.ds(pl.multiple_of(lax.rem(group + k, GROUPS) * span, LANES), span)
        both = jnp.concatenate([wgate[:, columns], wup[:, columns]], axis=1)
        both = jnp.dot(scaled_mid, both, preferred_element_type=F32)
        return both[:, :span], both[:, span:]

    def ship(k, parts):
        target = lax.rem(group + k, GROUPS)
        largest = jnp.maximum(jnp.abs(parts[0]), jnp.abs(parts[1]))
        unit_code = jnp.ceil(code_of(jnp.max(largest, axis=1, keepdims=True)))
        to_steps = STEPS / value_of(unit_code)
        unit_line = jnp.broadcast_to(unit_code, (rows, LANES))
        for index, (part, extra) in enumerate(zip(parts, (unit_line, square_line))):
            base = (2 * k + index) * tall
            steps = jnp.floor(part * to_steps + 0.5)
            for c in range(chunks):
                g6[pl.ds(base + c, rows, stride=LINES), :] = steps[:, c * LANES : (c + 1) * LANES]
            g6[pl.ds(base + chunks, rows, stride=LINES), :] = extra
            for q in range(GROUPS):
                piece = g6[base + q * short : base + (q + 1) * short, :]
                s6[k, q, index * short : (index + 1) * short, :] = piece.astype(jnp.int32).astype(
                    jnp.int16
                )
        for j in (2, 1, 3, 0) if k else (2, 1, 3):
            other = lax.rem(quarter + j, GROUPS)
            pltpu.make_async_remote_copy(
                src_ref=s6.at[k, other],
                dst_ref=r6.at[me],
                send_sem=send_sem.at[5],
                recv_sem=quarter_sem.at[k],
                device_id={"mem": other * GROUPS + target},
                device_id_type=MESH,
            ).start()

    order = (2, 1, 3, 0)
    parts = multiply(order[0])
    for index, k in enumerate(order):
        later = multiply(order[index + 1]) if index + 1 < GROUPS else None
        ship(k, parts)
        parts = later
    r6[me] = s6[0, quarter]

    gates = [jnp.zeros((LINES, LANES), F32)] * GROUPS
    ups = [jnp.zeros((LINES, LANES), F32)] * GROUPS
    square = jnp.zeros((GROUPS, LANES), F32)
    lane_codes = lax.broadcasted_iota(jnp.int32, (GROUPS, LANES), 1)
    for k, q in [(k, q) for k in order for q in range(GROUPS)]:
        if q == 0:
            arriving = GROUPS if k else GROUPS - 1
            wait_bytes(r6.at[pl.ds(0, arriving)], quarter_sem.at[k])
        sender = q * GROUPS + lax.rem(group + GROUPS - k, GROUPS)
        part = r6[sender].astype(jnp.int32).astype(F32)
        units, squares = (
            jnp.concatenate(
                [
                    part[start + r * LINES + chunks : start + r * LINES + chunks + 1]
                    for r in range(GROUPS)
                ],
                axis=0,
            )
            for start in (0, short)
        )
        units = value_of(units) * (1.0 / STEPS)
        squares = jnp.where(lane_codes < LANES // 2, squares, squares * (1.0 / STEPS))
        square = square + value_of(squares + pltpu.roll(squares, LANES // 2, 1))
        for r in range(GROUPS):
            own = slice(r * LINES, (r + 1) * LINES)
            gates[r] = gates[r] + part[:short][own] * units[r : r + 1]
            ups[r] = ups[r] + part[short:][own] * units[r : r + 1]
    inverse_two = 1.0 / jnp.sqrt(square / model_width + EPSILON)
    hidden = []
    for r in range(GROUPS):
        gate = gates[r] * inverse_two[r : r + 1]
        hidden.append(gate / (1.0 + jnp.exp(-gate)) * (ups[r] * inverse_two[r : r + 1]))
    s7[...] = jnp.concatenate(hidden, axis=0).astype(BF16)
    for other in member_order:
        pltpu.make_async_remote_copy(
            src_ref=s7,
            dst_ref=r7.at[me],
            send_sem=send_sem.at[6],
            recv_sem=group_sem.at[group],
            device_id={"mem": other},
            device_id_type=MESH,
        ).start()
    r7[me] = s7[...]
    ready("wdown")

    down = jnp.zeros((rows, wdown.shape[1]), F32)
    for k in (0, 1, 3, 2):
        source = lax.rem(group + k, GROUPS)
        arriving = GROUPS - 1 if k == 0 else GROUPS
        wait_bytes(r7.at[pl.ds(0, arriving)], group_sem.at[source])
        for q in range(GROUPS):
            line = k * tall + q * short
            g7[line : line + short, :] = r7[q * GROUPS + source].astype(F32)
        piece = jnp.concatenate(
            [
                g7[pl.ds(k * tall + c, rows, stride=LINES), :].astype(BF16)
                for c in range(chunks)
            ],
            axis=1,
        )
        down = down + jnp.dot(
            piece,
            wdown[pl.ds(pl.multiple_of(source * span, LANES), span), :],
            preferred_element_type=F32,
        )
    out_ref[...] = (after_f + sum_peers(7, down, s7b, r7b)).astype(BF16)

    wait_bytes(r1.at[pl.ds(0, members - 1), pl.ds(0, used)], send_sem.at[0])
    wait_bytes(r2.at[pl.ds(0, members - 1)], send_sem.at[1])
    wait_bytes(r4.at[pl.ds(0, (members - 1) * sent)], send_sem.at[2])
    wait_bytes(r5.at[pl.ds(0, (members - 1) * HEADS)], send_sem.at[3])
    for phase, landed in ((4, r5b), (7, r7b)):
        wait_bytes(landed.at[pl.ds(0, peers - 1)], send_sem.at[phase])
    for phase, landed in ((5, r6), (6, r7)):
        wait_bytes(landed.at[pl.ds(0, members - 1)], send_sem.at[phase])


def local(
    members,
    peers,
    tokens,
    attn_gain,
    query_key_value_weight,
    paged_key_store,
    paged_value_store,
    lengths,
    block_table,
    out_weight,
    mlp_gain,
    gate_weight,
    up_weight,
    down_weight,
):
    rows, width_part = tokens.shape
    slots, _, block_len, head_dim = paged_key_store.shape
    short = rows * LINES // GROUPS
    runs = slots // RUN + REQUESTS
    exponents = np.arange(head_dim // 2, dtype=np.float32) * np.float32(
        -2.0 * math.log(ROPE_BASE) / head_dim
    )
    inverse = np.exp(exponents.astype(np.float64)).astype(np.float32)
    freq = jnp.asarray(np.concatenate([inverse, inverse])[None, :])

    any_spec = pl.BlockSpec(memory_space=pl.ANY)
    vmem_spec = pl.BlockSpec(memory_space=pltpu.VMEM)
    scratch = [
        pltpu.SMEM(lengths.shape, jnp.int32),
        pltpu.VMEM(tokens.shape, BF16),
        pltpu.VMEM(attn_gain.shape, BF16),
        pltpu.VMEM(mlp_gain.shape, BF16),
        pltpu.VMEM(freq.shape, F32),
        pltpu.VMEM(block_table.shape, jnp.int32),
        pltpu.VMEM(query_key_value_weight.shape, BF16),
        pltpu.VMEM((slots, block_len, head_dim), BF16),
        pltpu.VMEM((slots, block_len, head_dim), BF16),
        pltpu.VMEM(out_weight.shape, BF16),
        pltpu.VMEM(gate_weight.shape, BF16),
        pltpu.VMEM(up_weight.shape, BF16),
        pltpu.VMEM(down_weight.shape, BF16),
        pltpu.VMEM((REQUESTS, GROUP, head_dim), BF16),
        pltpu.VMEM((8, 2 * LANES), jnp.int32),
        pltpu.SMEM((8, 2 * LANES), jnp.int32),
        pltpu.VMEM((REQUESTS, GROUP, LANES), F32),
        pltpu.VMEM((runs, GROUP, RUN * LANES), F32),
        pltpu.VMEM((rows * rows, LANES), F32),
        pltpu.VMEM((members, rows, LANES), F32),
        pltpu.VMEM((16, LANES), BF16),
        pltpu.VMEM((members, 16, LANES), BF16),
        pltpu.VMEM((members * PARTIAL, LANES), F32),
        pltpu.VMEM((members * PARTIAL, LANES), F32),
        pltpu.VMEM((HEADS, LANES), F32),
        pltpu.VMEM((members * HEADS, LANES), F32),
        pltpu.VMEM((rows, width_part + LANES), jnp.int16),
        pltpu.VMEM((peers, rows, width_part + LANES), jnp.int16),
        pltpu.VMEM((2 * GROUPS * rows * LINES, LANES), F32),
        pltpu.VMEM((GROUPS, GROUPS, 2 * short, LANES), jnp.int16),
        pltpu.VMEM((members, 2 * short, LANES), jnp.int16),
        pltpu.VMEM((short, LANES), BF16),
        pltpu.VMEM((members, short, LANES), BF16),
        pltpu.VMEM((GROUPS * rows * LINES, LANES), F32),
        pltpu.VMEM((rows, width_part + LANES), jnp.int16),
        pltpu.VMEM((peers, rows, width_part + LANES), jnp.int16),
        pltpu.SemaphoreType.DMA,
        pltpu.SemaphoreType.DMA((6 + 7 * PIECES + 2,)),
        pltpu.SemaphoreType.DMA((8,)),
        pltpu.SemaphoreType.DMA((8,)),
        pltpu.SemaphoreType.DMA((GROUPS,)),
        pltpu.SemaphoreType.DMA((GROUPS,)),
    ]
    return pl.pallas_call(
        functools.partial(kernel, members, peers, width_part * members),
        out_shape=pltpu.VMEM(tokens.shape, BF16),
        in_specs=[any_spec] * 13,
        out_specs=vmem_spec,
        scratch_shapes=scratch,
        compiler_params=pltpu.CompilerParams(
            collective_id=0, has_side_effects=True, vmem_limit_bytes=56 * 1024 * 1024
        ),
        name="decoder_layer",
    )(
        lengths,
        tokens,
        attn_gain,
        mlp_gain,
        freq,
        block_table,
        query_key_value_weight,
        paged_key_store,
        paged_value_store,
        out_weight,
        gate_weight,
        up_weight,
        down_weight,
    )


def solution(mesh):
    return jax.shard_map(
        functools.partial(local, mesh.shape["mem"], mesh.shape["mp"]),
        mesh=mesh,
        in_specs=(
            P(None, "mem"),
            P("mem"),
            P("mem", "mp"),
            P("mem", "mp", None, None),
            P("mem", "mp", None, None),
            P(),
            P(),
            P("mp", "mem"),
            P("mem"),
            P("mem", "mp"),
            P("mem", "mp"),
            P("mp", "mem"),
        ),
        out_specs=P(None, "mem"),
        check_vma=False,
    )
```

```python
import functools
import math

import jax
import jax.numpy as jnp
import numpy as np
from jax import lax
from jax.experimental import pallas as pl
from jax.experimental.pallas import tpu as pltpu
from jax.sharding import PartitionSpec as P

MESH = pl.DeviceIdType.MESH
F32 = jnp.float32
BF16 = jnp.bfloat16

EPSILON = 1e-05
ROPE_BASE = 500000.0
FLOOR_SCORE = -1e30
LANES = 128
HEADS = 8
NEW = 4
REQUESTS = 4
GROUP = NEW * HEADS
OWNER = 256
RUN = 4
TILE = 36
PARTIAL = 16
GROUPS = 4
LINES = 8
PIECES = 4

HALF_PI = (1.5703125, 0.000484466552734375, -6.397578377557687e-07)


def sine_cosine(angle):
    turns = jnp.floor(angle * (2.0 / math.pi) + 0.5)
    r = ((angle - turns * HALF_PI[0]) - turns * HALF_PI[1]) - turns * HALF_PI[2]
    z = r * r
    sine = r + r * z * (-1.6666654611e-1 + z * (8.3321608736e-3 + z * (-1.9515295891e-4)))
    cosine = 1.0 - 0.5 * z + z * z * (
        4.166664568298827e-2 + z * (-1.388731625493765e-3 + z * 2.443315711809948e-5)
    )
    quadrant = turns - 4.0 * jnp.floor(turns * 0.25)
    odd = (quadrant == 1.0) | (quadrant == 3.0)
    s, c = jnp.where(odd, cosine, sine), jnp.where(odd, sine, cosine)
    s = jnp.where(quadrant >= 2.0, -s, s)
    c = jnp.where((quadrant == 1.0) | (quadrant == 2.0), -c, c)
    return s, c


STEPS = 32000.0
FINE = 256.0


def code_of(value):
    return jnp.log(jnp.maximum(value, 1e-30)) * (FINE / math.log(2.0))


def value_of(code):
    return jnp.exp2(code * (1.0 / FINE))


def kernel(
    members,
    peers,
    model_width,
    lengths_hbm,
    tokens_hbm,
    gain_one_hbm,
    gain_two_hbm,
    freq_hbm,
    table_hbm,
    wqkv_hbm,
    keys_hbm,
    values_hbm,
    wout_hbm,
    wgate_hbm,
    wup_hbm,
    wdown_hbm,
    out_ref,
    lengths,
    tokens,
    gain_one,
    gain_two,
    freq,
    table,
    wqkv,
    keys,
    values,
    wout,
    wgate,
    wup,
    wdown,
    queries,
    codes,
    slot_codes,
    tops_ref,
    scores,
    s1,
    r1,
    s2,
    r2,
    s4,
    r4,
    s5,
    r5,
    s5b,
    r5b,
    g6,
    s6,
    r6,
    s7,
    r7,
    g7,
    s7b,
    r7b,
    code_sem,
    fetch_sem,
    send_sem,
    recv_sem,
    quarter_sem,
    group_sem,
):
    me = lax.axis_index("mem")
    mine = lax.axis_index("mp")
    rows = tokens.shape[0]
    slots = keys.shape[0]
    block_len = keys.shape[1]

    side = math.isqrt(members)
    z, x = me // side, lax.rem(me, side)
    steps_of = lambda d, n: min(d, n - d)
    offsets = sorted(
        ((dz, dx) for dz in range(side) for dx in range(side) if dz or dx),
        key=lambda d: -steps_of(d[0], side) - steps_of(d[1], side),
    )
    member_order = [lax.rem(z + dz, side) * side + lax.rem(x + dx, side) for dz, dx in offsets]
    ring, cores = peers // 2, 2
    y, core = mine // cores, lax.rem(mine, cores)
    offsets = sorted(
        ((dy, dc) for dy in range(ring) for dc in range(cores) if dy or dc),
        key=lambda d: -steps_of(d[0], ring),
    )
    peer_order = [lax.rem(y + dy, ring) * cores + lax.rem(core + dc, cores) for dy, dc in offsets]

    fetched = {}

    def fetch(name, source, target, pieces=1):
        size = target.shape[0] // pieces
        fetched[name] = []
        for p in range(pieces):
            index = sum(len(v) for v in fetched.values())
            if pieces > 1:
                part = pl.ds(p * size, size)
                copy = pltpu.make_async_copy(source.at[part], target.at[part], fetch_sem.at[index])
            else:
                copy = pltpu.make_async_copy(source, target, fetch_sem.at[index])
            copy.start()
            fetched[name].append(copy)

    def ready(*names):
        for name in names:
            for copy in fetched[name]:
                copy.wait()

    fetch("tokens", tokens_hbm, tokens)
    fetch("gain_one", gain_one_hbm, gain_one)
    fetch("wqkv", wqkv_hbm, wqkv, 2 * PIECES)
    fetch("lengths", lengths_hbm, lengths)
    fetch("freq", freq_hbm, freq)

    barrier = pltpu.get_barrier_semaphore()
    for other in member_order:
        pl.semaphore_signal(barrier, inc=1, device_id={"mem": other}, device_id_type=MESH)
    for other in peer_order:
        pl.semaphore_signal(barrier, inc=1, device_id={"mp": other}, device_id_type=MESH)

    fetch("table", table_hbm, table)
    fetch("gain_two", gain_two_hbm, gain_two)

    def send_members(phase, source_of, target):
        for other in member_order:
            pltpu.make_async_remote_copy(
                src_ref=source_of(other),
                dst_ref=target,
                send_sem=send_sem.at[phase],
                recv_sem=recv_sem.at[phase],
                device_id={"mem": other},
                device_id_type=MESH,
            ).start()

    def send_peers(phase, source, target):
        for other in peer_order:
            pltpu.make_async_remote_copy(
                src_ref=source,
                dst_ref=target,
                send_sem=send_sem.at[phase],
                recv_sem=recv_sem.at[phase],
                device_id={"mp": other},
                device_id_type=MESH,
            ).start()

    width = tokens.shape[1]

    def sum_peers(phase, partial, staged, landed):
        unit_code = jnp.ceil(code_of(jnp.max(jnp.abs(partial), axis=1, keepdims=True)))
        steps = jnp.floor(partial * (STEPS / value_of(unit_code)) + 0.5)
        staged[:, :width] = steps.astype(jnp.int32).astype(jnp.int16)
        staged[:, width:] = (
            jnp.broadcast_to(unit_code, (rows, LANES)).astype(jnp.int32).astype(jnp.int16)
        )
        send_peers(phase, staged, landed.at[mine])
        landed[mine] = staged[...]
        wait_bytes(landed.at[pl.ds(0, peers - 1)], recv_sem.at[phase])
        total = jnp.zeros((rows, width), F32)
        for j in range(peers):
            part = landed[j].astype(jnp.int32).astype(F32)
            unit = value_of(part[:, width:]) * (1.0 / STEPS)
            total = total + part[:, :width] * jnp.concatenate([unit] * (width // LANES), axis=1)
        return total

    def wait_bytes(window, semaphore):
        pltpu.make_async_copy(window, window, semaphore).wait()

    ready("tokens", "gain_one")
    token_f = tokens[...].astype(F32)
    scaled_in = (token_f * gain_one[...].astype(F32)[None, :]).astype(BF16)
    square_one = jnp.sum(token_f * token_f, axis=1, keepdims=True)
    request, place = me // NEW, lax.rem(me, NEW)
    ready("lengths", "freq")
    position = (lengths[request] + place).astype(F32)
    sine, cosine = sine_cosine(position * freq[...])
    lane_row = lax.broadcasted_iota(jnp.int32, (1, LANES), 1)
    sine = jnp.where(lane_row < LANES // 2, -sine, sine)
    ready("wqkv")
    projected = jnp.dot(scaled_in, wqkv[...], preferred_element_type=F32)
    for c in range(HEADS + 2):
        s1[pl.ds(c, rows, stride=rows), :] = projected[:, c * LANES : (c + 1) * LANES]
    s1[pl.ds(HEADS + 2, rows, stride=rows), :] = jnp.broadcast_to(square_one, (rows, LANES))

    pl.semaphore_wait(barrier, members - 1 + peers - 1)

    used = HEADS + 3
    send_members(
        0, lambda other: s1.at[pl.ds(other * rows, used)], r1.at[me, pl.ds(0, used)]
    )
    r1[me] = s1[pl.ds(pl.multiple_of(me * rows, rows), rows), :]

    fetch("keys", keys_hbm.at[:, 0], keys, PIECES)

    ready("table")
    first_slot = me * slots
    max_blocks = table.shape[1]
    block_start = lax.broadcasted_iota(jnp.int32, (1, max_blocks), 1) * block_len
    slot_ids = first_slot + lax.broadcasted_iota(jnp.int32, (slots, max_blocks), 0)
    code = jnp.zeros((slots, max_blocks), jnp.int32)
    for r in range(REQUESTS):
        held = jnp.clip(lengths[r] - block_start, 0, block_len)
        held = jnp.where(held > 0, held + r * OWNER, 0)
        code = code + jnp.where(table[r : r + 1, :] == slot_ids, held, 0)
    code = jnp.sum(code, axis=1, keepdims=True)
    wait_bytes(r1.at[pl.ds(0, members - 1), pl.ds(0, used)], recv_sem.at[0])
    total = r1[0]
    for j in range(1, members):
        total = total + r1[j]
    inverse_one = 1.0 / jnp.sqrt(total[HEADS + 2 : HEADS + 3, :] / model_width + EPSILON)
    total = total * inverse_one
    turned = total * cosine + pltpu.roll(total, LANES // 2, 1) * sine
    head_row = lax.broadcasted_iota(jnp.int32, total.shape, 0)
    s2[...] = jnp.where(head_row <= HEADS, turned, total).astype(BF16)
    send_members(1, lambda other: s2, r2.at[me])
    r2[me] = s2[...]
    fetch("values", values_hbm.at[:, 0], values, PIECES)

    sub = lax.broadcasted_iota(jnp.int32, (slots, slots), 0)
    lane = lax.broadcasted_iota(jnp.int32, (slots, slots), 1)
    code_line = jnp.sum(jnp.where(sub == lane, code, 0), axis=0, keepdims=True)
    owner_column = jnp.where(code > 0, code >> 8, REQUESTS)
    owner_line = jnp.where(code_line > 0, code_line >> 8, REQUESTS)
    ahead = jnp.where((owner_line == owner_column) & (lane < sub), 1, 0)
    place_column = jnp.sum(ahead, axis=1, keepdims=True)
    positions = codes.shape[1]
    run_ids = lax.broadcasted_iota(jnp.int32, (1, positions), 1) * RUN
    run_owner = jnp.zeros((1, positions), jnp.int32)
    start = jnp.zeros((1, 1), jnp.int32)
    for r in range(REQUESTS):
        if r > 0:
            run_owner = run_owner + jnp.where(run_ids >= start, 1, 0)
        place_column = place_column + jnp.where(owner_column == r, start, 0)
        number = jnp.sum(jnp.where(owner_line == r, 1, 0), axis=1, keepdims=True)
        start = start + ((number + (RUN - 1)) & -RUN)
    place_column = jnp.where(code > 0, place_column, -1)
    position_ids = lax.broadcasted_iota(jnp.int32, (slots, positions), 1)
    entry = lax.broadcasted_iota(jnp.int32, (slots, positions), 0) * OWNER + (code & (OWNER - 1))
    entry = jnp.where(position_ids == place_column, entry, 0)
    codes[0:1, :] = jnp.sum(entry, axis=0, keepdims=True)
    codes[1:2, :] = run_owner
    owner_row = run_owner[:, :LANES]
    to_scalars = pltpu.make_async_copy(codes, slot_codes, code_sem)
    to_scalars.start()
    fetch("wout", wout_hbm, wout, 2)
    fetch("wgate", wgate_hbm, wgate, PIECES)
    fetch("wup", wup_hbm, wup, PIECES)

    wait_bytes(r2.at[pl.ds(0, members - 1)], recv_sem.at[1])

    for r in range(REQUESTS):
        queries[r] = jnp.concatenate(
            [r2[r * NEW + t].astype(F32)[:HEADS] for t in range(NEW)], axis=0
        ).astype(BF16)
    factor = math.log2(math.e) / math.sqrt(LANES)
    lane_group = lax.broadcasted_iota(jnp.int32, (GROUP, LANES), 1)
    to_scalars.wait()
    ready("keys")

    def run_of(run):
        entries = [slot_codes[0, run * RUN + i] for i in range(RUN)]
        return slot_codes[1, run], [(e >> 8, e & (OWNER - 1)) for e in entries]

    blank = jnp.zeros((GROUP, LANES), BF16)

    def score_step(step, best):
        for j in range(0, TILE, 2):
            pair = [(step * TILE + j + i,) + run_of(step * TILE + j + i) for i in range(2)]
            first, second = (queries[owner] for _, owner, _ in pair)
            left = jnp.concatenate(
                [
                    jnp.concatenate([first, blank], axis=1),
                    jnp.concatenate([blank, second], axis=1),
                ],
                axis=0,
            )
            right = jnp.concatenate(
                [
                    jnp.concatenate([keys[slot] for slot, _ in members_of], axis=0)
                    for _, _, members_of in pair
                ],
                axis=1,
            )
            both = lax.dot_general(
                left, right, (((1,), (1,)), ((), ())), preferred_element_type=F32
            )
            for half, (run, _, members_of) in enumerate(pair):
                score = both[half * GROUP : (half + 1) * GROUP]
                tops = []
                for i, (_, count) in enumerate(members_of):
                    part = slice(i * LANES, (i + 1) * LANES)
                    tops.append(jnp.where(lane_group < count, score[:, part], FLOOR_SCORE))
                    scores[run, :, part] = tops[-1]
                top = jnp.max(functools.reduce(jnp.maximum, tops), axis=1, keepdims=True)
                best = jnp.where(lane_group == run, top, best)
        return best

    floor = jnp.full((GROUP, LANES), FLOOR_SCORE, F32)
    runs = scores.shape[0]
    run_best = lax.fori_loop(0, runs // TILE, score_step, floor)
    best = []
    for r in range(REQUESTS):
        own = jnp.where(owner_row == r, run_best, FLOOR_SCORE)
        best.append(jnp.broadcast_to(jnp.max(own, axis=1, keepdims=True), (GROUP, LANES)))
        tops_ref[r] = best[r]
    ready("values")

    def value_step(step, carry):
        sums, mixed = carry[0], list(carry[1])
        for j in range(TILE):
            run = step * TILE + j
            owner, members_of = run_of(run)
            top = tops_ref[owner]
            weights, highs, lows = [], [], []
            for i in range(RUN):
                weight = jnp.exp2((scores[run, :, i * LANES : (i + 1) * LANES] - top) * factor)
                weights.append(weight)
                highs.append(weight.astype(BF16))
                lows.append((weight - highs[-1].astype(F32)).astype(BF16))
            total = jnp.sum(functools.reduce(jnp.add, weights), axis=1, keepdims=True)
            sums = jnp.where(lane_group == run, total, sums)
            both = jnp.dot(
                jnp.concatenate(
                    [jnp.concatenate(highs, axis=1), jnp.concatenate(lows, axis=1)], axis=0
                ),
                jnp.concatenate([values[slot] for slot, _ in members_of], axis=0),
                preferred_element_type=F32,
            )
            both = both[:GROUP] + both[GROUP:]
            for r in range(REQUESTS):
                mixed[r] = mixed[r] + jnp.where(owner == r, both, 0.0)
        return sums, tuple(mixed)

    zero = jnp.zeros((GROUP, LANES), F32)
    run_sums, mixed = lax.fori_loop(0, runs // TILE, value_step, (zero, (zero,) * REQUESTS))
    lane_head = lax.broadcasted_iota(jnp.int32, (HEADS, LANES), 1) // (LANES // HEADS)
    by_head = lane_head == lax.broadcasted_iota(jnp.int32, (HEADS, LANES), 0)

    def to_line(column):
        return jnp.sum(jnp.where(by_head, column, 0.0), axis=0, keepdims=True)

    def to_column(line):
        column = jnp.max(jnp.where(by_head, line, -jnp.inf), axis=1, keepdims=True)
        return jnp.broadcast_to(column, (HEADS, LANES))

    for r in range(REQUESTS):
        own = jnp.where(owner_row == r, run_sums, 0.0)
        whole = jnp.broadcast_to(jnp.sum(own, axis=1, keepdims=True), (GROUP, LANES))
        for t in range(NEW):
            part = slice(t * HEADS, (t + 1) * HEADS)
            line = (r * NEW + t) * PARTIAL
            s4[line : line + HEADS, :] = mixed[r][part]
            s4[line + HEADS : line + HEADS + 1, :] = to_line(best[r][part])
            s4[line + HEADS + 1 : line + HEADS + 2, :] = to_line(whole[part])
    mine_4 = pl.ds(pl.multiple_of(me * PARTIAL, PARTIAL), PARTIAL)
    sent = HEADS + 2
    send_members(
        2,
        lambda other: s4.at[pl.ds(other * PARTIAL, sent)],
        r4.at[pl.ds(me * PARTIAL, sent)],
    )
    r4[mine_4, :] = s4[mine_4, :]
    fetch("wdown", wdown_hbm, wdown, PIECES)

    row_queries = r2[me].astype(F32)[:HEADS]
    own_scores, own_values = [], []
    for t in range(NEW):
        fresh = r2[request * NEW + t].astype(F32)
        score = jnp.sum(row_queries * fresh[HEADS : HEADS + 1], axis=1, keepdims=True)
        score = jnp.broadcast_to(score, (HEADS, LANES))
        own_scores.append(jnp.where(t <= place, score, FLOOR_SCORE))
        own_values.append(fresh[HEADS + 1 : HEADS + 2])
    top = to_line(functools.reduce(jnp.maximum, own_scores))

    wait_bytes(r4.at[pl.ds(0, (members - 1) * sent)], recv_sem.at[2])
    tops = r4[pl.ds(HEADS, members, stride=PARTIAL), :]
    wholes = r4[pl.ds(HEADS + 1, members, stride=PARTIAL), :]
    top = jnp.maximum(top, jnp.max(tops, axis=0, keepdims=True))
    shrink = jnp.exp2((tops - top) * factor)
    whole = to_column(jnp.sum(wholes * shrink, axis=0, keepdims=True))
    top = to_column(top)
    mix = jnp.zeros((HEADS, LANES), F32)
    for t in range(NEW):
        weight = jnp.exp2((own_scores[t] - top) * factor)
        whole = whole + weight
        mix = mix + weight * own_values[t]
    for j in range(members):
        mix = mix + r4[j * PARTIAL : j * PARTIAL + HEADS, :] * to_column(shrink[j : j + 1])
    s5[...] = mix / whole
    own_rows = pl.ds(pl.multiple_of(me * HEADS, HEADS), HEADS)
    send_members(3, lambda other: s5, r5.at[own_rows])
    r5[own_rows, :] = s5[...]
    ready("wout")
    wait_bytes(r5.at[pl.ds(0, (members - 1) * HEADS)], recv_sem.at[3])

    attended = jnp.concatenate(
        [r5[pl.ds(h, rows, stride=HEADS), :].astype(BF16) for h in range(HEADS)], axis=1
    )
    partial = jnp.dot(attended, wout[...], preferred_element_type=F32)
    after_f = (token_f + sum_peers(4, partial, s5b, r5b)).astype(BF16).astype(F32)
    ready("gain_two", "wgate", "wup")

    scaled_mid = (after_f * gain_two[...].astype(F32)[None, :]).astype(BF16)
    square_mid = jnp.sum(after_f * after_f, axis=1, keepdims=True)
    square_code = code_of(square_mid)
    square_whole = jnp.floor(square_code)
    square_rest = jnp.floor((square_code - square_whole) * STEPS + 0.5)
    lane_rows = lax.broadcasted_iota(jnp.int32, (rows, LANES), 1)
    square_line = jnp.where(lane_rows < LANES // 2, square_whole, square_rest)

    quarter, group = me // GROUPS, lax.rem(me, GROUPS)
    span = wgate.shape[1] // GROUPS
    chunks = span // LANES
    tall = rows * LINES
    short = tall // GROUPS

    def multiply(k):
        columns = pl.ds(pl.multiple_of(lax.rem(group + k, GROUPS) * span, LANES), span)
        both = jnp.concatenate([wgate[:, columns], wup[:, columns]], axis=1)
        both = jnp.dot(scaled_mid, both, preferred_element_type=F32)
        return both[:, :span], both[:, span:]

    def ship(k, parts):
        target = lax.rem(group + k, GROUPS)
        largest = jnp.maximum(jnp.abs(parts[0]), jnp.abs(parts[1]))
        unit_code = jnp.ceil(code_of(jnp.max(largest, axis=1, keepdims=True)))
        to_steps = STEPS / value_of(unit_code)
        unit_line = jnp.broadcast_to(unit_code, (rows, LANES))
        for index, (part, extra) in enumerate(zip(parts, (unit_line, square_line))):
            base = (2 * k + index) * tall
            steps = jnp.floor(part * to_steps + 0.5)
            for c in range(chunks):
                g6[pl.ds(base + c, rows, stride=LINES), :] = steps[:, c * LANES : (c + 1) * LANES]
            g6[pl.ds(base + chunks, rows, stride=LINES), :] = extra
            for q in range(GROUPS):
                piece = g6[base + q * short : base + (q + 1) * short, :]
                s6[k, q, index * short : (index + 1) * short, :] = piece.astype(jnp.int32).astype(
                    jnp.int16
                )
        for j in (2, 1, 3, 0) if k else (2, 1, 3):
            other = lax.rem(quarter + j, GROUPS)
            pltpu.make_async_remote_copy(
                src_ref=s6.at[k, other],
                dst_ref=r6.at[me],
                send_sem=send_sem.at[5],
                recv_sem=quarter_sem.at[k],
                device_id={"mem": other * GROUPS + target},
                device_id_type=MESH,
            ).start()

    order = (2, 1, 3, 0)
    parts = multiply(order[0])
    for index, k in enumerate(order):
        later = multiply(order[index + 1]) if index + 1 < GROUPS else None
        ship(k, parts)
        parts = later
    r6[me] = s6[0, quarter]

    gates = [jnp.zeros((LINES, LANES), F32)] * GROUPS
    ups = [jnp.zeros((LINES, LANES), F32)] * GROUPS
    square = jnp.zeros((GROUPS, LANES), F32)
    lane_codes = lax.broadcasted_iota(jnp.int32, (GROUPS, LANES), 1)
    for k, q in [(k, q) for k in order for q in range(GROUPS)]:
        if q == 0:
            arriving = GROUPS if k else GROUPS - 1
            wait_bytes(r6.at[pl.ds(0, arriving)], quarter_sem.at[k])
        sender = q * GROUPS + lax.rem(group + GROUPS - k, GROUPS)
        part = r6[sender].astype(jnp.int32).astype(F32)
        units, squares = (
            jnp.concatenate(
                [
                    part[start + r * LINES + chunks : start + r * LINES + chunks + 1]
                    for r in range(GROUPS)
                ],
                axis=0,
            )
            for start in (0, short)
        )
        units = value_of(units) * (1.0 / STEPS)
        squares = jnp.where(lane_codes < LANES // 2, squares, squares * (1.0 / STEPS))
        square = square + value_of(squares + pltpu.roll(squares, LANES // 2, 1))
        for r in range(GROUPS):
            own = slice(r * LINES, (r + 1) * LINES)
            gates[r] = gates[r] + part[:short][own] * units[r : r + 1]
            ups[r] = ups[r] + part[short:][own] * units[r : r + 1]
    inverse_two = 1.0 / jnp.sqrt(square / model_width + EPSILON)
    hidden = []
    for r in range(GROUPS):
        gate = gates[r] * inverse_two[r : r + 1]
        hidden.append(gate / (1.0 + jnp.exp(-gate)) * (ups[r] * inverse_two[r : r + 1]))
    s7[...] = jnp.concatenate(hidden, axis=0).astype(BF16)
    for other in member_order:
        pltpu.make_async_remote_copy(
            src_ref=s7,
            dst_ref=r7.at[me],
            send_sem=send_sem.at[6],
            recv_sem=group_sem.at[group],
            device_id={"mem": other},
            device_id_type=MESH,
        ).start()
    r7[me] = s7[...]
    ready("wdown")

    down = jnp.zeros((rows, wdown.shape[1]), F32)
    for k in (0, 1, 3, 2):
        source = lax.rem(group + k, GROUPS)
        arriving = GROUPS - 1 if k == 0 else GROUPS
        wait_bytes(r7.at[pl.ds(0, arriving)], group_sem.at[source])
        for q in range(GROUPS):
            line = k * tall + q * short
            g7[line : line + short, :] = r7[q * GROUPS + source].astype(F32)
        piece = jnp.concatenate(
            [
                g7[pl.ds(k * tall + c, rows, stride=LINES), :].astype(BF16)
                for c in range(chunks)
            ],
            axis=1,
        )
        down = down + jnp.dot(
            piece,
            wdown[pl.ds(pl.multiple_of(source * span, LANES), span), :],
            preferred_element_type=F32,
        )
    out_ref[...] = (after_f + sum_peers(7, down, s7b, r7b)).astype(BF16)

    wait_bytes(r1.at[pl.ds(0, members - 1), pl.ds(0, used)], send_sem.at[0])
    wait_bytes(r2.at[pl.ds(0, members - 1)], send_sem.at[1])
    wait_bytes(r4.at[pl.ds(0, (members - 1) * sent)], send_sem.at[2])
    wait_bytes(r5.at[pl.ds(0, (members - 1) * HEADS)], send_sem.at[3])
    for phase, landed in ((4, r5b), (7, r7b)):
        wait_bytes(landed.at[pl.ds(0, peers - 1)], send_sem.at[phase])
    for phase, landed in ((5, r6), (6, r7)):
        wait_bytes(landed.at[pl.ds(0, members - 1)], send_sem.at[phase])


def local(
    members,
    peers,
    tokens,
    attn_gain,
    query_key_value_weight,
    paged_key_store,
    paged_value_store,
    lengths,
    block_table,
    out_weight,
    mlp_gain,
    gate_weight,
    up_weight,
    down_weight,
):
    rows, width_part = tokens.shape
    slots, _, block_len, head_dim = paged_key_store.shape
    short = rows * LINES // GROUPS
    runs = slots // RUN + REQUESTS
    exponents = np.arange(head_dim // 2, dtype=np.float32) * np.float32(
        -2.0 * math.log(ROPE_BASE) / head_dim
    )
    inverse = np.exp(exponents.astype(np.float64)).astype(np.float32)
    freq = jnp.asarray(np.concatenate([inverse, inverse])[None, :])

    any_spec = pl.BlockSpec(memory_space=pl.ANY)
    vmem_spec = pl.BlockSpec(memory_space=pltpu.VMEM)
    scratch = [
        pltpu.SMEM(lengths.shape, jnp.int32),
        pltpu.VMEM(tokens.shape, BF16),
        pltpu.VMEM(attn_gain.shape, BF16),
        pltpu.VMEM(mlp_gain.shape, BF16),
        pltpu.VMEM(freq.shape, F32),
        pltpu.VMEM(block_table.shape, jnp.int32),
        pltpu.VMEM(query_key_value_weight.shape, BF16),
        pltpu.VMEM((slots, block_len, head_dim), BF16),
        pltpu.VMEM((slots, block_len, head_dim), BF16),
        pltpu.VMEM(out_weight.shape, BF16),
        pltpu.VMEM(gate_weight.shape, BF16),
        pltpu.VMEM(up_weight.shape, BF16),
        pltpu.VMEM(down_weight.shape, BF16),
        pltpu.VMEM((REQUESTS, GROUP, head_dim), BF16),
        pltpu.VMEM((8, 2 * LANES), jnp.int32),
        pltpu.SMEM((8, 2 * LANES), jnp.int32),
        pltpu.VMEM((REQUESTS, GROUP, LANES), F32),
        pltpu.VMEM((runs, GROUP, RUN * LANES), F32),
        pltpu.VMEM((rows * rows, LANES), F32),
        pltpu.VMEM((members, rows, LANES), F32),
        pltpu.VMEM((16, LANES), BF16),
        pltpu.VMEM((members, 16, LANES), BF16),
        pltpu.VMEM((members * PARTIAL, LANES), F32),
        pltpu.VMEM((members * PARTIAL, LANES), F32),
        pltpu.VMEM((HEADS, LANES), F32),
        pltpu.VMEM((members * HEADS, LANES), F32),
        pltpu.VMEM((rows, width_part + LANES), jnp.int16),
        pltpu.VMEM((peers, rows, width_part + LANES), jnp.int16),
        pltpu.VMEM((2 * GROUPS * rows * LINES, LANES), F32),
        pltpu.VMEM((GROUPS, GROUPS, 2 * short, LANES), jnp.int16),
        pltpu.VMEM((members, 2 * short, LANES), jnp.int16),
        pltpu.VMEM((short, LANES), BF16),
        pltpu.VMEM((members, short, LANES), BF16),
        pltpu.VMEM((GROUPS * rows * LINES, LANES), F32),
        pltpu.VMEM((rows, width_part + LANES), jnp.int16),
        pltpu.VMEM((peers, rows, width_part + LANES), jnp.int16),
        pltpu.SemaphoreType.DMA,
        pltpu.SemaphoreType.DMA((6 + 7 * PIECES + 2,)),
        pltpu.SemaphoreType.DMA((8,)),
        pltpu.SemaphoreType.DMA((8,)),
        pltpu.SemaphoreType.DMA((GROUPS,)),
        pltpu.SemaphoreType.DMA((GROUPS,)),
    ]
    return pl.pallas_call(
        functools.partial(kernel, members, peers, width_part * members),
        out_shape=pltpu.VMEM(tokens.shape, BF16),
        in_specs=[any_spec] * 13,
        out_specs=vmem_spec,
        scratch_shapes=scratch,
        compiler_params=pltpu.CompilerParams(
            collective_id=0, has_side_effects=True, vmem_limit_bytes=56 * 1024 * 1024
        ),
        name="decoder_layer",
    )(
        lengths,
        tokens,
        attn_gain,
        mlp_gain,
        freq,
        block_table,
        query_key_value_weight,
        paged_key_store,
        paged_value_store,
        out_weight,
        gate_weight,
        up_weight,
        down_weight,
    )


def solution(mesh):
    return jax.shard_map(
        functools.partial(local, mesh.shape["mem"], mesh.shape["mp"]),
        mesh=mesh,
        in_specs=(
            P(None, "mem"),
            P("mem"),
            P("mem", "mp"),
            P("mem", "mp", None, None),
            P("mem", "mp", None, None),
            P(),
            P(),
            P("mp", "mem"),
            P("mem"),
            P("mem", "mp"),
            P("mem", "mp"),
            P("mp", "mem"),
        ),
        out_specs=P(None, "mem"),
        check_vma=False,
    )
```
